32 devices in a mesh: crop: 4 (over y, x), img: 8 (over z, core).
Axes of the slice: x: 2, y: 2, z: 4, core: 2. Of those that a mesh axis runs over, the one named last changes fastest.
Arguments:
- pixels: bfloat16 [4, 8, 784, 2016], P('crop', 'img'), may hold values from -6 to 6
- counts: int32 [8, 4], P('img'), may hold values from 1 to 10, 32 in all within a row
- slot_order: int32 [8, 32], P('img'), may hold values from 0 to 31, each once within a row
- w_in: bfloat16 [2016, 2016], replicated, may hold values from -0.125 to 0.125
- kernel: bfloat16 [9, 36, 56, 56], replicated, may hold values from -0.25 to 0.25
- w_red: bfloat16 [2016, 504], replicated, may hold values from -0.125 to 0.125
- b_red: float32 [504], replicated, may hold values from -3 to 3
- w_exp: bfloat16 [504, 2016], replicated, may hold values from -0.25 to 0.25
- b_exp: float32 [2016], replicated, may hold values from -3 to 3
- w_out: bfloat16 [2016, 2016], replicated, may hold values from -0.125 to 0.125
- gain_one: float32 [2016], replicated, may hold values from 0.5 to 1.5
- shift_one: float32 [2016], replicated, may hold values from -1.8 to 1.8
- gain_two: float32 [2016], replicated, may hold values from 0.5 to 1.5
- shift_two: float32 [2016], replicated, may hold values from -1.8 to 1.8
- gain_three: float32 [2016], replicated, may hold values from 0.5 to 1.5
- shift_three: float32 [2016], replicated, may hold values from -1.8 to 1.8
- protos: bfloat16 [2016, 3000], replicated, may hold values from -1.1953125 to 1.1953125
Outputs:
- loss: float32 [], replicated
- block_out: bfloat16 [4, 8, 784, 2016], P('crop', 'img')
- grad_pixels: float32 [4, 8, 784, 2016], P('crop', 'img')
- grad_w_in: float32 [4064256], P('img')
- grad_kernel: float32 [1016064], P('img')
- grad_w_red: float32 [1016064], P('img')
- grad_w_exp: float32 [1016064], P('img')
- grad_w_out: float32 [4064256], P('img')
- grad_protos: float32 [6048000], P('img')
- grad_b_red: float32 [504], replicated
- grad_b_exp: float32 [2016], replicated
- grad_gain_one: float32 [2016], replicated
- grad_shift_one: float32 [2016], replicated
- grad_gain_two: float32 [2016], replicated
- grad_shift_two: float32 [2016], replicated
- grad_gain_three: float32 [2016], replicated
- grad_shift_three: float32 [2016], replicated
The draws below stay inside these ranges and needn't reach their ends.
Inputs may be any that keep to these rules, and one draw needn't show every extreme that they name: `counts`: each row sums to 32 and its largest entry is 10. `slot_order`: each row is a permutation.
All inputs are finite; a program needn't handle non-finite values.
Results may differ from the reference program's by a relative error of at most 0.015.
Values sent between devices are 32-bit elements; how exact they have to be, the bound alone decides.
No kernel may reach another device: no remote copies, remote signals or barrier semaphores. Data moves between devices by JAX's collectives and lax.ppermute only.
A program may use at most 448 MiB of HBM per device.

```python
import math
import jax
import jax.numpy as jnp
import numpy as np
from jax import lax

NG = 36
GS = 56
K = 3000
W = 2016
SE = 504
IMG_DEV = 4
SIDE = 14
SMALL_SIDE = 7
ROWS = 784
SEGS = 16
SLOTS = 32
GROUPS = 8
IMAGES = 32
CROPS = 4


def block_levels(rng, extent, pieces, low, largest):
    loudness, own = 1.0, jax.random.fold_in(rng, 6)
    for axis_at, blocks in pieces:
        heights = jnp.exp(jax.random.uniform(jax.random.fold_in(own, axis_at), (blocks,), jnp.float32, low / len(pieces), largest / len(pieces)))
        loudness = loudness * jnp.repeat(heights, extent[axis_at] // blocks).reshape([-1 if axis == axis_at else 1 for axis in range(len(extent))])
    return loudness


def length_profile(number_of, total, most, lean):
    weights = [(1 << 20) // math.isqrt(grade ** lean) + 1 for grade in range(2, number_of + 1)]
    spare, holding = total - most - (number_of - 1), [1] * (number_of - 1)
    while spare > 0:
        candidates = [i for i in range(number_of - 1) if holding[i] < most]
        whole, remaining = sum([weights[i] for i in candidates]), spare
        for i in candidates:
            addition = min(most - holding[i], max(1, remaining * weights[i] // whole), spare)
            holding[i] = holding[i] + addition
            spare = spare - addition
    return np.array([most] + holding)


def ragged(rng, amount, total, most, slope):
    if amount == 2:
        one = jax.random.randint(rng, (), max(1, total - most), min(most, total - 1) + 1)
        return jnp.stack([one, total - one])
    lengths = jnp.asarray(length_profile(amount, total, most, slope), jnp.int32)
    twos = (amount - 1) // 2
    source_of, taker = lengths[1:1 + 2 * twos:2], lengths[2:2 + 2 * twos:2]
    room = jnp.minimum(source_of - 1, most - taker)
    passed = jax.random.randint(jax.random.fold_in(rng, 1), (twos,), 0, 1 << 20) % (room + 1)
    lengths = lengths.at[1:1 + 2 * twos:2].set(source_of - passed).at[2:2 + 2 * twos:2].set(taker + passed)
    return lengths[jax.random.permutation(jax.random.fold_in(rng, 2), amount)]


def gaussian(own_key, shape, width, reach, shards=(), kind=jnp.bfloat16):
    result = jax.random.normal(own_key, shape, jnp.float32) * width
    if len(shards) > 0:
        result = block_levels(own_key, shape, shards, -0.22, 0.18) * result
    return jnp.clip(result, min=-reach, max=reach).astype(kind)


def setup_inputs(seed: int = 0) -> dict:
    streams_of = jax.random.split(jax.random.key(seed), 18)
    return {
        "pixels": gaussian(streams_of[0], (CROPS, GROUPS, ROWS, W), 1.0, 6.0, ((0, 4), (1, 8))),
        "counts": jax.vmap(lambda own: ragged(own, IMG_DEV, SLOTS, 10, 2))(jax.random.split(streams_of[1], GROUPS)).reshape((GROUPS, IMG_DEV)).astype(jnp.int32),
        "slot_order": jax.vmap(lambda own: jax.random.permutation(own, SLOTS))(jax.random.split(streams_of[2], GROUPS)).reshape((GROUPS, SLOTS)).astype(jnp.int32),
        "w_in": gaussian(streams_of[3], (W, W), W ** -0.5, 0.125),
        "kernel": gaussian(streams_of[4], (9, NG, GS, GS), (9 * GS) ** -0.5, 0.25),
        "w_red": gaussian(streams_of[5], (W, SE), W ** -0.5, 0.125),
        "b_red": gaussian(streams_of[6], (SE,), 0.5, 3.0, (), jnp.float32),
        "w_exp": gaussian(streams_of[7], (SE, W), SE ** -0.5, 0.25),
        "b_exp": gaussian(streams_of[8], (W,), 0.5, 3.0, (), jnp.float32),
        "w_out": gaussian(streams_of[9], (W, W), W ** -0.5, 0.125),
        "gain_one": jnp.clip(1.0 + 0.1 * jax.random.normal(streams_of[10], (W,), jnp.float32), 0.5, 1.5),
        "shift_one": gaussian(streams_of[11], (W,), 0.3, 1.8, (), jnp.float32),
        "gain_two": jnp.clip(1.0 + 0.1 * jax.random.normal(streams_of[12], (W,), jnp.float32), 0.5, 1.5),
        "shift_two": gaussian(streams_of[13], (W,), 0.3, 1.8, (), jnp.float32),
        "gain_three": jnp.clip(1.0 + 0.1 * jax.random.normal(streams_of[14], (W,), jnp.float32), 0.5, 1.5),
        "shift_three": gaussian(streams_of[15], (W,), 0.3, 1.8, (), jnp.float32),
        "protos": gaussian(streams_of[16], (W, K), 0.2, 1.1953125),
    }


@jax.custom_vjp
def low(v):
    return lax.optimization_barrier(v.astype(jnp.bfloat16)).astype(jnp.float32)

@jax.custom_vjp
def low_back(v):
    return v

def low_keep(v):
    return (low(v), None)

def low_pass(kept, grad):
    return (grad,)

def back_keep(v):
    return (v, None)

def back_low(kept, grad):
    return (low(grad),)
low.defvjp(low_keep, low_pass)
low_back.defvjp(back_keep, back_low)
norm_epsilon = 1e-05
length_epsilon = 1e-06
sharpening_divisor = 0.1
sharpness = 0.05
exact_mode = lax.Precision.HIGHEST

def matmul_exact(left, right):
    return jnp.dot(left, right, precision=exact_mode, preferred_element_type=jnp.float32)

def smooth_gate(values):
    return values * jax.nn.sigmoid(values)

def stream_norm(hidden, gain, shift):
    average = lax.optimization_barrier(jnp.mean(hidden, axis=(0, 1, 2)))
    squares = lax.optimization_barrier(jnp.mean(hidden * hidden, axis=(0, 1, 2)))
    scale_inv = lax.rsqrt(squares - average * average + norm_epsilon)
    return (hidden - average) * scale_inv * gain + shift

def batch_norm(hidden, gain, shift):
    return jnp.concatenate([stream_norm(hidden[:2], gain, shift), stream_norm(hidden[2:], gain, shift)], axis=0)

def grouped_conv(field_rows, kernel, crop_count, edge_cells):
    grid_view = field_rows.reshape(crop_count, edge_cells, edge_cells, NG, GS)
    padded = jnp.pad(grid_view, ((0, 0), (1, 1), (1, 1), (0, 0), (0, 0)))
    summed = jnp.zeros(grid_view.shape, jnp.float32)
    for offset_index in range(9):
        row_shift = offset_index // 3
        col_shift = offset_index % 3
        window = padded[:, row_shift:row_shift + edge_cells, col_shift:col_shift + edge_cells]
        summed = summed + jnp.einsum('nhwgc,gcd->nhwgd', window, kernel[offset_index], precision=exact_mode)
    return summed.reshape(crop_count * edge_cells * edge_cells, W)

def crop_mean(values, per_device, pixels_each):
    return lax.optimization_barrier(jnp.mean(values.reshape(2, GROUPS, per_device, pixels_each, W), axis=3))

def spread_rows(per_crop, pixels_each):
    shaped = jnp.broadcast_to(per_crop[:, :, :, None, :], per_crop.shape[:3] + (pixels_each, W))
    return shaped.reshape(2, GROUPS, ROWS, W)

def forward(pixels, w_in, kernel, w_red, b_red, w_exp, b_exp, w_out, gain_one, shift_one, gain_two, shift_two, gain_three, shift_three, protos):
    flat_in = pixels.reshape(-1, W)
    hidden_one = low_back(matmul_exact(flat_in, w_in)).reshape(pixels.shape)
    act_one = low(smooth_gate(batch_norm(hidden_one, gain_one, shift_one)))
    global_part = grouped_conv(act_one[:2].reshape(-1, W), kernel, 2 * GROUPS * IMG_DEV, SIDE)
    local_part = grouped_conv(act_one[2:].reshape(-1, W), kernel, 2 * GROUPS * SEGS, SMALL_SIDE)
    hidden_two = low_back(jnp.concatenate([global_part.reshape(2, GROUPS, ROWS, W), local_part.reshape(2, GROUPS, ROWS, W)], axis=0))
    act_two = smooth_gate(batch_norm(hidden_two, gain_two, shift_two))

    def excite(values, per_device, pixels_each):
        pooled = crop_mean(values, per_device, pixels_each)
        reduced = smooth_gate(matmul_exact(pooled.reshape(-1, W), w_red) + b_red)
        gate_values = jax.nn.sigmoid(matmul_exact(reduced, w_exp) + b_exp).reshape(pooled.shape)
        return values * spread_rows(gate_values, pixels_each)
    excited = low(jnp.concatenate([excite(act_two[:2], IMG_DEV, SIDE * SIDE), excite(act_two[2:], SEGS, SMALL_SIDE * SMALL_SIDE)], axis=0))
    hidden_three = low_back(matmul_exact(excited.reshape(-1, W), w_out)).reshape(pixels.shape)
    output = smooth_gate(pixels + batch_norm(hidden_three, gain_three, shift_three))

    def project(values, per_device, pixels_each):
        pooled = crop_mean(values, per_device, pixels_each)
        unit_rows = low(pooled * lax.rsqrt(lax.optimization_barrier(jnp.sum(pooled * pooled, axis=-1, keepdims=True)) + length_epsilon))
        return low_back(matmul_exact(unit_rows.reshape(-1, W), protos)).reshape(pooled.shape[:3] + (K,))
    return ((project(output[:2], IMG_DEV, SIDE * SIDE), project(output[2:], SEGS, SMALL_SIDE * SMALL_SIDE)), output)

def balance(match_matrix):
    plan_rows = jnp.exp(match_matrix / sharpness)
    for sweep_index in range(3):
        plan_rows = plan_rows / lax.optimization_barrier(jnp.sum(plan_rows, axis=0, keepdims=True))
        plan_rows = plan_rows / lax.optimization_barrier(jnp.sum(plan_rows, axis=1, keepdims=True))
    return plan_rows

def reference(pixels, counts, slot_order, w_in, kernel, w_red, b_red, w_exp, b_exp, w_out, gain_one, shift_one, gain_two, shift_two, gain_three, shift_three, protos):
    floats = [value.astype(jnp.float32) for value in (pixels, w_in, kernel, w_red, b_red, w_exp, b_exp, w_out, gain_one, shift_one, gain_two, shift_two, gain_three, shift_three, protos)]
    primal, pull_back = jax.vjp(forward, *floats)
    (wide_scores, narrow_scores), output = primal
    first_codes = balance(wide_scores[0].reshape(IMAGES, K)).reshape(GROUPS, IMG_DEV, K)
    second_codes = balance(wide_scores[1].reshape(IMAGES, K)).reshape(GROUPS, IMG_DEV, K)
    ends = jnp.cumsum(counts, axis=1)
    owner = lax.optimization_barrier(jnp.sum((slot_order[:, :, None] >= ends[:, None, :]).astype(jnp.int32), axis=2))
    picks = (owner[:, :, None] == jnp.arange(IMG_DEV, dtype=jnp.int32)[None, None, :]).astype(jnp.float32)
    picks = jnp.transpose(picks.reshape(GROUPS, 2, SEGS, IMG_DEV), (1, 0, 2, 3))
    wide_targets = jnp.stack([second_codes, first_codes])
    narrow_targets = jnp.einsum('cgsi,gik->cgsk', picks, first_codes + second_codes, precision=exact_mode)
    total_pairs = 2 * GROUPS * (IMG_DEV + SLOTS)

    def swav_loss(wide_part, narrow_part):
        wide_logs = jax.nn.log_softmax(wide_part / sharpening_divisor, axis=-1)
        narrow_logs = jax.nn.log_softmax(narrow_part / sharpening_divisor, axis=-1)
        return -(jnp.sum(wide_targets * wide_logs) + jnp.sum(narrow_targets * narrow_logs)) / total_pairs
    loss_value, loss_pull = jax.vjp(swav_loss, wide_scores, narrow_scores)
    grad_wide, grad_narrow = loss_pull(jnp.ones_like(loss_value))
    grads = pull_back(((grad_wide, grad_narrow), jnp.zeros_like(output)))
    return (loss_value, output.astype(jnp.bfloat16), grads[0], grads[1].reshape(-1), grads[2].reshape(-1), grads[3].reshape(-1), grads[5].reshape(-1), grads[7].reshape(-1), grads[14].reshape(-1), grads[4], grads[6], grads[8], grads[9], grads[10], grads[11], grads[12], grads[13])
```

```python
import functools
import jax
import jax.numpy as jnp
from jax import lax
from jax.experimental import pallas as pl
from jax.experimental.pallas import tpu as pltpu

VMEM_LIMIT = 56 * 1024 * 1024
PACK = 4


def window_of(block, width):
    start = block * width
    base = jnp.minimum(start // 128, 13) * 128
    return pl.multiple_of(base, 128), start - base


def take_window(ref, block, width, cast=None):
    base, offset = window_of(block, width)
    value = ref[:, pl.ds(base, 384)]
    if value.dtype != jnp.float32:
        value = value.astype(jnp.float32)
    moved = pltpu.roll(value, jnp.where(offset == 0, 0, 384 - offset), 1)[:, :256]
    lanes = lax.broadcasted_iota(jnp.int32, moved.shape, 1)
    return jnp.where(lanes < width, moved, 0.0)


def put_window(ref, block, width, value):
    base, offset = window_of(block, width)
    wide = jnp.concatenate([value, jnp.zeros((value.shape[0], 128), jnp.float32)], axis=1)
    moved = pltpu.roll(wide, offset, 1)
    lanes = lax.broadcasted_iota(jnp.int32, moved.shape, 1)
    old = ref[:, pl.ds(base, 384)]
    ref[:, pl.ds(base, 384)] = jnp.where(lanes >= offset, moved.astype(ref.dtype), old)


def shift_rows(value, step):
    rows = value.shape[0]
    return pltpu.roll(value, (-step) % rows, 0)


def bn_act(h, p_ref, block, width):
    par = take_window(p_ref, block, width)
    return h * par[0:1] + par[1:2], par


def stack_cols(act, mask_ref, dest):
    dest[:, 0:256] = (shift_rows(act, -1) * mask_ref[0]).astype(jnp.bfloat16)
    dest[:, 256:512] = act.astype(jnp.bfloat16)
    dest[:, 512:768] = (shift_rows(act, 1) * mask_ref[1]).astype(jnp.bfloat16)


def stack_rows(grad, mask_ref, dest, side):
    dest[:, 0:256] = (shift_rows(grad, side) * mask_ref[3]).astype(jnp.bfloat16)
    dest[:, 256:512] = grad.astype(jnp.bfloat16)
    dest[:, 512:768] = (shift_rows(grad, -side) * mask_ref[2]).astype(jnp.bfloat16)


def fwd_kernel(width, sides, glob_ref, h_ref, p_ref, mask_ref, k_ref, out_ref, st_ref, stack):
    block = pl.program_id(0)
    h = take_window(h_ref, block, width)
    pre, _ = bn_act(h, p_ref, block, width)
    act = pre * jax.nn.sigmoid(pre)
    stack_cols(act.astype(jnp.bfloat16).astype(jnp.float32), mask_ref, stack)
    y = jnp.dot(stack[...], k_ref[0], preferred_element_type=jnp.float32)

    def finish(side):
        total = (
            y[:, 256:512]
            + shift_rows(y[:, 0:256], -side) * mask_ref[2]
            + shift_rows(y[:, 512:768], side) * mask_ref[3]
        )
        put_window(out_ref, block, width, total)
        sums = jnp.concatenate(
            [
                jnp.sum(total, axis=0, keepdims=True),
                jnp.sum(total * total, axis=0, keepdims=True),
                jnp.zeros((6, 256), jnp.float32),
            ],
            axis=0,
        )
        put_window(st_ref, block, width, sums)

    @pl.when(glob_ref[0] == 1)
    def _():
        finish(sides[0])

    @pl.when(glob_ref[0] == 0)
    def _():
        finish(sides[1])


def dgrad_kernel(width, sides, glob_ref, g_ref, h_ref, p_ref, mask_ref, k_ref, out_ref, st_ref, stack):
    block = pl.program_id(0)
    grad = take_window(g_ref, block, width)

    @pl.when(glob_ref[0] == 1)
    def _():
        stack_rows(grad, mask_ref, stack, sides[0])

    @pl.when(glob_ref[0] == 0)
    def _():
        stack_rows(grad, mask_ref, stack, sides[1])

    z = lax.dot_general(
        stack[...], k_ref[0], (((1,), (1,)), ((), ())), preferred_element_type=jnp.float32
    )
    total = (
        z[:, 256:512]
        + shift_rows(z[:, 0:256], 1) * mask_ref[1]
        + shift_rows(z[:, 512:768], -1) * mask_ref[0]
    )
    h = take_window(h_ref, block, width)
    pre, par = bn_act(h, p_ref, block, width)
    sig = jax.nn.sigmoid(pre)
    ga = total * (sig * (1.0 + pre * (1.0 - sig)))
    xhat = h * par[2:3] + par[3:4]
    put_window(out_ref, block, width, ga)
    sums = jnp.concatenate(
        [
            jnp.sum(ga, axis=0, keepdims=True),
            jnp.sum(ga * xhat, axis=0, keepdims=True),
            jnp.zeros((6, 256), jnp.float32),
        ],
        axis=0,
    )
    put_window(st_ref, block, width, sums)


def wgrad_kernel(width, sides, glob_ref, g_ref, h_ref, p_ref, mask_ref, out_ref, cols, rows):
    block = pl.program_id(0)
    h = take_window(h_ref, block, width)
    pre, _ = bn_act(h, p_ref, block, width)
    stack_cols((pre * jax.nn.sigmoid(pre)).astype(jnp.bfloat16).astype(jnp.float32), mask_ref, cols)
    grad = take_window(g_ref, block, width)

    @pl.when(glob_ref[0] == 1)
    def _():
        stack_rows(grad, mask_ref, rows, sides[0])

    @pl.when(glob_ref[0] == 0)
    def _():
        stack_rows(grad, mask_ref, rows, sides[1])

    gw = width // PACK
    for dx in range(3):
        acc = lax.dot_general(
            cols[:, 256 * dx : 256 * dx + 256],
            rows[...],
            (((0,), (0,)), ((), ())),
            preferred_element_type=jnp.float32,
        )
        lanes = lax.broadcasted_iota(jnp.int32, (gw, 256), 1)
        for dy in range(3):
            small = jnp.zeros((gw, 256), jnp.float32)
            for g in range(PACK):
                piece = acc[gw * g : gw * g + gw, 256 * dy : 256 * dy + 256]
                small = jnp.where((lanes >= gw * g) & (lanes < gw * g + gw), piece, small)
            out_ref[3 * dy + dx, 0] = small


def pack_kernel(gw, kc_ref, out_ref):
    lanes = lax.broadcasted_iota(jnp.int32, (gw, 256), 1)
    for dy in range(3):
        for dx in range(3):
            small = kc_ref[3 * dy + dx, 0].astype(jnp.float32)
            parts = [
                jnp.where((lanes >= gw * g) & (lanes < gw * g + gw), small, 0.0)
                for g in range(PACK)
            ]
            parts.append(jnp.zeros((256 - PACK * gw, 256), jnp.float32))
            out_ref[0, 256 * dx : 256 * dx + 256, 256 * dy : 256 * dy + 256] = jnp.concatenate(
                parts, axis=0
            ).astype(jnp.bfloat16)


def params():
    return pltpu.CompilerParams(vmem_limit_bytes=VMEM_LIMIT)


def pack_blocks(kernel):
    taps, groups, gw, _ = kernel.shape
    blocks = groups // PACK
    kc = kernel.reshape(taps, blocks, PACK, gw, gw).transpose(0, 1, 3, 2, 4).reshape(taps, blocks, gw, PACK * gw)
    kc = jnp.pad(kc, ((0, 0), (0, 0), (0, 0), (0, 256 - PACK * gw)))
    return pl.pallas_call(
        functools.partial(pack_kernel, gw),
        grid=(blocks,),
        in_specs=[pl.BlockSpec((taps, 1, gw, 256), lambda b: (0, b, 0, 0))],
        out_specs=pl.BlockSpec((1, 768, 768), lambda b: (b, 0, 0)),
        out_shape=jax.ShapeDtypeStruct((blocks, 768, 768), jnp.bfloat16),
        compiler_params=params(),
        name="pack",
    )(kc)


def conv_specs(rows):
    whole = lambda r: pl.BlockSpec((r, 2048), lambda b, s: (0, 0))
    mask = pl.BlockSpec((4, rows, 256), lambda b, s: (0, 0, 0))
    kern = pl.BlockSpec((1, 768, 768), lambda b, s: (b, 0, 0))
    return whole, mask, kern


def conv_fwd(glob, h, par, masks, packed, width, sides):
    rows, chans = h.shape
    whole, mask, kern = conv_specs(rows)
    return pl.pallas_call(
        functools.partial(fwd_kernel, width, sides),
        grid_spec=pltpu.PrefetchScalarGridSpec(
            num_scalar_prefetch=1,
            grid=(packed.shape[0],),
            in_specs=[whole(rows), whole(8), mask, kern],
            out_specs=[whole(rows), whole(8)],
            scratch_shapes=[pltpu.VMEM((rows, 768), jnp.bfloat16)],
        ),
        out_shape=[
            jax.ShapeDtypeStruct((rows, chans), jnp.float32),
            jax.ShapeDtypeStruct((8, chans), jnp.float32),
        ],
        compiler_params=params(),
        name="conv_fwd",
    )(glob, h, par, masks, packed)


def conv_dgrad(glob, grad, h, par, masks, packed, width, sides):
    rows, chans = h.shape
    whole, mask, kern = conv_specs(rows)
    return pl.pallas_call(
        functools.partial(dgrad_kernel, width, sides),
        grid_spec=pltpu.PrefetchScalarGridSpec(
            num_scalar_prefetch=1,
            grid=(packed.shape[0],),
            in_specs=[whole(rows), whole(rows), whole(8), mask, kern],
            out_specs=[whole(rows), whole(8)],
            scratch_shapes=[pltpu.VMEM((rows, 768), jnp.bfloat16)],
        ),
        out_shape=[
            jax.ShapeDtypeStruct((rows, chans), jnp.float32),
            jax.ShapeDtypeStruct((8, chans), jnp.float32),
        ],
        compiler_params=params(),
        name="conv_dgrad",
    )(glob, grad, h, par, masks, packed)


def conv_wgrad(glob, grad, h, par, masks, blocks, width, sides):
    rows, chans = h.shape
    whole, mask, kern = conv_specs(rows)
    gw = width // PACK
    return pl.pallas_call(
        functools.partial(wgrad_kernel, width, sides),
        grid_spec=pltpu.PrefetchScalarGridSpec(
            num_scalar_prefetch=1,
            grid=(blocks,),
            in_specs=[whole(rows), whole(rows), whole(8), mask],
            out_specs=pl.BlockSpec((9, 1, gw, 256), lambda b, s: (0, b, 0, 0)),
            scratch_shapes=[pltpu.VMEM((rows, 768), jnp.bfloat16)] * 2,
        ),
        out_shape=jax.ShapeDtypeStruct((9, blocks, gw, 256), jnp.float32),
        compiler_params=params(),
        name="conv_wgrad",
    )(glob, grad, h, par, masks)


from jax.sharding import PartitionSpec as P

IMG_DEV = 4
SIDE = 14
SMALL_SIDE = 7

norm_epsilon = 1e-05
length_epsilon = 1e-06
sharpening_divisor = 0.1
sharpness = 0.05
exact_mode = lax.Precision.HIGHEST


def swap(value, axis, mask):
    pairs = [(source, source ^ mask) for source in range(lax.axis_size(axis))]
    return lax.ppermute(value, axis, pairs)


def smooth_gate(values):
    return values * jax.nn.sigmoid(values)


def smooth_slope(values):
    sigma_values = jax.nn.sigmoid(values)
    return sigma_values * (1.0 + values * (1.0 - sigma_values))


def exact_dot(left, right):
    return jnp.dot(left, right, precision=exact_mode, preferred_element_type=jnp.float32)


def bits_of(size):
    return [1 << bit for bit in range(size.bit_length() - 1)]


def img_sum(value):
    for mask in bits_of(lax.axis_size("img")):
        value = value + swap(value, "img", mask)
    return value


def stream_sum(value):
    value = value + swap(value, "crop", 1)
    return img_sum(value)


def pick(value, index, axis):
    return lax.dynamic_index_in_dim(value, index, axis, keepdims=False)


def slab_rows(width, devices):
    return -(-(width // devices) // 8) * 8


def slab_offset(index, width, devices):
    share = width // devices
    return 2 * share * (index // 2) + (index % 2) * (2 * share - slab_rows(width, devices))


def slab_kernel(core_ref, left_ref, right_ref, out_ref):
    out_ref[0] = lax.dot_general(
        left_ref[0], right_ref[...], (((0,), (0,)), ((), ())), preferred_element_type=jnp.float32
    )


def slab_product(core, left, right):
    slabs, rows, height = left.shape
    wide = right.shape[1]
    return pl.pallas_call(
        slab_kernel,
        grid_spec=pltpu.PrefetchScalarGridSpec(
            num_scalar_prefetch=1,
            grid=(slabs // 2,),
            in_specs=[
                pl.BlockSpec((1, rows, height), lambda z, c: (2 * z + c[0], 0, 0)),
                pl.BlockSpec((rows, wide), lambda z, c: (0, 0)),
            ],
            out_specs=pl.BlockSpec((1, height, wide), lambda z, c: (z, 0, 0)),
        ),
        out_shape=jax.ShapeDtypeStruct((slabs // 2, height, wide), jnp.float32),
        compiler_params=pltpu.CompilerParams(vmem_limit_bytes=32 * 1024 * 1024),
        name="slab_product",
    )(core, left, right)


def share_kernel(left_ref, right_ref, out_ref):
    out_ref[...] = lax.dot_general(
        left_ref[...].astype(jnp.bfloat16),
        right_ref[...].astype(jnp.bfloat16),
        (((0,), (0,)), ((), ())),
        preferred_element_type=jnp.float32,
    )


def share_product(left, right):
    return pl.pallas_call(
        share_kernel,
        out_shape=jax.ShapeDtypeStruct((left.shape[1], right.shape[1]), jnp.float32),
        compiler_params=pltpu.CompilerParams(vmem_limit_bytes=32 * 1024 * 1024),
        name="share_product",
    )(left, right)


def make_slabs(value, devices):
    width = value.shape[1]
    height = slab_rows(width, devices)
    return jnp.stack(
        [
            lax.slice_in_dim(value, start, start + height, axis=1)
            for start in (slab_offset(i, width, devices) for i in range(devices))
        ]
    )


def crop_scatter(value):
    lead, rows, cols = value.shape
    crop = lax.axis_index("crop")
    bits = (crop & 1, crop >> 1)
    whole = value.reshape(lead, 2, 2, 2, rows // 8, cols)
    parts = []
    for half, order in ((0, (0, 1)), (1, (1, 0))):
        part = whole[:, half]
        for axis in order:
            part = pick(part, bits[axis], 1) + swap(pick(part, 1 - bits[axis], 1), "crop", 1 << axis)
        parts.append(part)
    return parts


def crop_gather(parts):
    crop = lax.axis_index("crop")
    bits = (crop & 1, crop >> 1)
    halves = []
    for part, order in zip(parts, ((1, 0), (0, 1))):
        for axis in order:
            other = swap(part, "crop", 1 << axis)
            upper = bits[axis] == 1
            part = jnp.stack(
                [jnp.where(upper, other, part), jnp.where(upper, part, other)], axis=1
            ) if part.ndim == 3 else jnp.stack(
                [jnp.where(upper, other, part), jnp.where(upper, part, other)], axis=1
            )
        halves.append(part)
    both = jnp.stack(halves, axis=1)
    lead, cols = both.shape[0], both.shape[-1]
    return both.reshape(lead, -1, cols)


def chip_scatter(value):
    chip = lax.axis_index("img") // 2
    for mask in bits_of(value.shape[0]):
        bit = (chip // mask) % 2
        value = value.reshape((value.shape[0] // 2, 2) + value.shape[1:])
        value = pick(value, bit, 1) + swap(pick(value, 1 - bit, 1), "img", 2 * mask)
    return value[0]


def shards(
    pixels,
    counts,
    slot_order,
    w_in,
    kernel,
    w_red,
    b_red,
    w_exp,
    b_exp,
    w_out,
    gain_one,
    shift_one,
    gain_two,
    shift_two,
    gain_three,
    shift_three,
    protos,
):
    row_count = pixels.shape[2]
    width = pixels.shape[3]
    proto_count = protos.shape[1]
    squeeze = w_red.shape[1]
    seg_count = row_count // (SMALL_SIDE * SMALL_SIDE)
    slot_total = slot_order.shape[1]
    devices = lax.axis_size("img")
    img_index = lax.axis_index("img")
    crop_index = lax.axis_index("crop")
    core = img_index % 2
    fast = width % devices == 0 and (2 * width // devices) % 8 == 0
    is_global = crop_index < 2
    glob = is_global.astype(jnp.int32).reshape(1)
    stream_rows = 2.0 * devices * row_count
    couple_number = 2.0 * devices * (IMG_DEV + slot_total)
    inputs = pixels.reshape(row_count, width)
    row_ids = jnp.arange(row_count, dtype=jnp.int32)
    side = jnp.where(is_global, SIDE, SMALL_SIDE)
    seg_of_row = row_ids // (side * side)
    across = row_ids % side
    down = (row_ids // side) % side
    masks = jnp.stack([across > 0, across < side - 1, down > 0, down < side - 1])
    masks = jnp.broadcast_to(masks.astype(jnp.float32)[:, :, None], (4, row_count, 256))
    member = (seg_of_row[None, :] == jnp.arange(seg_count, dtype=jnp.int32)[:, None]).astype(
        jnp.float32
    )
    member_rows = member.T
    crop_pixels = jnp.where(is_global, float(SIDE * SIDE), float(SMALL_SIDE * SMALL_SIDE))
    block_width = PACK * kernel.shape[2]
    block_count = kernel.shape[1] // PACK
    sides = (SIDE, SMALL_SIDE)

    def norm_rows(local_sums, gain, shift):
        sums = stream_sum(local_sums)
        average = sums[0] / stream_rows
        inv = lax.rsqrt(sums[1] / stream_rows - average * average + norm_epsilon)
        return average, inv

    def back_rows(local_sums, gain, inv):
        sums = stream_sum(local_sums)
        return sums, gain * inv, sums[0] / stream_rows, sums[1] / stream_rows

    hidden_one = jnp.dot(inputs, w_in, preferred_element_type=jnp.float32)
    sums = jnp.stack([jnp.sum(hidden_one, axis=0), jnp.sum(hidden_one * hidden_one, axis=0)])
    mean_one, inv_one = norm_rows(sums, gain_one, shift_one)
    packed = pack_blocks(kernel)
    zero_row = jnp.zeros((width,), jnp.float32)
    scale_one = gain_one * inv_one
    par = jnp.stack(
        [scale_one, shift_one - mean_one * scale_one, inv_one, -mean_one * inv_one] + [zero_row] * 4
    )
    hidden_two, sums = conv_fwd(glob, hidden_one, par, masks, packed, block_width, sides)
    mean_two, inv_two = norm_rows(sums[:2], gain_two, shift_two)
    centred_two = (hidden_two - mean_two) * inv_two
    pre_two = centred_two * gain_two + shift_two
    act_two = smooth_gate(pre_two)
    red_float = w_red.astype(jnp.float32)
    exp_float = w_exp.astype(jnp.float32)
    pooled = exact_dot(member, act_two) / crop_pixels
    reduce_pre = exact_dot(pooled, red_float) + b_red
    reduced = smooth_gate(reduce_pre)
    gate_values = jax.nn.sigmoid(exact_dot(reduced, exp_float) + b_exp)
    gate_rows = exact_dot(member_rows, gate_values)
    excited = (act_two * gate_rows).astype(jnp.bfloat16)
    hidden_three = jnp.dot(excited, w_out, preferred_element_type=jnp.float32)
    sums = jnp.stack([jnp.sum(hidden_three, axis=0), jnp.sum(hidden_three * hidden_three, axis=0)])
    mean_three, inv_three = norm_rows(sums, gain_three, shift_three)
    centred_three = (hidden_three - mean_three) * inv_three
    summed_in = inputs.astype(jnp.float32) + centred_three * gain_three + shift_three
    output = smooth_gate(summed_in)
    pooled_out = exact_dot(member, output) / crop_pixels
    length_inv = lax.rsqrt(jnp.sum(pooled_out * pooled_out, axis=1, keepdims=True) + length_epsilon)
    unit_wide = pooled_out * length_inv
    unit_rows = unit_wide.astype(jnp.bfloat16)
    match_matrix = jnp.dot(unit_rows, protos, preferred_element_type=jnp.float32)

    every = match_matrix[:IMG_DEV]
    for mask in bits_of(devices):
        every = jnp.concatenate([every, swap(every, "img", mask)], axis=0)
    plan_rows = jnp.exp(every / sharpness)
    for sweep_index in range(3):
        plan_rows = plan_rows / jnp.sum(plan_rows, axis=0, keepdims=True)
        plan_rows = plan_rows / jnp.sum(plan_rows, axis=1, keepdims=True)
    codes = plan_rows[:IMG_DEV]
    partner = lax.ppermute(codes, "crop", [(0, 1), (1, 0)])
    both_codes = lax.ppermute(codes, "crop", [(0, 2), (1, 3)]) + lax.ppermute(
        codes, "crop", [(0, 3), (1, 2)]
    )
    wide_target = jnp.concatenate(
        [partner, jnp.zeros((seg_count - IMG_DEV, proto_count), jnp.float32)], axis=0
    )
    ends = [jnp.sum(counts[0, : i + 1]) for i in range(IMG_DEV)]
    first_slot = jnp.maximum(crop_index - 2, 0) * seg_count
    order_here = lax.dynamic_slice_in_dim(slot_order[0], first_slot, seg_count)
    owner = sum((order_here >= end).astype(jnp.int32) for end in ends)
    narrow_target = jnp.zeros((seg_count, proto_count), jnp.float32)
    for i in range(IMG_DEV):
        narrow_target = jnp.where(owner[:, None] == i, both_codes[i : i + 1], narrow_target)
    target = jnp.where(is_global, wide_target, narrow_target)
    sharpened = match_matrix / sharpening_divisor
    shifted = sharpened - jnp.max(sharpened, axis=1, keepdims=True)
    log_probs = shifted - jnp.log(jnp.sum(jnp.exp(shifted), axis=1, keepdims=True))
    loss_here = -jnp.sum(target * log_probs) / couple_number
    scores_wide = (jnp.exp(log_probs) * jnp.sum(target, axis=1, keepdims=True) - target) / (
        sharpening_divisor * couple_number
    )
    grad_scores = scores_wide.astype(jnp.bfloat16)

    grad_unit = jnp.einsum("sk,wk->sw", grad_scores, protos, preferred_element_type=jnp.float32)
    inner_term = jnp.sum(pooled_out * grad_unit, axis=1, keepdims=True)
    grad_pooled_out = (
        length_inv * grad_unit - pooled_out * length_inv * length_inv * length_inv * inner_term
    )
    grad_output = exact_dot(member_rows, grad_pooled_out / crop_pixels)
    grad_summed = grad_output * smooth_slope(summed_in)
    sums_three, scale_three, first, second = back_rows(
        jnp.stack([jnp.sum(grad_summed, axis=0), jnp.sum(grad_summed * centred_three, axis=0)]),
        gain_three,
        inv_three,
    )
    grad_three_low = (scale_three * (grad_summed - first - centred_three * second)).astype(
        jnp.bfloat16
    )
    grad_excited = jnp.einsum(
        "rv,wv->rw", grad_three_low, w_out, preferred_element_type=jnp.float32
    )
    grad_gate = exact_dot(member, grad_excited * act_two)
    grad_gate_pre = grad_gate * gate_values * (1.0 - gate_values)
    grad_reduce_pre = exact_dot(grad_gate_pre, exp_float.T) * smooth_slope(reduce_pre)
    grad_pooled = exact_dot(grad_reduce_pre, red_float.T)
    grad_act_two = grad_excited * gate_rows + exact_dot(member_rows, grad_pooled / crop_pixels)
    grad_pre_two = grad_act_two * smooth_slope(pre_two)
    bias_row = jnp.concatenate(
        [
            jnp.sum(grad_reduce_pre, axis=0),
            loss_here.reshape(1),
            jnp.zeros((width - squeeze - 1,), jnp.float32),
        ]
    )
    sums_two, scale_two, first, second = back_rows(
        jnp.stack(
            [
                jnp.sum(grad_pre_two, axis=0),
                jnp.sum(grad_pre_two * centred_two, axis=0),
                jnp.sum(grad_gate_pre, axis=0),
                bias_row,
            ]
        ),
        gain_two,
        inv_two,
    )
    grad_two_low = (scale_two * (grad_pre_two - first - centred_two * second)).astype(jnp.bfloat16)
    grad_pre_one, sums = conv_dgrad(
        glob, grad_two_low, hidden_one, par, masks, packed, block_width, sides
    )
    sums_one, scale_one, first, second = back_rows(sums[:2], gain_one, inv_one)
    small_kernel = conv_wgrad(
        glob, grad_two_low, hidden_one, par, masks, block_count, block_width, sides
    )
    centred_one = (hidden_one - mean_one) * inv_one
    grad_one_low = (scale_one * (grad_pre_one - first - centred_one * second)).astype(jnp.bfloat16)
    grad_inputs = (
        jnp.einsum("rv,wv->rw", grad_one_low, w_in, preferred_element_type=jnp.float32)
        + grad_summed
    )

    last = jnp.concatenate([sums_one, sums_two, sums_three], axis=0)
    last = last + swap(last, "crop", 2)
    tail = (
        last[5, :squeeze],
        last[4],
        last[1],
        last[0],
        last[3],
        last[2],
        last[7],
        last[6],
    )
    loss_total = last[5, squeeze]

    if fast:
        share = width // devices
        near = core.reshape(1)
        far = (1 - core).reshape(1)

        def kept(value):
            skip = core * (value.shape[0] - share)
            return lax.dynamic_slice_in_dim(value, skip, share, axis=0)

        def my_columns(value):
            count = value.shape[1] // devices
            return lax.dynamic_slice_in_dim(value, img_index * count, count, axis=1)

        seen = lax.all_gather(
            jnp.concatenate([unit_wide, scores_wide], axis=1), "img", tiled=True
        )
        share_protos = share_product(my_columns(seen[:, :width]), seen[:, width:])
        seen = lax.all_gather(
            jnp.concatenate([pooled, reduced, grad_reduce_pre, grad_gate_pre], axis=1),
            "img",
            tiled=True,
        )
        share_red = exact_dot(
            my_columns(seen[:, :width]).T, seen[:, width + squeeze : width + 2 * squeeze]
        )
        share_exp = exact_dot(
            my_columns(seen[:, width : width + squeeze]).T, seen[:, width + 2 * squeeze :]
        )

        def pad_rows(value):
            rows = -(-value.shape[0] // 64) * 64
            return jnp.pad(value, ((0, rows - value.shape[0]), (0, 0)))

        slabs = make_slabs(excited, devices)
        own = slab_product(near, slabs, grad_three_low)
        own = own + swap(slab_product(far, slabs, grad_three_low), "img", 1)
        share_out = chip_scatter(own)
        pieces = [share_out, share_protos, share_red, share_exp]
        summed = [crop_gather(crop_scatter(pad_rows(piece)[None]))[0] for piece in pieces]
        flat_out = kept(summed[0][: share_out.shape[0]]).reshape(-1)
        flat_protos = summed[1][: share_protos.shape[0]].reshape(-1)
        flat_red = summed[2][: share_red.shape[0]].reshape(-1)
        flat_exp = summed[3][: share_exp.shape[0]].reshape(-1)

        slabs = make_slabs(inputs, devices)
        own = slab_product(near, slabs, grad_one_low)
        own = own + swap(slab_product(far, slabs, grad_one_low), "img", 1)
        parts = [chip_scatter(part)[None] for part in crop_scatter(own)]
        flat_in = kept(crop_gather(parts)[0]).reshape(-1)

        gw = kernel.shape[2]
        units = small_kernel.reshape(9 * block_count, gw, 256)
        total = kernel.size // devices
        unit_size = gw * gw * PACK
        span = -(-total // unit_size) + 1
        firsts = [min(total * i // unit_size, units.shape[0] - span) for i in range(devices)]
        slabs = jnp.stack([units[f : f + span] for f in firsts])
        mine = lax.psum_scatter(slabs, "img", scatter_dimension=0, tiled=False)
        mine = lax.psum(mine, "crop")
        mine = mine[:, :, : PACK * gw].reshape(span, gw, PACK, gw).transpose(0, 2, 1, 3).reshape(-1)
        skips = jnp.asarray([total * i - unit_size * f for i, f in enumerate(firsts)], jnp.int32)
        flat_kernel = lax.dynamic_slice_in_dim(mine, skips[img_index], total)
        shares = (flat_in, flat_kernel, flat_red, flat_exp, flat_out, flat_protos)
    else:
        gw = kernel.shape[2]
        grads = (
            jnp.einsum("rw,rv->wv", inputs, grad_one_low, preferred_element_type=jnp.float32),
            small_kernel[..., : PACK * gw]
            .reshape(9, block_count, gw, PACK, gw)
            .transpose(0, 1, 3, 2, 4),
            exact_dot(pooled.T, grad_reduce_pre),
            exact_dot(reduced.T, grad_gate_pre),
            jnp.einsum("rw,rv->wv", excited, grad_three_low, preferred_element_type=jnp.float32),
            jnp.einsum("sw,sk->wk", unit_rows, grad_scores, preferred_element_type=jnp.float32),
        )
        shares = tuple(
            lax.psum(
                lax.psum_scatter(grad.reshape(-1), "img", scatter_dimension=0, tiled=True), "crop"
            )
            for grad in grads
        )
    return (
        loss_total,
        output.astype(jnp.bfloat16).reshape(pixels.shape),
        grad_inputs.reshape(pixels.shape),
        *shares,
        *tail,
    )


def solution(mesh):
    return jax.shard_map(
        shards,
        mesh=mesh,
        in_specs=(P("crop", "img", None, None), P("img", None), P("img", None)) + (P(),) * 14,
        out_specs=(P(), P("crop", "img", None, None), P("crop", "img", None, None))
        + (P("img"),) * 6
        + (P(),) * 8,
        check_vma=False,
    )
```

```python
import functools
import jax
import jax.numpy as jnp
from jax import lax
from jax.experimental import pallas as pl
from jax.experimental.pallas import tpu as pltpu

VMEM_LIMIT = 56 * 1024 * 1024
PACK = 4
EDGE = 16
CHUNK = 112


def cost(micros):
    return pl.CostEstimate(flops=micros * 1000000, bytes_accessed=micros * 1000, transcendentals=0)


def params():
    return pltpu.CompilerParams(vmem_limit_bytes=VMEM_LIMIT)


def lane_of(rows):
    return lax.broadcasted_iota(jnp.int32, (rows, 128), 1)


def take(refs, start, rows, skip, width):
    a, b, c = [ref[start : start + rows, :].astype(jnp.float32) for ref in refs]
    back = lax.rem(128 - skip, 128)
    a, b, c = [pltpu.roll(v, back, 1) for v in (a, b, c)]
    lane = lane_of(rows)
    near = lane < 128 - skip
    return jnp.where(near, a, b), jnp.where(lane < width - 128, jnp.where(near, b, c), 0.0)


def put(ref, start, rows, base, skip, first, second):
    first, second = pltpu.roll(first, skip, 1), pltpu.roll(second, skip, 1)
    lane = lane_of(rows)
    inside = lane >= skip
    last = jnp.minimum(base + 2, ref.shape[1] // 128 - 1)

    def at(tile):
        return (slice(start, start + rows), pl.ds(pl.multiple_of(tile * 128, 128), 128))

    ref[at(last)] = second
    ref[at(base + 1)] = jnp.where(inside, second, first)
    ref[at(base)] = jnp.where(inside, first, ref[at(base)])


def place_of(block, width):
    start = block * width
    base = start // 128
    return base, start - base * 128


def clear_edges(ref):
    @pl.when(pl.program_id(0) == 0)
    def _():
        ref[0:EDGE, :] = jnp.zeros((EDGE, ref.shape[1]), ref.dtype)
        ref[ref.shape[0] - EDGE :, :] = jnp.zeros((EDGE, ref.shape[1]), ref.dtype)


def chunks(rows):
    return range(0, rows, CHUNK)


def fill_act(h_refs, p_refs, skip, width, starts, act):
    scale = take(p_refs, 0, 8, skip, width)
    for r in starts:
        for tile, h in enumerate(take(h_refs, r, CHUNK, skip, width)):
            pre = h * scale[tile][0:1] + scale[tile][1:2]
            value = pre * jax.nn.sigmoid(pre)
            act[EDGE + r : EDGE + r + CHUNK, 128 * tile : 128 * tile + 128] = value.astype(
                jnp.bfloat16
            ).astype(jnp.float32)


def fill_grad(g_refs, skip, width, starts, grad):
    for r in starts:
        for tile, g in enumerate(take(g_refs, r, CHUNK, skip, width)):
            grad[EDGE + r : EDGE + r + CHUNK, 128 * tile : 128 * tile + 128] = g


def stack(source, mask_ref, low, high, step, starts, dest):
    for r in starts:
        for tile in range(2):
            cols = slice(128 * tile, 128 * tile + 128)
            here = slice(r, r + CHUNK)
            before = source[EDGE + r - step : EDGE + r - step + CHUNK, cols] * mask_ref[low, here, :]
            after = source[EDGE + r + step : EDGE + r + step + CHUNK, cols] * mask_ref[high, here, :]
            middle = source[EDGE + r : EDGE + r + CHUNK, cols]
            dest[here, 128 * tile : 128 * tile + 128] = before.astype(jnp.bfloat16)
            dest[here, 256 + 128 * tile : 384 + 128 * tile] = middle.astype(jnp.bfloat16)
            dest[here, 512 + 128 * tile : 640 + 128 * tile] = after.astype(jnp.bfloat16)


def fwd_step(width, side, glob_ref, refs):
    h_refs, p_refs, (mask_ref, k_ref, out_ref, st_ref, act, cols, wide) = refs[:3], refs[3:6], refs[6:]
    rows = h_refs[0].shape[0]
    base, skip = place_of(pl.program_id(0), width)
    starts = list(chunks(rows))
    fill_act(h_refs, p_refs, skip, width, starts[:1], act)
    for i, r in enumerate(starts):
        fill_act(h_refs, p_refs, skip, width, starts[i + 1 : i + 2], act)
        stack(act, mask_ref, 0, 1, 1, [r], cols)
        wide[EDGE + r : EDGE + r + CHUNK, :] = jnp.dot(
            cols[r : r + CHUNK, :], k_ref[0], preferred_element_type=jnp.float32
        )
    sums = [jnp.zeros((8, 128), jnp.float32)] * 4
    for r in starts:
        here = slice(r, r + CHUNK)
        tiles = []
        for tile in range(2):
            lo = 128 * tile
            total = (
                wide[EDGE + r : EDGE + r + CHUNK, 256 + lo : 384 + lo]
                + wide[EDGE + r - side : EDGE + r - side + CHUNK, lo : 128 + lo] * mask_ref[2, here, :]
                + wide[EDGE + r + side : EDGE + r + side + CHUNK, 512 + lo : 640 + lo] * mask_ref[3, here, :]
            )
            tiles.append(total)
            sums[tile] += jnp.sum(total.reshape(-1, 8, 128), axis=0)
            sums[2 + tile] += jnp.sum((total * total).reshape(-1, 8, 128), axis=0)
        put(out_ref, r, CHUNK, base, skip, *tiles)
    put_sums(st_ref, base, skip, sums)


def put_sums(st_ref, base, skip, sums):
    line = lax.broadcasted_iota(jnp.int32, (8, 128), 0)
    tiles = [
        jnp.where(
            line == 0,
            jnp.sum(sums[tile], axis=0, keepdims=True),
            jnp.sum(sums[2 + tile], axis=0, keepdims=True),
        )
        for tile in range(2)
    ]
    put(st_ref, 0, 8, base, skip, *tiles)


def dgrad_step(width, side, glob_ref, refs):
    g_refs, h_refs, p_refs = refs[:3], refs[3:6], refs[6:9]
    mask_ref, k_ref, out_ref, st_ref, grad, lines, wide = refs[9:]
    rows = h_refs[0].shape[0]
    base, skip = place_of(pl.program_id(0), width)
    starts = list(chunks(rows))
    fill_grad(g_refs, skip, width, starts[:1], grad)
    for i, r in enumerate(starts):
        fill_grad(g_refs, skip, width, starts[i + 1 : i + 2], grad)
        stack_lines(grad, mask_ref, side, [r], lines)
    wide[EDGE : EDGE + rows, :] = lax.dot_general(
        lines[...], k_ref[0], (((1,), (1,)), ((), ())), preferred_element_type=jnp.float32
    )
    par = take(p_refs, 0, 8, skip, width)
    sums = [jnp.zeros((8, 128), jnp.float32)] * 4
    for r in starts:
        here = slice(r, r + CHUNK)
        h_tiles = take(h_refs, r, CHUNK, skip, width)
        tiles = []
        for tile in range(2):
            lo = 128 * tile
            total = (
                wide[EDGE + r : EDGE + r + CHUNK, 256 + lo : 384 + lo]
                + wide[EDGE + r + 1 : EDGE + r + 1 + CHUNK, lo : 128 + lo] * mask_ref[1, here, :]
                + wide[EDGE + r - 1 : EDGE + r - 1 + CHUNK, 512 + lo : 640 + lo] * mask_ref[0, here, :]
            )
            p = par[tile]
            pre = h_tiles[tile] * p[0:1] + p[1:2]
            sig = jax.nn.sigmoid(pre)
            ga = total * (sig * (1.0 + pre * (1.0 - sig)))
            xhat = h_tiles[tile] * p[2:3] + p[3:4]
            tiles.append(ga)
            sums[tile] += jnp.sum(ga.reshape(-1, 8, 128), axis=0)
            sums[2 + tile] += jnp.sum((ga * xhat).reshape(-1, 8, 128), axis=0)
        put(out_ref, r, CHUNK, base, skip, *tiles)
    put_sums(st_ref, base, skip, sums)


def stack_lines(grad, mask_ref, side, starts, dest):
    for r in starts:
        for tile in range(2):
            cols = slice(128 * tile, 128 * tile + 128)
            here = slice(r, r + CHUNK)
            below = grad[EDGE + r + side : EDGE + r + side + CHUNK, cols] * mask_ref[3, here, :]
            above = grad[EDGE + r - side : EDGE + r - side + CHUNK, cols] * mask_ref[2, here, :]
            middle = grad[EDGE + r : EDGE + r + CHUNK, cols]
            dest[here, 128 * tile : 128 * tile + 128] = below.astype(jnp.bfloat16)
            dest[here, 256 + 128 * tile : 384 + 128 * tile] = middle.astype(jnp.bfloat16)
            dest[here, 512 + 128 * tile : 640 + 128 * tile] = above.astype(jnp.bfloat16)


def wgrad_step(width, side, glob_ref, refs):
    g_refs, h_refs, p_refs = refs[:3], refs[3:6], refs[6:9]
    mask_ref, out_ref, source, grad, cols, lines = refs[9], *refs[-5:]
    rows = h_refs[0].shape[0]
    block = pl.program_id(0) + glob_ref[1]
    _, skip = place_of(block, width)
    starts = list(chunks(rows))
    fill_act(h_refs, p_refs, skip, width, starts, source)
    fill_grad(g_refs, skip, width, starts, grad)
    stack(source, mask_ref, 0, 1, 1, starts, cols)
    stack_lines(grad, mask_ref, side, starts, lines)
    gw = width // PACK
    lanes = lax.broadcasted_iota(jnp.int32, (gw, 256), 1)
    for dx in range(3):
        acc = lax.dot_general(
            cols[:, 256 * dx : 256 * dx + 256],
            lines[...],
            (((0,), (0,)), ((), ())),
            preferred_element_type=jnp.float32,
        )
        for dy in range(3):
            small = jnp.zeros((gw, 256), jnp.float32)
            for g in range(PACK):
                piece = acc[gw * g : gw * g + gw, 256 * dy : 256 * dy + 256]
                small = jnp.where((lanes >= gw * g) & (lanes < gw * g + gw), piece, small)
            out_ref[3 * dy + dx, 0] = small


def conv_kernel(step, tall, width, sides, glob_ref, *refs):
    for ref in refs:
        if ref.shape[0] == tall:
            clear_edges(ref)
    for flag, side in ((1, sides[0]), (0, sides[1])):

        @pl.when(glob_ref[0] == flag)
        def _(side=side):
            step(width, side, glob_ref, refs)


def pack_kernel(gw, k_ref, out_ref):
    width = PACK * gw
    lane = lax.broadcasted_iota(jnp.int32, (gw, 256), 1)
    row = lax.broadcasted_iota(jnp.int32, (gw, 256), 0)
    spread = jnp.zeros((gw, 256), jnp.float32)
    for g in range(PACK):
        spread = jnp.where(lane == row + gw * g, 1.0, spread)
    spread = spread.astype(jnp.bfloat16)
    lane = lax.broadcasted_iota(jnp.int32, (width, 256), 1)
    row = lax.broadcasted_iota(jnp.int32, (width, 256), 0)
    inside = lane < 0
    for g in range(PACK):
        low, high = gw * g, gw * g + gw
        inside = inside | ((lane >= low) & (lane < high) & (row >= low) & (row < high))
    rest = jnp.zeros((256 - width, 256), jnp.float32)
    for dy in range(3):
        for dx in range(3):
            tap = k_ref[3 * dy + dx].astype(jnp.float32).reshape(width, gw).astype(jnp.bfloat16)
            wide = jnp.dot(tap, spread, preferred_element_type=jnp.float32)
            out_ref[0, 256 * dx : 256 * dx + 256, 256 * dy : 256 * dy + 256] = jnp.concatenate(
                [jnp.where(inside, wide, 0.0), rest], axis=0
            ).astype(jnp.bfloat16)


def pack_blocks(first, count, kernel, done=None):
    taps, groups, gw, _ = kernel.shape
    given = () if done is None else (done,)

    def body(k_ref, *refs):
        pack_kernel(gw, k_ref, refs[-1])

    return pl.pallas_call(
        body,
        grid=(count,),
        in_specs=[pl.BlockSpec((taps, PACK, gw, gw), lambda b: (0, b + first, 0, 0))]
        + [pl.BlockSpec(memory_space=pl.ANY)] * len(given),
        out_specs=pl.BlockSpec((1, 768, 768), lambda b: (b + first, 0, 0)),
        out_shape=jax.ShapeDtypeStruct((groups // PACK, 768, 768), jnp.bfloat16),
        input_output_aliases={1: 0} if given else {},
        compiler_params=params(),
        cost_estimate=cost(3),
        name="pack",
    )(kernel, *given)


def tile_specs(rows, width, chans, first=0):
    def spec(j):
        last = -(-chans // 128) - 1
        return pl.BlockSpec(
            (rows, 128), lambda b, s: (0, jnp.minimum((b + first) * width // 128 + j, last))
        )

    return [spec(j) for j in range(3)]


def conv_specs(rows):
    whole = lambda r: pl.BlockSpec((r, 2048), lambda b, s: (0, 0))
    mask = pl.BlockSpec((4, rows, 128), lambda b, s: (0, 0, 0))
    kern = pl.BlockSpec((1, 768, 768), lambda b, s: (b, 0, 0))
    return whole, mask, kern


def conv_scratch(rows, count):
    tall = rows + 2 * EDGE
    return [pltpu.VMEM((tall, 256), jnp.float32)] + [pltpu.VMEM((rows, 768), jnp.bfloat16)] * count


def conv_fwd(glob, h, par, masks, packed, width, sides):
    rows, chans = h.shape
    whole, mask, kern = conv_specs(rows)
    tiles = functools.partial(tile_specs, width=width, chans=chans)
    return pl.pallas_call(
        functools.partial(conv_kernel, fwd_step, rows + 2 * EDGE, width, sides),
        grid_spec=pltpu.PrefetchScalarGridSpec(
            num_scalar_prefetch=1,
            grid=(packed.shape[0],),
            in_specs=tiles(rows) + tiles(8) + [mask, kern],
            out_specs=[whole(rows), whole(8)],
            scratch_shapes=conv_scratch(rows, 1) + [pltpu.VMEM((rows + 2 * EDGE, 768), jnp.float32)],
        ),
        out_shape=[
            jax.ShapeDtypeStruct((rows, chans), jnp.float32),
            jax.ShapeDtypeStruct((8, chans), jnp.float32),
        ],
        compiler_params=params(),
        cost_estimate=cost(20),
        name="conv_fwd",
    )(glob, h, h, h, par, par, par, masks, packed)


def conv_dgrad(glob, grad, h, par, masks, packed, width, sides):
    rows, chans = h.shape
    whole, mask, kern = conv_specs(rows)
    tiles = functools.partial(tile_specs, width=width, chans=chans)
    return pl.pallas_call(
        functools.partial(conv_kernel, dgrad_step, rows + 2 * EDGE, width, sides),
        grid_spec=pltpu.PrefetchScalarGridSpec(
            num_scalar_prefetch=1,
            grid=(packed.shape[0],),
            in_specs=tiles(rows) + tiles(rows) + tiles(8) + [mask, kern],
            out_specs=[whole(rows), whole(8)],
            scratch_shapes=conv_scratch(rows, 1) + [pltpu.VMEM((rows + 2 * EDGE, 768), jnp.float32)],
        ),
        out_shape=[
            jax.ShapeDtypeStruct((rows, chans), jnp.float32),
            jax.ShapeDtypeStruct((8, chans), jnp.float32),
        ],
        compiler_params=params(),
        cost_estimate=cost(20),
        name="conv_dgrad",
    )(glob, grad, grad, grad, h, h, h, par, par, par, masks, packed)


def conv_wgrad(glob, grad, h, par, masks, first, count, blocks, width, sides, done=None):
    rows, chans = h.shape
    whole, mask, kern = conv_specs(rows)
    tiles = functools.partial(tile_specs, width=width, chans=chans, first=first)
    gw = width // PACK
    given = () if done is None else (done,)
    return pl.pallas_call(
        functools.partial(conv_kernel, wgrad_step, rows + 2 * EDGE, width, sides),
        grid_spec=pltpu.PrefetchScalarGridSpec(
            num_scalar_prefetch=1,
            grid=(count,),
            in_specs=tiles(rows) + tiles(rows) + tiles(8) + [mask]
            + [pl.BlockSpec(memory_space=pl.ANY)] * len(given),
            out_specs=pl.BlockSpec((9, 1, gw, 256), lambda b, s: (0, b + first, 0, 0)),
            scratch_shapes=conv_scratch(rows, 0) + conv_scratch(rows, 2),
        ),
        out_shape=jax.ShapeDtypeStruct((9, blocks, gw, 256), jnp.float32),
        input_output_aliases={11: 0} if given else {},
        compiler_params=params(),
        cost_estimate=cost(2 * count),
        name="conv_wgrad",
    )(
        jnp.concatenate([glob, jnp.full((1,), first, jnp.int32)]),
        grad,
        grad,
        grad,
        h,
        h,
        h,
        par,
        par,
        par,
        masks,
        *given,
    )


from jax.experimental.layout import Layout, with_layout_constraint
from jax.sharding import PartitionSpec as P

IMG_DEV = 4
SIDE = 14
SMALL_SIDE = 7
LOW_COLUMNS = 0
TAIL = (0, 2, 0, 2, 1, 0, 2, 0, 2, 1, 2, 0, 2)
WIDE = 2048
WIDE_PROTOS = 3072

norm_epsilon = 1e-05
length_epsilon = 1e-06
sharpening_divisor = 0.1
sharpness = 0.05
exact_mode = lax.Precision.HIGHEST


def plain(value):
    return with_layout_constraint(value, Layout(major_to_minor=tuple(range(value.ndim))))


def swap(value, axis, mask):
    pairs = [(source, source ^ mask) for source in range(lax.axis_size(axis))]
    if value.ndim < 3:
        return lax.ppermute(value, axis, pairs)
    return plain(lax.ppermute(plain(value), axis, pairs))


def tie(*values):
    return lax.optimization_barrier(values)


def smooth_gate(values):
    return values * jax.nn.sigmoid(values)


def smooth_slope(values):
    sigma_values = jax.nn.sigmoid(values)
    return sigma_values * (1.0 + values * (1.0 - sigma_values))


def exact_dot(left, right):
    return jnp.dot(left, right, precision=exact_mode, preferred_element_type=jnp.float32)


def bits_of(size):
    return [1 << bit for bit in range(size.bit_length() - 1)]


def stream_sum(value, work=(), inputs=()):
    made = []
    if work:
        value, inputs = tie(value, inputs)
    for k, mask in enumerate([0] + bits_of(lax.axis_size("img"))):
        other = swap(value, "img", mask) if mask else swap(value, "crop", 1)
        if k < len(work):
            made.append(work[k](*inputs, *made[-1:]))
            value, other, inputs, made[-1] = tie(value, other, inputs, made[-1])
        value = value + other
    return value, made


def quarters(blocks):
    cuts = [blocks * i // 4 for i in range(5)]
    return [(low, high - low) for low, high in zip(cuts, cuts[1:])]


def pick(value, index, axis):
    return lax.dynamic_index_in_dim(value, index, axis, keepdims=False)


def slab_rows(width, devices):
    return -(-(width // devices) // 8) * 8


def slab_offset(index, width, devices):
    share = width // devices
    return 2 * share * (index // 2) + (index % 2) * (2 * share - slab_rows(width, devices))


def slab_part(devices, width, height, place_ref, left_ref, right_ref):
    step = pl.program_id(0)
    half = devices // 4
    apart = jnp.where(step < half, 2 * step, 2 * (step - half) + 1)
    index = 2 * (apart ^ place_ref[1]) + place_ref[0]
    offset = slab_offset(index, width, devices)
    base = jnp.minimum(offset // 128, left_ref.shape[1] // 128 - 3) * 128
    wide = left_ref[:, pl.ds(pl.multiple_of(base, 128), 384)].astype(jnp.float32)
    shift = offset - base
    moved = pltpu.roll(wide, jnp.where(shift == 0, 0, 384 - shift), 1)[:, :height]
    return lax.dot_general(
        moved.astype(jnp.bfloat16),
        right_ref[...],
        (((0,), (0,)), ((), ())),
        preferred_element_type=jnp.float32,
    )


def far_kernel(devices, width, height, low, place_ref, left_ref, right_ref, *refs):
    acc = slab_part(devices, width, height, place_ref, left_ref, right_ref)
    if low:
        refs[0][0] = acc[:, :low]
    refs[-1][0] = acc[:, low:]


def near_kernel(devices, width, height, low, place_ref, left_ref, right_ref, *refs):
    held = refs[-1]
    keep_x, send_x, keep_y, send_y = refs[-5:-1]
    acc = slab_part(devices, width, height, place_ref, left_ref, right_ref)
    step = pl.program_id(0)
    if low:
        low_in, high_in, keep_low, send_low = refs[:4]
        total = acc[:, :low] + low_in[0]

        @pl.when(step < devices // 4)
        def _():
            keep_low[0] = total

        @pl.when(step >= devices // 4)
        def _():
            send_low[0] = total

    else:
        high_in = refs[0]
    held[...] = acc[:, low:] + high_in[0]
    rows = height // 8
    bits = (place_ref[2], place_ref[3])
    for half, keep, send in ((0, keep_x, send_x), (1, keep_y, send_y)):
        first, second = bits[half], bits[1 - half]
        for other, ref in ((0, keep), (1, send)):
            for last in range(2):
                block = 4 * half + 2 * (first ^ other) + (second ^ last)
                ref[last, 0] = held[pl.ds(pl.multiple_of(block * rows, rows), rows), :]


def slab_specs(devices, rows, height, low):
    sides = [pl.BlockSpec((rows, WIDE), lambda t, c: (0, 0))] * 2
    widths = [low, WIDE - low] if low else [WIDE]
    parts = [pl.BlockSpec((1, height, n), lambda t, c: (t, 0, 0)) for n in widths]
    shapes = [jax.ShapeDtypeStruct((devices // 2, height, n), jnp.float32) for n in widths]
    return sides, parts, shapes


def far_product(place, left, right, devices, low):
    rows, width = left.shape
    height = slab_rows(width, devices)
    sides, parts, shapes = slab_specs(devices, rows, height, low)
    return pl.pallas_call(
        functools.partial(far_kernel, devices, width, height, low),
        grid_spec=pltpu.PrefetchScalarGridSpec(
            num_scalar_prefetch=1, grid=(devices // 2,), in_specs=sides, out_specs=parts
        ),
        out_shape=shapes,
        compiler_params=pltpu.CompilerParams(vmem_limit_bytes=40 * 1024 * 1024),
        cost_estimate=cost(9),
        name="far_product",
    )(place, left, right)


def near_product(place, left, right, devices, low, arrived):
    rows, width = left.shape
    height = slab_rows(width, devices)
    sides, parts, _ = slab_specs(devices, rows, height, low)
    chips, half = devices // 2, devices // 4
    high = WIDE - low
    piece = pl.BlockSpec((2, 1, height // 8, high), lambda t, c: (0, t, 0, 0))
    out_specs = [piece] * 4
    out_shape = [jax.ShapeDtypeStruct((2, chips, height // 8, high), jnp.float32)] * 4
    if low:
        out_specs = [
            pl.BlockSpec((1, height, low), lambda t, c: (jnp.minimum(t, half - 1), 0, 0)),
            pl.BlockSpec((1, height, low), lambda t, c: (jnp.maximum(t - half, 0), 0, 0)),
        ] + out_specs
        out_shape = [jax.ShapeDtypeStruct((half, height, low), jnp.float32)] * 2 + out_shape
    return pl.pallas_call(
        functools.partial(near_kernel, devices, width, height, low),
        grid_spec=pltpu.PrefetchScalarGridSpec(
            num_scalar_prefetch=1,
            grid=(chips,),
            in_specs=sides + parts,
            out_specs=out_specs,
            scratch_shapes=[pltpu.VMEM((height, high), jnp.float32)],
        ),
        out_shape=out_shape,
        compiler_params=pltpu.CompilerParams(vmem_limit_bytes=48 * 1024 * 1024),
        cost_estimate=cost(13),
        name="near_product",
    )(place, left, right, *arrived)


UNIT_ROWS = 704


def unit_start(index, share, unit, gw, rows):
    return jnp.minimum((share * index // unit) * gw, rows - UNIT_ROWS)


def unit_part(devices, size, gw, place_ref, units_ref):
    step = pl.program_id(0)
    half = devices // 4
    apart = jnp.where(step < half, 2 * step, 2 * (step - half) + 1)
    index = 2 * (apart ^ place_ref[1]) + place_ref[0]
    start = unit_start(index, size // devices, gw * gw * PACK, gw, units_ref.shape[0])
    return pl.multiple_of(start, 8)


def far_units_kernel(devices, size, gw, place_ref, units_ref, out_ref):
    start = unit_part(devices, size, gw, place_ref, units_ref)
    out_ref[0] = units_ref[pl.ds(start, UNIT_ROWS), :]


def near_units_kernel(devices, size, gw, place_ref, units_ref, in_ref, *refs):
    keep_x, send_x, keep_y, send_y = refs
    start = unit_part(devices, size, gw, place_ref, units_ref)
    rows = UNIT_ROWS // 8
    bits = (place_ref[2], place_ref[3])
    for half, keep, send in ((0, keep_x, send_x), (1, keep_y, send_y)):
        first, second = bits[half], bits[1 - half]
        for other, ref in ((0, keep), (1, send)):
            for last in range(2):
                block = 4 * half + 2 * (first ^ other) + (second ^ last)
                skip = pl.multiple_of(block * rows, 8)
                ref[last, 0] = (
                    units_ref[pl.ds(pl.multiple_of(start + skip, 8), rows), :]
                    + in_ref[0, pl.ds(skip, rows), :]
                )


def unit_call(place, units, devices, size, gw, arrived=None):
    rows = units.shape[0]
    chips = devices // 2
    part = pl.BlockSpec((1, UNIT_ROWS, 256), lambda t, c: (t, 0, 0))
    if arrived is None:
        body, extra = far_units_kernel, ()
        out_specs, out_shape = part, jax.ShapeDtypeStruct((chips, UNIT_ROWS, 256), jnp.float32)
    else:
        body, extra = near_units_kernel, (arrived,)
        piece = (2, chips, UNIT_ROWS // 8, 256)
        out_specs = [pl.BlockSpec((2, 1) + piece[2:], lambda t, c: (0, t, 0, 0))] * 4
        out_shape = [jax.ShapeDtypeStruct(piece, jnp.float32)] * 4
    return pl.pallas_call(
        functools.partial(body, devices, size, gw),
        grid_spec=pltpu.PrefetchScalarGridSpec(
            num_scalar_prefetch=1,
            grid=(chips,),
            in_specs=[pl.BlockSpec((rows, 256), lambda t, c: (0, 0))] + [part] * len(extra),
            out_specs=out_specs,
        ),
        out_shape=out_shape,
        compiler_params=pltpu.CompilerParams(vmem_limit_bytes=32 * 1024 * 1024),
        cost_estimate=cost(3),
        name="units",
    )(place, units, *extra)


def share_kernel(left_ref, right_ref, out_ref):
    out_ref[...] = lax.dot_general(
        left_ref[...].astype(jnp.bfloat16),
        right_ref[...].astype(jnp.bfloat16),
        (((0,), (0,)), ((), ())),
        preferred_element_type=jnp.float32,
    )


def share_product(left, right):
    return pl.pallas_call(
        share_kernel,
        out_shape=jax.ShapeDtypeStruct((left.shape[1], right.shape[1]), jnp.float32),
        compiler_params=pltpu.CompilerParams(vmem_limit_bytes=32 * 1024 * 1024),
        cost_estimate=cost(3),
        name="share_product",
    )(left, right)


def crop_bits():
    crop = lax.axis_index("crop")
    return (crop & 1, crop >> 1)


def crop_halves(value):
    lead, rows, cols = value.shape
    whole = value.reshape(lead, 2, 2, 2, rows // 8, cols)
    return [whole[:, 0], whole[:, 1]]


CROP_ORDER = ((0, 1), (1, 0))


def crop_send(parts, step):
    bits = crop_bits()
    return [
        swap(pick(part, 1 - bits[order[step]], 1), "crop", 1 << order[step])
        for part, order in zip(parts, CROP_ORDER)
    ]


def crop_add(parts, arrived, step):
    bits = crop_bits()
    return [
        pick(part, bits[order[step]], 1) + other
        for part, other, order in zip(parts, arrived, CROP_ORDER)
    ]


def crop_fetch(parts, step):
    return [swap(part, "crop", 1 << order[1 - step]) for part, order in zip(parts, CROP_ORDER)]


def crop_join(parts, arrived, step):
    bits = crop_bits()
    joined = []
    for part, other, order in zip(parts, arrived, CROP_ORDER):
        upper = bits[order[1 - step]] == 1
        joined.append(
            jnp.stack([jnp.where(upper, other, part), jnp.where(upper, part, other)], axis=1)
        )
    return joined


def crop_whole(parts):
    both = jnp.stack(parts, axis=1)
    return both.reshape(both.shape[0], -1, both.shape[-1])


def chip_swap(value, step):
    return swap(value, "img", 2 << step)


class LowChain:
    def __init__(self, keep, send):
        self.keep, self.away = keep, [send]
        self.chips = keep.shape[0].bit_length()
        self.steps, self.step = self.chips + 4, 0

    def send(self):
        if self.step < self.chips:
            return [chip_swap(v, self.step) for v in self.away]
        if self.step < self.chips + 2:
            return crop_send(self.keep, self.step - self.chips)
        return crop_fetch(self.keep, self.step - self.chips - 2)

    def take(self, arrived):
        step, chips = self.step, self.chips
        if step < chips:
            total = self.keep + arrived[0]
            half = total.shape[0] // 2
            self.keep, self.away = total[:half], [total[half:]]
            if step == chips - 1:
                self.keep, self.away = crop_halves(total), []
        elif step < chips + 2:
            self.keep = crop_add(self.keep, arrived, step - chips)
        else:
            self.keep = crop_join(self.keep, arrived, step - chips - 2)
        self.step += 1

    def result(self):
        return crop_whole(self.keep)[0]


class HighChain:
    def __init__(self, keep_x, send_x, keep_y, send_y):
        self.keep, self.away = [keep_x, keep_y], [send_x, send_y]
        self.chips = keep_x.shape[1].bit_length() - 1
        self.steps, self.step = self.chips + 4, 0

    def send(self):
        step = self.step
        if step < 2:
            return [swap(v, "crop", 1 << order[step]) for v, order in zip(self.away, CROP_ORDER)]
        if step < self.chips + 2:
            return [chip_swap(v, step - 2) for v in self.away]
        return crop_fetch(self.keep, step - self.chips - 2)

    def take(self, arrived):
        step, chips = self.step, self.chips
        if step < chips + 2:
            total = [keep + other for keep, other in zip(self.keep, arrived)]
            if step == 0:
                self.keep, self.away = [v[0] for v in total], [v[1] for v in total]
            else:
                if step == 1:
                    total = [jnp.concatenate(total, axis=1)]
                half = total[0].shape[0] // 2
                self.keep, self.away = [total[0][:half]], [total[0][half:]]
            if step == chips + 1:
                rows = total[0].shape[1] // 2
                self.keep, self.away = [total[0][:, :rows], total[0][:, rows:]], []
        else:
            self.keep = crop_join(self.keep, arrived, step - chips - 2)
        self.step += 1

    def result(self):
        return crop_whole(self.keep)[0]


class CropSum:
    steps = 4

    def __init__(self, value):
        self.away = []
        self.keep = crop_halves(value[None])
        self.step = 0

    def send(self):
        if self.step < 2:
            return crop_send(self.keep, self.step)
        return crop_fetch(self.keep, self.step - 2)

    def take(self, arrived):
        if self.step < 2:
            self.keep = crop_add(self.keep, arrived, self.step)
        else:
            self.keep = crop_join(self.keep, arrived, self.step - 2)
        self.step += 1

    def result(self):
        return crop_whole(self.keep)[0]


class Flow:
    def __init__(self):
        self.sent = {}

    def begin(self, chain):
        self.sent[id(chain)] = chain.send()

    def advance(self, chain, beside):
        arrived, beside = tie(self.sent[id(chain)], beside)
        chain.take(arrived)
        (chain.keep, chain.away), beside = tie((chain.keep, chain.away), beside)
        if chain.step < chain.steps:
            self.begin(chain)
        return beside


def shards(
    pixels,
    counts,
    slot_order,
    w_in,
    kernel,
    w_red,
    b_red,
    w_exp,
    b_exp,
    w_out,
    gain_one,
    shift_one,
    gain_two,
    shift_two,
    gain_three,
    shift_three,
    protos,
):
    row_count = pixels.shape[2]
    width = pixels.shape[3]
    proto_count = protos.shape[1]
    squeeze = w_red.shape[1]
    seg_count = row_count // (SMALL_SIDE * SMALL_SIDE)
    slot_total = slot_order.shape[1]
    devices = lax.axis_size("img")
    img_index = lax.axis_index("img")
    crop_index = lax.axis_index("crop")
    core = img_index % 2
    fast = width % devices == 0 and (2 * width // devices) % 8 == 0
    is_global = crop_index < 2
    glob = is_global.astype(jnp.int32).reshape(1)
    stream_rows = 2.0 * devices * row_count
    couple_number = 2.0 * devices * (IMG_DEV + slot_total)
    inputs = pixels.reshape(row_count, width)
    row_ids = jnp.arange(row_count, dtype=jnp.int32)
    side = jnp.where(is_global, SIDE, SMALL_SIDE)
    seg_of_row = row_ids // (side * side)
    across = row_ids % side
    down = (row_ids // side) % side
    masks = jnp.stack([across > 0, across < side - 1, down > 0, down < side - 1])
    masks = jnp.broadcast_to(masks.astype(jnp.float32)[:, :, None], (4, row_count, 128))
    member = (seg_of_row[None, :] == jnp.arange(seg_count, dtype=jnp.int32)[:, None]).astype(
        jnp.float32
    )
    member_rows = member.T
    crop_pixels = jnp.where(is_global, float(SIDE * SIDE), float(SMALL_SIDE * SMALL_SIDE))
    block_width = PACK * kernel.shape[2]
    block_count = kernel.shape[1] // PACK
    sides = (SIDE, SMALL_SIDE)

    def norm_rows(local_sums, work=(), inputs=()):
        sums, made = stream_sum(local_sums, work, inputs)
        average = sums[0] / stream_rows
        inv = lax.rsqrt(sums[1] / stream_rows - average * average + norm_epsilon)
        return average, inv, made

    def back_rows(local_sums, gain, inv, work=(), inputs=()):
        sums, made = stream_sum(local_sums, work, inputs)
        return sums, gain * inv, sums[0] / stream_rows, sums[1] / stream_rows, made

    hidden_one = jnp.dot(inputs, w_in, preferred_element_type=jnp.float32)
    sums = jnp.stack([jnp.sum(hidden_one, axis=0), jnp.sum(hidden_one * hidden_one, axis=0)])
    mean_one, inv_one, packed = norm_rows(
        sums,
        [functools.partial(pack_blocks, low, count) for low, count in quarters(block_count)],
        (kernel,),
    )
    packed = packed[-1]
    zero_row = jnp.zeros((width,), jnp.float32)
    scale_one = gain_one * inv_one
    par = jnp.stack(
        [scale_one, shift_one - mean_one * scale_one, inv_one, -mean_one * inv_one] + [zero_row] * 4
    )
    hidden_two, sums = conv_fwd(glob, hidden_one, par, masks, packed, block_width, sides)
    mean_two, inv_two, _ = norm_rows(sums[:2])
    centred_two = (hidden_two - mean_two) * inv_two
    pre_two = centred_two * gain_two + shift_two
    act_two = smooth_gate(pre_two)
    red_float = w_red.astype(jnp.float32)
    exp_float = w_exp.astype(jnp.float32)
    pooled = exact_dot(member, act_two) / crop_pixels
    reduce_pre = exact_dot(pooled, red_float) + b_red
    reduced = smooth_gate(reduce_pre)
    gate_values = jax.nn.sigmoid(exact_dot(reduced, exp_float) + b_exp)
    gate_rows = exact_dot(member_rows, gate_values)
    excited = (act_two * gate_rows).astype(jnp.bfloat16)
    hidden_three = jnp.dot(excited, w_out, preferred_element_type=jnp.float32)
    sums = jnp.stack([jnp.sum(hidden_three, axis=0), jnp.sum(hidden_three * hidden_three, axis=0)])
    mean_three, inv_three, _ = norm_rows(sums)
    centred_three = (hidden_three - mean_three) * inv_three
    summed_in = inputs.astype(jnp.float32) + centred_three * gain_three + shift_three
    output = smooth_gate(summed_in)
    pooled_out = exact_dot(member, output) / crop_pixels
    length_inv = lax.rsqrt(jnp.sum(pooled_out * pooled_out, axis=1, keepdims=True) + length_epsilon)
    unit_wide = pooled_out * length_inv
    unit_rows = unit_wide.astype(jnp.bfloat16)
    match_matrix = jnp.dot(unit_rows, protos, preferred_element_type=jnp.float32)

    every = match_matrix[:IMG_DEV]
    for mask in bits_of(devices):
        every = jnp.concatenate([every, swap(every, "img", mask)], axis=0)
    plan_rows = jnp.exp(every / sharpness)
    for sweep_index in range(3):
        plan_rows = plan_rows / jnp.sum(plan_rows, axis=0, keepdims=True)
        plan_rows = plan_rows / jnp.sum(plan_rows, axis=1, keepdims=True)
    codes = plan_rows[:IMG_DEV]
    partner = lax.ppermute(codes, "crop", [(0, 1), (1, 0)])
    both_codes = lax.ppermute(codes, "crop", [(0, 2), (1, 3)]) + lax.ppermute(
        codes, "crop", [(0, 3), (1, 2)]
    )
    wide_target = jnp.concatenate(
        [partner, jnp.zeros((seg_count - IMG_DEV, proto_count), jnp.float32)], axis=0
    )
    ends = [jnp.sum(counts[0, : i + 1]) for i in range(IMG_DEV)]
    first_slot = jnp.maximum(crop_index - 2, 0) * seg_count
    order_here = lax.dynamic_slice_in_dim(slot_order[0], first_slot, seg_count)
    owner = sum((order_here >= end).astype(jnp.int32) for end in ends)
    narrow_target = jnp.zeros((seg_count, proto_count), jnp.float32)
    for i in range(IMG_DEV):
        narrow_target = jnp.where(owner[:, None] == i, both_codes[i : i + 1], narrow_target)
    target = jnp.where(is_global, wide_target, narrow_target)
    sharpened = match_matrix / sharpening_divisor
    shifted = sharpened - jnp.max(sharpened, axis=1, keepdims=True)
    log_probs = shifted - jnp.log(jnp.sum(jnp.exp(shifted), axis=1, keepdims=True))
    loss_here = -jnp.sum(target * log_probs) / couple_number
    scores_wide = (jnp.exp(log_probs) * jnp.sum(target, axis=1, keepdims=True) - target) / (
        sharpening_divisor * couple_number
    )
    grad_scores = scores_wide.astype(jnp.bfloat16)

    grad_unit = jnp.einsum("sk,wk->sw", grad_scores, protos, preferred_element_type=jnp.float32)
    inner_term = jnp.sum(pooled_out * grad_unit, axis=1, keepdims=True)
    grad_pooled_out = (
        length_inv * grad_unit - pooled_out * length_inv * length_inv * length_inv * inner_term
    )
    grad_output = exact_dot(member_rows, grad_pooled_out / crop_pixels)
    grad_summed = grad_output * smooth_slope(summed_in)
    sums_three, scale_three, first, second, _ = back_rows(
        jnp.stack([jnp.sum(grad_summed, axis=0), jnp.sum(grad_summed * centred_three, axis=0)]),
        gain_three,
        inv_three,
    )
    grad_three_low = (scale_three * (grad_summed - first - centred_three * second)).astype(
        jnp.bfloat16
    )
    if fast:
        share = width // devices
        height = slab_rows(width, devices)
        chip = img_index // 2
        near = jnp.stack([core, chip, crop_index & 1, crop_index >> 1]).astype(jnp.int32)
        far = jnp.stack([1 - core, chip, crop_index & 1, crop_index >> 1]).astype(jnp.int32)

        def kept(value):
            skip = core * (value.shape[0] - share)
            return lax.dynamic_slice_in_dim(value, skip, share, axis=0)

        seen_scores = lax.all_gather(
            jnp.concatenate(
                [
                    unit_wide,
                    jnp.zeros((seg_count, WIDE - width), jnp.float32),
                    scores_wide,
                    jnp.zeros((seg_count, WIDE_PROTOS - proto_count), jnp.float32),
                ],
                axis=1,
            ),
            "img",
            tiled=True,
        )

    grad_excited = jnp.einsum(
        "rv,wv->rw", grad_three_low, w_out, preferred_element_type=jnp.float32
    )
    flow = Flow()
    if fast:
        grad_excited, seen_scores = tie(grad_excited, seen_scores)
        protos_sum = CropSum(
            share_product(
                lax.dynamic_slice_in_dim(seen_scores, img_index * share, height, axis=1),
                seen_scores[:, WIDE:],
            )
        )
        (protos_sum.keep, grad_excited) = tie(protos_sum.keep, grad_excited)
        flow.begin(protos_sum)
    grad_gate = exact_dot(member, grad_excited * act_two)
    grad_gate_pre = grad_gate * gate_values * (1.0 - gate_values)
    grad_reduce_pre = exact_dot(grad_gate_pre, exp_float.T) * smooth_slope(reduce_pre)
    grad_pooled = exact_dot(grad_reduce_pre, red_float.T)
    grad_act_two = grad_excited * gate_rows + exact_dot(member_rows, grad_pooled / crop_pixels)
    grad_pre_two = grad_act_two * smooth_slope(pre_two)
    bias_row = jnp.concatenate(
        [
            jnp.sum(grad_reduce_pre, axis=0),
            loss_here.reshape(1),
            jnp.zeros((width - squeeze - 1,), jnp.float32),
        ]
    )
    local_two = jnp.stack(
        [
            jnp.sum(grad_pre_two, axis=0),
            jnp.sum(grad_pre_two * centred_two, axis=0),
            jnp.sum(grad_gate_pre, axis=0),
            bias_row,
        ]
    )
    work = []
    if fast:
        seen_gates = lax.all_gather(
            jnp.concatenate([pooled, reduced, grad_reduce_pre, grad_gate_pre], axis=1),
            "img",
            tiled=True,
        )

        def out_far(left, right):
            return far_product(far, left, right, devices, 0)

        def proto_step(left, right, arrived):
            return flow.advance(protos_sum, arrived)

        work = [out_far, proto_step]
    sums_two, scale_two, first, second, made = back_rows(
        local_two, gain_two, inv_two, work, (excited, grad_three_low)
    )
    if fast:
        arrived = [swap(v, "img", 1) for v in made[-1]]
    grad_two_low = (scale_two * (grad_pre_two - first - centred_two * second)).astype(jnp.bfloat16)
    if fast:
        grad_two_low, arrived = tie(grad_two_low, arrived)
        arrived = flow.advance(protos_sum, arrived)
        outs = HighChain(*near_product(near, excited, grad_three_low, devices, 0, arrived))
        outs.keep, outs.away, grad_two_low = tie(outs.keep, outs.away, grad_two_low)
        flow.begin(outs)
    grad_pre_one, sums = conv_dgrad(
        glob, grad_two_low, hidden_one, par, masks, packed, block_width, sides
    )

    def some_wgrad(low, count, grad, done=None):
        return conv_wgrad(
            glob, grad, hidden_one, par, masks, low, count, block_count, block_width, sides, done
        )

    cut = block_count // 2
    steps = [
        functools.partial(some_wgrad, 0, cut),
        functools.partial(some_wgrad, cut, block_count - cut),
    ]
    early = []
    if fast:
        grad_two_low, grad_pre_one, sums = tie(grad_two_low, grad_pre_one, sums)
        units = steps[0](grad_two_low)
        units = flow.advance(outs, units)
        units, sums = tie(units, sums)

        def my_columns(value):
            count = value.shape[1] // devices
            return lax.dynamic_slice_in_dim(value, img_index * count, count, axis=1)

        def shares_of(seen):
            seen = flow.advance(protos_sum, seen)
            return (
                exact_dot(
                    my_columns(seen[:, :width]).T, seen[:, width + squeeze : width + 2 * squeeze]
                ),
                exact_dot(my_columns(seen[:, width : width + squeeze]).T, seen[:, width + 2 * squeeze :]),
            )

        early = [shares_of]
    sums_one, scale_one, first, second, made = back_rows(
        sums[:2], gain_one, inv_one, early, (seen_gates,) if fast else ()
    )
    centred_one = (hidden_one - mean_one) * inv_one
    grad_one_low = (scale_one * (grad_pre_one - first - centred_one * second)).astype(jnp.bfloat16)
    if fast:
        share_red, share_exp = made[-1]
        share_red, share_exp = lax.psum((share_red, share_exp), "crop")
        grad_one_low = flow.advance(outs, grad_one_low)
        arrived = far_product(far, inputs, grad_one_low, devices, LOW_COLUMNS)
        arrived = [swap(v, "img", 1) for v in arrived]
        arrived = flow.advance(protos_sum, arrived)
        arrived = flow.advance(outs, arrived)
        parts = near_product(near, inputs, grad_one_low, devices, LOW_COLUMNS, arrived)
        ins = HighChain(*parts)
        units, grad_two_low, grad_one_low, ins.keep, ins.away = tie(
            units, grad_two_low, grad_one_low, ins.keep, ins.away
        )
        flow.begin(ins)
        units = steps[1](grad_two_low, units)
        units = flow.advance(outs, units)
        gw = kernel.shape[2]
        unit_size = gw * gw * PACK
        units = units.reshape(-1, 256)
        swapped = unit_call(far, units, devices, kernel.size, gw)
        swapped, units, grad_one_low = tie(swapped, units, grad_one_low)
        swapped, units, grad_one_low = flow.advance(ins, (swapped, units, grad_one_low))
        swapped = swap(swapped, "img", 1)
        grad_inputs = (
            jnp.einsum("rv,wv->rw", grad_one_low, w_in, preferred_element_type=jnp.float32)
            + grad_summed
        )
        swapped, grad_inputs = tie(swapped, grad_inputs)
        gks = HighChain(*unit_call(near, units, devices, kernel.size, gw, swapped))
        flow.begin(gks)
        chains = [ins, outs, gks]
        last = None
        for chain in (chains[index] for index in TAIL):
            arrived = flow.sent[id(chain)]
            if last is not None:
                arrived, _ = tie(arrived, (last.keep, last.away))
            chain.take(arrived)
            if chain.step < chain.steps:
                flow.begin(chain)
            last = chain
    else:
        made = None
        for step in steps:
            made = step(grad_two_low, made)
        small_kernel = made
        grad_inputs = (
            jnp.einsum("rv,wv->rw", grad_one_low, w_in, preferred_element_type=jnp.float32)
            + grad_summed
        )

    last = jnp.concatenate([sums_one, sums_two, sums_three], axis=0)
    last = last + swap(last, "crop", 2)
    tail = (
        last[5, :squeeze],
        last[4],
        last[1],
        last[0],
        last[3],
        last[2],
        last[7],
        last[6],
    )
    loss_total = last[5, squeeze]

    if fast:
        flat_in = kept(ins.result()[:, :width]).reshape(-1)
        flat_out = kept(outs.result()[:, :width]).reshape(-1)
        flat_protos = protos_sum.result()[:share, :proto_count].reshape(-1)
        flat_red = share_red.reshape(-1)
        flat_exp = share_exp.reshape(-1)
        total = kernel.size // devices
        first_unit = total * img_index // unit_size
        start = unit_start(img_index, total, unit_size, gw, units.size // 256)
        span = -(-total // unit_size) + 1
        mine = jnp.pad(gks.result(), ((0, gw), (0, 0)))
        mine = lax.dynamic_slice_in_dim(mine, first_unit * gw - start, span * gw, axis=0)
        mine = mine[:, : PACK * gw].reshape(span, gw, PACK, gw).transpose(0, 2, 1, 3).reshape(-1)
        flat_kernel = lax.dynamic_slice_in_dim(mine, total * img_index - unit_size * first_unit, total)
        shares = (flat_in, flat_kernel, flat_red, flat_exp, flat_out, flat_protos)
    else:
        gw = kernel.shape[2]
        grads = (
            jnp.einsum("rw,rv->wv", inputs, grad_one_low, preferred_element_type=jnp.float32),
            small_kernel[..., : PACK * gw]
            .reshape(9, block_count, gw, PACK, gw)
            .transpose(0, 1, 3, 2, 4),
            exact_dot(pooled.T, grad_reduce_pre),
            exact_dot(reduced.T, grad_gate_pre),
            jnp.einsum("rw,rv->wv", excited, grad_three_low, preferred_element_type=jnp.float32),
            jnp.einsum("sw,sk->wk", unit_rows, grad_scores, preferred_element_type=jnp.float32),
        )
        shares = tuple(
            lax.psum(
                lax.psum_scatter(grad.reshape(-1), "img", scatter_dimension=0, tiled=True), "crop"
            )
            for grad in grads
        )
    return (
        loss_total,
        output.astype(jnp.bfloat16).reshape(pixels.shape),
        grad_inputs.reshape(pixels.shape),
        *shares,
        *tail,
    )


def solution(mesh):
    return jax.shard_map(
        shards,
        mesh=mesh,
        in_specs=(P("crop", "img", None, None), P("img", None), P("img", None)) + (P(),) * 14,
        out_specs=(P(), P("crop", "img", None, None), P("crop", "img", None, None))
        + (P("img"),) * 6
        + (P(),) * 8,
        check_vma=False,
    )
```

```python
import functools
import jax
import jax.numpy as jnp
from jax import lax
from jax.experimental import pallas as pl
from jax.experimental.pallas import tpu as pltpu

VMEM_LIMIT = 56 * 1024 * 1024
PACK = 4
EDGE = 16
CHUNK = 112


def cost(micros):
    return pl.CostEstimate(flops=micros * 1000000, bytes_accessed=micros * 1000, transcendentals=0)


def params():
    return pltpu.CompilerParams(vmem_limit_bytes=VMEM_LIMIT)


def lane_of(rows):
    return lax.broadcasted_iota(jnp.int32, (rows, 128), 1)


def take(refs, start, rows, skip, width):
    a, b, c = [ref[start : start + rows, :].astype(jnp.float32) for ref in refs]
    back = lax.rem(128 - skip, 128)
    a, b, c = [pltpu.roll(v, back, 1) for v in (a, b, c)]
    lane = lane_of(rows)
    near = lane < 128 - skip
    return jnp.where(near, a, b), jnp.where(lane < width - 128, jnp.where(near, b, c), 0.0)


def put(ref, start, rows, base, skip, first, second):
    first, second = pltpu.roll(first, skip, 1), pltpu.roll(second, skip, 1)
    lane = lane_of(rows)
    inside = lane >= skip
    last = jnp.minimum(base + 2, ref.shape[1] // 128 - 1)

    def at(tile):
        return (slice(start, start + rows), pl.ds(pl.multiple_of(tile * 128, 128), 128))

    ref[at(last)] = second
    ref[at(base + 1)] = jnp.where(inside, second, first)
    ref[at(base)] = jnp.where(inside, first, ref[at(base)])


def place_of(block, width):
    start = block * width
    base = start // 128
    return base, start - base * 128


def clear_edges(ref):
    @pl.when(pl.program_id(0) == 0)
    def _():
        ref[0:EDGE, :] = jnp.zeros((EDGE, ref.shape[1]), ref.dtype)
        ref[ref.shape[0] - EDGE :, :] = jnp.zeros((EDGE, ref.shape[1]), ref.dtype)


def chunks(rows):
    return range(0, rows, CHUNK)


def fill_act(h_refs, p_refs, skip, width, starts, act):
    scale = take(p_refs, 0, 8, skip, width)
    for r in starts:
        for tile, h in enumerate(take(h_refs, r, CHUNK, skip, width)):
            pre = h * scale[tile][0:1] + scale[tile][1:2]
            value = pre * jax.nn.sigmoid(pre)
            act[EDGE + r : EDGE + r + CHUNK, 128 * tile : 128 * tile + 128] = value.astype(
                jnp.bfloat16
            ).astype(jnp.float32)


def fill_grad(g_refs, skip, width, starts, grad):
    for r in starts:
        for tile, g in enumerate(take(g_refs, r, CHUNK, skip, width)):
            grad[EDGE + r : EDGE + r + CHUNK, 128 * tile : 128 * tile + 128] = g


def stack(source, mask_ref, low, high, step, starts, dest):
    for r in starts:
        for tile in range(2):
            cols = slice(128 * tile, 128 * tile + 128)
            here = slice(r, r + CHUNK)
            before = source[EDGE + r - step : EDGE + r - step + CHUNK, cols] * mask_ref[low, here, :]
            after = source[EDGE + r + step : EDGE + r + step + CHUNK, cols] * mask_ref[high, here, :]
            middle = source[EDGE + r : EDGE + r + CHUNK, cols]
            dest[here, 128 * tile : 128 * tile + 128] = before.astype(jnp.bfloat16)
            dest[here, 256 + 128 * tile : 384 + 128 * tile] = middle.astype(jnp.bfloat16)
            dest[here, 512 + 128 * tile : 640 + 128 * tile] = after.astype(jnp.bfloat16)


def fwd_step(width, side, glob_ref, refs):
    h_refs, p_refs, (mask_ref, k_ref, out_ref, st_ref, act, cols, wide) = refs[:3], refs[3:6], refs[6:]
    rows = h_refs[0].shape[0]
    base, skip = place_of(pl.program_id(0), width)
    starts = list(chunks(rows))
    fill_act(h_refs, p_refs, skip, width, starts[:1], act)
    for i, r in enumerate(starts):
        fill_act(h_refs, p_refs, skip, width, starts[i + 1 : i + 2], act)
        stack(act, mask_ref, 0, 1, 1, [r], cols)
        wide[EDGE + r : EDGE + r + CHUNK, :] = jnp.dot(
            cols[r : r + CHUNK, :], k_ref[0], preferred_element_type=jnp.float32
        )
    sums = [jnp.zeros((8, 128), jnp.float32)] * 4
    for r in starts:
        here = slice(r, r + CHUNK)
        tiles = []
        for tile in range(2):
            lo = 128 * tile
            total = (
                wide[EDGE + r : EDGE + r + CHUNK, 256 + lo : 384 + lo]
                + wide[EDGE + r - side : EDGE + r - side + CHUNK, lo : 128 + lo] * mask_ref[2, here, :]
                + wide[EDGE + r + side : EDGE + r + side + CHUNK, 512 + lo : 640 + lo] * mask_ref[3, here, :]
            )
            tiles.append(total)
            sums[tile] += jnp.sum(total.reshape(-1, 8, 128), axis=0)
            sums[2 + tile] += jnp.sum((total * total).reshape(-1, 8, 128), axis=0)
        put(out_ref, r, CHUNK, base, skip, *tiles)
    put_sums(st_ref, base, skip, sums)


def put_sums(st_ref, base, skip, sums):
    line = lax.broadcasted_iota(jnp.int32, (8, 128), 0)
    tiles = [
        jnp.where(
            line == 0,
            jnp.sum(sums[tile], axis=0, keepdims=True),
            jnp.sum(sums[2 + tile], axis=0, keepdims=True),
        )
        for tile in range(2)
    ]
    put(st_ref, 0, 8, base, skip, *tiles)


def dgrad_step(width, side, glob_ref, refs):
    g_refs, h_refs, p_refs = refs[:3], refs[3:6], refs[6:9]
    mask_ref, k_ref, out_ref, st_ref, grad, lines, wide = refs[9:]
    rows = h_refs[0].shape[0]
    base, skip = place_of(pl.program_id(0), width)
    starts = list(chunks(rows))
    fill_grad(g_refs, skip, width, starts[:1], grad)
    for i, r in enumerate(starts):
        fill_grad(g_refs, skip, width, starts[i + 1 : i + 2], grad)
        stack_lines(grad, mask_ref, side, [r], lines)
    wide[EDGE : EDGE + rows, :] = lax.dot_general(
        lines[...], k_ref[0], (((1,), (1,)), ((), ())), preferred_element_type=jnp.float32
    )
    par = take(p_refs, 0, 8, skip, width)
    sums = [jnp.zeros((8, 128), jnp.float32)] * 4
    for r in starts:
        here = slice(r, r + CHUNK)
        h_tiles = take(h_refs, r, CHUNK, skip, width)
        tiles = []
        for tile in range(2):
            lo = 128 * tile
            total = (
                wide[EDGE + r : EDGE + r + CHUNK, 256 + lo : 384 + lo]
                + wide[EDGE + r + 1 : EDGE + r + 1 + CHUNK, lo : 128 + lo] * mask_ref[1, here, :]
                + wide[EDGE + r - 1 : EDGE + r - 1 + CHUNK, 512 + lo : 640 + lo] * mask_ref[0, here, :]
            )
            p = par[tile]
            pre = h_tiles[tile] * p[0:1] + p[1:2]
            sig = jax.nn.sigmoid(pre)
            ga = total * (sig * (1.0 + pre * (1.0 - sig)))
            xhat = h_tiles[tile] * p[2:3] + p[3:4]
            tiles.append(ga)
            sums[tile] += jnp.sum(ga.reshape(-1, 8, 128), axis=0)
            sums[2 + tile] += jnp.sum((ga * xhat).reshape(-1, 8, 128), axis=0)
        put(out_ref, r, CHUNK, base, skip, *tiles)
    put_sums(st_ref, base, skip, sums)


def stack_lines(grad, mask_ref, side, starts, dest):
    for r in starts:
        for tile in range(2):
            cols = slice(128 * tile, 128 * tile + 128)
            here = slice(r, r + CHUNK)
            below = grad[EDGE + r + side : EDGE + r + side + CHUNK, cols] * mask_ref[3, here, :]
            above = grad[EDGE + r - side : EDGE + r - side + CHUNK, cols] * mask_ref[2, here, :]
            middle = grad[EDGE + r : EDGE + r + CHUNK, cols]
            dest[here, 128 * tile : 128 * tile + 128] = below.astype(jnp.bfloat16)
            dest[here, 256 + 128 * tile : 384 + 128 * tile] = middle.astype(jnp.bfloat16)
            dest[here, 512 + 128 * tile : 640 + 128 * tile] = above.astype(jnp.bfloat16)


def wgrad_step(width, side, glob_ref, refs):
    g_refs, h_refs, p_refs = refs[:3], refs[3:6], refs[6:9]
    mask_ref, out_ref, source, grad, cols, lines = refs[9], *refs[-5:]
    rows = h_refs[0].shape[0]
    block = pl.program_id(0) + glob_ref[1]
    _, skip = place_of(block, width)
    starts = list(chunks(rows))
    fill_act(h_refs, p_refs, skip, width, starts, source)
    fill_grad(g_refs, skip, width, starts, grad)
    stack(source, mask_ref, 0, 1, 1, starts, cols)
    stack_lines(grad, mask_ref, side, starts, lines)
    gw = width // PACK
    lanes = lax.broadcasted_iota(jnp.int32, (gw, 256), 1)
    for dx in range(3):
        acc = lax.dot_general(
            cols[:, 256 * dx : 256 * dx + 256],
            lines[...],
            (((0,), (0,)), ((), ())),
            preferred_element_type=jnp.float32,
        )
        for dy in range(3):
            small = jnp.zeros((gw, 256), jnp.float32)
            for g in range(PACK):
                piece = acc[gw * g : gw * g + gw, 256 * dy : 256 * dy + 256]
                small = jnp.where((lanes >= gw * g) & (lanes < gw * g + gw), piece, small)
            out_ref[3 * dy + dx, 0] = small


def conv_kernel(step, tall, width, sides, glob_ref, *refs):
    for ref in refs:
        if ref.shape[0] == tall:
            clear_edges(ref)
    for flag, side in ((1, sides[0]), (0, sides[1])):

        @pl.when(glob_ref[0] == flag)
        def _(side=side):
            step(width, side, glob_ref, refs)


def pack_kernel(gw, k_ref, out_ref):
    width = PACK * gw
    lane = lax.broadcasted_iota(jnp.int32, (gw, 256), 1)
    row = lax.broadcasted_iota(jnp.int32, (gw, 256), 0)
    spread = jnp.zeros((gw, 256), jnp.float32)
    for g in range(PACK):
        spread = jnp.where(lane == row + gw * g, 1.0, spread)
    spread = spread.astype(jnp.bfloat16)
    lane = lax.broadcasted_iota(jnp.int32, (width, 256), 1)
    row = lax.broadcasted_iota(jnp.int32, (width, 256), 0)
    inside = lane < 0
    for g in range(PACK):
        low, high = gw * g, gw * g + gw
        inside = inside | ((lane >= low) & (lane < high) & (row >= low) & (row < high))
    rest = jnp.zeros((256 - width, 256), jnp.float32)
    for dy in range(3):
        for dx in range(3):
            tap = k_ref[3 * dy + dx].astype(jnp.float32).reshape(width, gw).astype(jnp.bfloat16)
            wide = jnp.dot(tap, spread, preferred_element_type=jnp.float32)
            out_ref[0, 256 * dx : 256 * dx + 256, 256 * dy : 256 * dy + 256] = jnp.concatenate(
                [jnp.where(inside, wide, 0.0), rest], axis=0
            ).astype(jnp.bfloat16)


def pack_blocks(first, count, kernel, done=None):
    taps, groups, gw, _ = kernel.shape
    given = () if done is None else (done,)

    def body(k_ref, *refs):
        pack_kernel(gw, k_ref, refs[-1])

    return pl.pallas_call(
        body,
        grid=(count,),
        in_specs=[pl.BlockSpec((taps, PACK, gw, gw), lambda b: (0, b + first, 0, 0))]
        + [pl.BlockSpec(memory_space=pl.ANY)] * len(given),
        out_specs=pl.BlockSpec((1, 768, 768), lambda b: (b + first, 0, 0)),
        out_shape=jax.ShapeDtypeStruct((groups // PACK, 768, 768), jnp.bfloat16),
        input_output_aliases={1: 0} if given else {},
        compiler_params=params(),
        cost_estimate=cost(3),
        name="pack",
    )(kernel, *given)


def tile_specs(rows, width, chans, first=0):
    def spec(j):
        last = -(-chans // 128) - 1
        return pl.BlockSpec(
            (rows, 128), lambda b, s: (0, jnp.minimum((b + first) * width // 128 + j, last))
        )

    return [spec(j) for j in range(3)]


def conv_specs(rows):
    whole = lambda r: pl.BlockSpec((r, 2048), lambda b, s: (0, 0))
    mask = pl.BlockSpec((4, rows, 128), lambda b, s: (0, 0, 0))
    kern = pl.BlockSpec((1, 768, 768), lambda b, s: (b, 0, 0))
    return whole, mask, kern


def conv_scratch(rows, count):
    tall = rows + 2 * EDGE
    return [pltpu.VMEM((tall, 256), jnp.float32)] + [pltpu.VMEM((rows, 768), jnp.bfloat16)] * count


def conv_fwd(glob, h, par, masks, packed, width, sides):
    rows, chans = h.shape
    whole, mask, kern = conv_specs(rows)
    tiles = functools.partial(tile_specs, width=width, chans=chans)
    return pl.pallas_call(
        functools.partial(conv_kernel, fwd_step, rows + 2 * EDGE, width, sides),
        grid_spec=pltpu.PrefetchScalarGridSpec(
            num_scalar_prefetch=1,
            grid=(packed.shape[0],),
            in_specs=tiles(rows) + tiles(8) + [mask, kern],
            out_specs=[whole(rows), whole(8)],
            scratch_shapes=conv_scratch(rows, 1) + [pltpu.VMEM((rows + 2 * EDGE, 768), jnp.float32)],
        ),
        out_shape=[
            jax.ShapeDtypeStruct((rows, chans), jnp.float32),
            jax.ShapeDtypeStruct((8, chans), jnp.float32),
        ],
        compiler_params=params(),
        cost_estimate=cost(20),
        name="conv_fwd",
    )(glob, h, h, h, par, par, par, masks, packed)


def conv_dgrad(glob, grad, h, par, masks, packed, width, sides):
    rows, chans = h.shape
    whole, mask, kern = conv_specs(rows)
    tiles = functools.partial(tile_specs, width=width, chans=chans)
    return pl.pallas_call(
        functools.partial(conv_kernel, dgrad_step, rows + 2 * EDGE, width, sides),
        grid_spec=pltpu.PrefetchScalarGridSpec(
            num_scalar_prefetch=1,
            grid=(packed.shape[0],),
            in_specs=tiles(rows) + tiles(rows) + tiles(8) + [mask, kern],
            out_specs=[whole(rows), whole(8)],
            scratch_shapes=conv_scratch(rows, 1) + [pltpu.VMEM((rows + 2 * EDGE, 768), jnp.float32)],
        ),
        out_shape=[
            jax.ShapeDtypeStruct((rows, chans), jnp.float32),
            jax.ShapeDtypeStruct((8, chans), jnp.float32),
        ],
        compiler_params=params(),
        cost_estimate=cost(20),
        name="conv_dgrad",
    )(glob, grad, grad, grad, h, h, h, par, par, par, masks, packed)


def conv_wgrad(glob, grad, h, par, masks, first, count, blocks, width, sides, done=None):
    rows, chans = h.shape
    whole, mask, kern = conv_specs(rows)
    tiles = functools.partial(tile_specs, width=width, chans=chans, first=first)
    gw = width // PACK
    given = () if done is None else (done,)
    return pl.pallas_call(
        functools.partial(conv_kernel, wgrad_step, rows + 2 * EDGE, width, sides),
        grid_spec=pltpu.PrefetchScalarGridSpec(
            num_scalar_prefetch=1,
            grid=(count,),
            in_specs=tiles(rows) + tiles(rows) + tiles(8) + [mask]
            + [pl.BlockSpec(memory_space=pl.ANY)] * len(given),
            out_specs=pl.BlockSpec((9, 1, gw, 256), lambda b, s: (0, b + first, 0, 0)),
            scratch_shapes=conv_scratch(rows, 0) + conv_scratch(rows, 2),
        ),
        out_shape=jax.ShapeDtypeStruct((9, blocks, gw, 256), jnp.float32),
        input_output_aliases={11: 0} if given else {},
        compiler_params=params(),
        cost_estimate=cost(2 * count),
        name="conv_wgrad",
    )(
        jnp.concatenate([glob, jnp.full((1,), first, jnp.int32)]),
        grad,
        grad,
        grad,
        h,
        h,
        h,
        par,
        par,
        par,
        masks,
        *given,
    )


from jax.experimental.layout import Layout, with_layout_constraint
from jax.sharding import PartitionSpec as P

IMG_DEV = 4
SIDE = 14
SMALL_SIDE = 7
LOW_COLUMNS = 0
TAIL = (0, 1, 2, 0, 2, 1, 0, 2, 0, 2, 1, 2, 0, 2)
WIDE = 2048
WIDE_PROTOS = 3072

norm_epsilon = 1e-05
length_epsilon = 1e-06
sharpening_divisor = 0.1
sharpness = 0.05
exact_mode = lax.Precision.HIGHEST


def plain(value):
    return with_layout_constraint(value, Layout(major_to_minor=tuple(range(value.ndim))))


def swap(value, axis, mask):
    pairs = [(source, source ^ mask) for source in range(lax.axis_size(axis))]
    if value.ndim < 3:
        return lax.ppermute(value, axis, pairs)
    return plain(lax.ppermute(plain(value), axis, pairs))


def tie(*values):
    return lax.optimization_barrier(values)


def smooth_gate(values):
    return values * jax.nn.sigmoid(values)


def smooth_slope(values):
    sigma_values = jax.nn.sigmoid(values)
    return sigma_values * (1.0 + values * (1.0 - sigma_values))


def exact_dot(left, right):
    return jnp.dot(left, right, precision=exact_mode, preferred_element_type=jnp.float32)


def spread_dot(member_rows, values):
    terms, rest = [], values
    for _ in range(3):
        term = lax.reduce_precision(rest, 8, 7)
        terms.append(term.astype(jnp.bfloat16))
        rest = rest - term
    return jnp.dot(
        jnp.concatenate([member_rows] * 3, axis=1),
        jnp.concatenate(terms, axis=0),
        preferred_element_type=jnp.float32,
    )


def pool_dot(member, values):
    return jnp.dot(member, values.astype(jnp.bfloat16), preferred_element_type=jnp.float32)


def bits_of(size):
    return [1 << bit for bit in range(size.bit_length() - 1)]


def stream_sum(value, work=(), inputs=()):
    made = []
    if work:
        value, inputs = tie(value, inputs)
    for k, mask in enumerate([0] + bits_of(lax.axis_size("img"))):
        other = swap(value, "img", mask) if mask else swap(value, "crop", 1)
        if k < len(work):
            made.append(work[k](*inputs, *made[-1:]))
            value, other, inputs, made[-1] = tie(value, other, inputs, made[-1])
        value = value + other
    return value, made


def quarters(blocks):
    cuts = [blocks * i // 4 for i in range(5)]
    return [(low, high - low) for low, high in zip(cuts, cuts[1:])]


def pick(value, index, axis):
    return lax.dynamic_index_in_dim(value, index, axis, keepdims=False)


def slab_rows(width, devices):
    return -(-(width // devices) // 8) * 8


def slab_offset(index, width, devices):
    share = width // devices
    return 2 * share * (index // 2) + (index % 2) * (2 * share - slab_rows(width, devices))


def slab_part(devices, width, height, place_ref, left_ref, right_ref):
    step = pl.program_id(0)
    half = devices // 4
    apart = jnp.where(step < half, 2 * step, 2 * (step - half) + 1)
    index = 2 * (apart ^ place_ref[1]) + place_ref[0]
    offset = slab_offset(index, width, devices)
    base = jnp.minimum(offset // 128, left_ref.shape[1] // 128 - 3) * 128
    wide = left_ref[:, pl.ds(pl.multiple_of(base, 128), 384)].astype(jnp.float32)
    shift = offset - base
    moved = pltpu.roll(wide, jnp.where(shift == 0, 0, 384 - shift), 1)[:, :height]
    return lax.dot_general(
        moved.astype(jnp.bfloat16),
        right_ref[...],
        (((0,), (0,)), ((), ())),
        preferred_element_type=jnp.float32,
    )


def far_kernel(devices, width, height, low, place_ref, left_ref, right_ref, *refs):
    acc = slab_part(devices, width, height, place_ref, left_ref, right_ref)
    if low:
        refs[0][0] = acc[:, :low]
    refs[-1][0] = acc[:, low:]


def near_kernel(devices, width, height, low, place_ref, left_ref, right_ref, *refs):
    held = refs[-1]
    keep_x, send_x, keep_y, send_y = refs[-5:-1]
    acc = slab_part(devices, width, height, place_ref, left_ref, right_ref)
    step = pl.program_id(0)
    if low:
        low_in, high_in, keep_low, send_low = refs[:4]
        total = acc[:, :low] + low_in[0]

        @pl.when(step < devices // 4)
        def _():
            keep_low[0] = total

        @pl.when(step >= devices // 4)
        def _():
            send_low[0] = total

    else:
        high_in = refs[0]
    held[...] = acc[:, low:] + high_in[0]
    rows = height // 8
    bits = (place_ref[2], place_ref[3])
    for half, keep, send in ((0, keep_x, send_x), (1, keep_y, send_y)):
        first, second = bits[half], bits[1 - half]
        for other, ref in ((0, keep), (1, send)):
            for last in range(2):
                block = 4 * half + 2 * (first ^ other) + (second ^ last)
                ref[last, 0] = held[pl.ds(pl.multiple_of(block * rows, rows), rows), :]


def slab_specs(devices, rows, height, low):
    sides = [pl.BlockSpec((rows, WIDE), lambda t, c: (0, 0))] * 2
    widths = [low, WIDE - low] if low else [WIDE]
    parts = [pl.BlockSpec((1, height, n), lambda t, c: (t, 0, 0)) for n in widths]
    shapes = [jax.ShapeDtypeStruct((devices // 2, height, n), jnp.float32) for n in widths]
    return sides, parts, shapes


def far_product(place, left, right, devices, low):
    rows, width = left.shape
    height = slab_rows(width, devices)
    sides, parts, shapes = slab_specs(devices, rows, height, low)
    return pl.pallas_call(
        functools.partial(far_kernel, devices, width, height, low),
        grid_spec=pltpu.PrefetchScalarGridSpec(
            num_scalar_prefetch=1, grid=(devices // 2,), in_specs=sides, out_specs=parts
        ),
        out_shape=shapes,
        compiler_params=pltpu.CompilerParams(vmem_limit_bytes=40 * 1024 * 1024),
        cost_estimate=cost(9),
        name="far_product",
    )(place, left, right)


def near_product(place, left, right, devices, low, arrived):
    rows, width = left.shape
    height = slab_rows(width, devices)
    sides, parts, _ = slab_specs(devices, rows, height, low)
    chips, half = devices // 2, devices // 4
    high = WIDE - low
    piece = pl.BlockSpec((2, 1, height // 8, high), lambda t, c: (0, t, 0, 0))
    out_specs = [piece] * 4
    out_shape = [jax.ShapeDtypeStruct((2, chips, height // 8, high), jnp.float32)] * 4
    if low:
        out_specs = [
            pl.BlockSpec((1, height, low), lambda t, c: (jnp.minimum(t, half - 1), 0, 0)),
            pl.BlockSpec((1, height, low), lambda t, c: (jnp.maximum(t - half, 0), 0, 0)),
        ] + out_specs
        out_shape = [jax.ShapeDtypeStruct((half, height, low), jnp.float32)] * 2 + out_shape
    return pl.pallas_call(
        functools.partial(near_kernel, devices, width, height, low),
        grid_spec=pltpu.PrefetchScalarGridSpec(
            num_scalar_prefetch=1,
            grid=(chips,),
            in_specs=sides + parts,
            out_specs=out_specs,
            scratch_shapes=[pltpu.VMEM((height, high), jnp.float32)],
        ),
        out_shape=out_shape,
        compiler_params=pltpu.CompilerParams(vmem_limit_bytes=48 * 1024 * 1024),
        cost_estimate=cost(13),
        name="near_product",
    )(place, left, right, *arrived)


UNIT_ROWS = 704


def unit_start(index, share, unit, gw, rows):
    return jnp.minimum((share * index // unit) * gw, rows - UNIT_ROWS)


def unit_part(devices, size, gw, place_ref, units_ref):
    step = pl.program_id(0)
    half = devices // 4
    apart = jnp.where(step < half, 2 * step, 2 * (step - half) + 1)
    index = 2 * (apart ^ place_ref[1]) + place_ref[0]
    start = unit_start(index, size // devices, gw * gw * PACK, gw, units_ref.shape[0])
    return pl.multiple_of(start, 8)


def far_units_kernel(devices, size, gw, place_ref, units_ref, out_ref):
    start = unit_part(devices, size, gw, place_ref, units_ref)
    out_ref[0] = units_ref[pl.ds(start, UNIT_ROWS), :]


def near_units_kernel(devices, size, gw, place_ref, units_ref, in_ref, *refs):
    keep_x, send_x, keep_y, send_y = refs
    start = unit_part(devices, size, gw, place_ref, units_ref)
    rows = UNIT_ROWS // 8
    bits = (place_ref[2], place_ref[3])
    for half, keep, send in ((0, keep_x, send_x), (1, keep_y, send_y)):
        first, second = bits[half], bits[1 - half]
        for other, ref in ((0, keep), (1, send)):
            for last in range(2):
                block = 4 * half + 2 * (first ^ other) + (second ^ last)
                skip = pl.multiple_of(block * rows, 8)
                ref[last, 0] = (
                    units_ref[pl.ds(pl.multiple_of(start + skip, 8), rows), :]
                    + in_ref[0, pl.ds(skip, rows), :]
                )


def unit_call(place, units, devices, size, gw, arrived=None):
    rows = units.shape[0]
    chips = devices // 2
    part = pl.BlockSpec((1, UNIT_ROWS, 256), lambda t, c: (t, 0, 0))
    if arrived is None:
        body, extra = far_units_kernel, ()
        out_specs, out_shape = part, jax.ShapeDtypeStruct((chips, UNIT_ROWS, 256), jnp.float32)
    else:
        body, extra = near_units_kernel, (arrived,)
        piece = (2, chips, UNIT_ROWS // 8, 256)
        out_specs = [pl.BlockSpec((2, 1) + piece[2:], lambda t, c: (0, t, 0, 0))] * 4
        out_shape = [jax.ShapeDtypeStruct(piece, jnp.float32)] * 4
    return pl.pallas_call(
        functools.partial(body, devices, size, gw),
        grid_spec=pltpu.PrefetchScalarGridSpec(
            num_scalar_prefetch=1,
            grid=(chips,),
            in_specs=[pl.BlockSpec((rows, 256), lambda t, c: (0, 0))] + [part] * len(extra),
            out_specs=out_specs,
        ),
        out_shape=out_shape,
        compiler_params=pltpu.CompilerParams(vmem_limit_bytes=32 * 1024 * 1024),
        cost_estimate=cost(3),
        name="units",
    )(place, units, *extra)


def share_kernel(left_ref, right_ref, out_ref):
    out_ref[...] = lax.dot_general(
        left_ref[...].astype(jnp.bfloat16),
        right_ref[...].astype(jnp.bfloat16),
        (((0,), (0,)), ((), ())),
        preferred_element_type=jnp.float32,
    )


def share_product(left, right):
    return pl.pallas_call(
        share_kernel,
        out_shape=jax.ShapeDtypeStruct((left.shape[1], right.shape[1]), jnp.float32),
        compiler_params=pltpu.CompilerParams(vmem_limit_bytes=32 * 1024 * 1024),
        cost_estimate=cost(3),
        name="share_product",
    )(left, right)


def crop_bits():
    crop = lax.axis_index("crop")
    return (crop & 1, crop >> 1)


def crop_halves(value):
    lead, rows, cols = value.shape
    whole = value.reshape(lead, 2, 2, 2, rows // 8, cols)
    return [whole[:, 0], whole[:, 1]]


CROP_ORDER = ((0, 1), (1, 0))


def crop_send(parts, step):
    bits = crop_bits()
    return [
        swap(pick(part, 1 - bits[order[step]], 1), "crop", 1 << order[step])
        for part, order in zip(parts, CROP_ORDER)
    ]


def crop_add(parts, arrived, step):
    bits = crop_bits()
    return [
        pick(part, bits[order[step]], 1) + other
        for part, other, order in zip(parts, arrived, CROP_ORDER)
    ]


def crop_fetch(parts, step):
    return [swap(part, "crop", 1 << order[1 - step]) for part, order in zip(parts, CROP_ORDER)]


def crop_join(parts, arrived, step):
    bits = crop_bits()
    joined = []
    for part, other, order in zip(parts, arrived, CROP_ORDER):
        upper = bits[order[1 - step]] == 1
        joined.append(
            jnp.stack([jnp.where(upper, other, part), jnp.where(upper, part, other)], axis=1)
        )
    return joined


def crop_whole(parts):
    both = jnp.stack(parts, axis=1)
    return both.reshape(both.shape[0], -1, both.shape[-1])


def chip_swap(value, step):
    return swap(value, "img", 2 << step)


class LowChain:
    def __init__(self, keep, send):
        self.keep, self.away = keep, [send]
        self.chips = keep.shape[0].bit_length()
        self.steps, self.step = self.chips + 4, 0

    def send(self):
        if self.step < self.chips:
            return [chip_swap(v, self.step) for v in self.away]
        if self.step < self.chips + 2:
            return crop_send(self.keep, self.step - self.chips)
        return crop_fetch(self.keep, self.step - self.chips - 2)

    def take(self, arrived):
        step, chips = self.step, self.chips
        if step < chips:
            total = self.keep + arrived[0]
            half = total.shape[0] // 2
            self.keep, self.away = total[:half], [total[half:]]
            if step == chips - 1:
                self.keep, self.away = crop_halves(total), []
        elif step < chips + 2:
            self.keep = crop_add(self.keep, arrived, step - chips)
        else:
            self.keep = crop_join(self.keep, arrived, step - chips - 2)
        self.step += 1

    def result(self):
        return crop_whole(self.keep)[0]


class HighChain:
    def __init__(self, keep_x, send_x, keep_y, send_y):
        self.keep, self.away = [keep_x, keep_y], [send_x, send_y]
        self.chips = keep_x.shape[1].bit_length() - 1
        self.steps, self.step = self.chips + 4, 0

    def send(self):
        step = self.step
        if step < 2:
            return [swap(v, "crop", 1 << order[step]) for v, order in zip(self.away, CROP_ORDER)]
        if step < self.chips + 2:
            return [chip_swap(v, step - 2) for v in self.away]
        return crop_fetch(self.keep, step - self.chips - 2)

    def take(self, arrived):
        step, chips = self.step, self.chips
        if step < chips + 2:
            total = [keep + other for keep, other in zip(self.keep, arrived)]
            if step == 0:
                self.keep, self.away = [v[0] for v in total], [v[1] for v in total]
            else:
                if step == 1:
                    total = [jnp.concatenate(total, axis=1)]
                half = total[0].shape[0] // 2
                self.keep, self.away = [total[0][:half]], [total[0][half:]]
            if step == chips + 1:
                rows = total[0].shape[1] // 2
                self.keep, self.away = [total[0][:, :rows], total[0][:, rows:]], []
        else:
            self.keep = crop_join(self.keep, arrived, step - chips - 2)
        self.step += 1

    def result(self):
        return crop_whole(self.keep)[0]


class CropSum:
    steps = 4

    def __init__(self, value):
        self.away = []
        self.keep = crop_halves(value[None])
        self.step = 0

    def send(self):
        if self.step < 2:
            return crop_send(self.keep, self.step)
        return crop_fetch(self.keep, self.step - 2)

    def take(self, arrived):
        if self.step < 2:
            self.keep = crop_add(self.keep, arrived, self.step)
        else:
            self.keep = crop_join(self.keep, arrived, self.step - 2)
        self.step += 1

    def result(self):
        return crop_whole(self.keep)[0]


class Flow:
    def __init__(self):
        self.sent = {}

    def begin(self, chain):
        self.sent[id(chain)] = chain.send()

    def advance(self, chain, beside):
        arrived, beside = tie(self.sent[id(chain)], beside)
        chain.take(arrived)
        (chain.keep, chain.away), beside = tie((chain.keep, chain.away), beside)
        if chain.step < chain.steps:
            self.begin(chain)
        return beside


def shards(
    pixels,
    counts,
    slot_order,
    w_in,
    kernel,
    w_red,
    b_red,
    w_exp,
    b_exp,
    w_out,
    gain_one,
    shift_one,
    gain_two,
    shift_two,
    gain_three,
    shift_three,
    protos,
):
    row_count = pixels.shape[2]
    width = pixels.shape[3]
    proto_count = protos.shape[1]
    squeeze = w_red.shape[1]
    seg_count = row_count // (SMALL_SIDE * SMALL_SIDE)
    slot_total = slot_order.shape[1]
    devices = lax.axis_size("img")
    img_index = lax.axis_index("img")
    crop_index = lax.axis_index("crop")
    core = img_index % 2
    fast = width % devices == 0 and (2 * width // devices) % 8 == 0
    is_global = crop_index < 2
    glob = is_global.astype(jnp.int32).reshape(1)
    stream_rows = 2.0 * devices * row_count
    couple_number = 2.0 * devices * (IMG_DEV + slot_total)
    inputs = pixels.reshape(row_count, width)
    row_ids = jnp.arange(row_count, dtype=jnp.int32)
    side = jnp.where(is_global, SIDE, SMALL_SIDE)
    seg_of_row = row_ids // (side * side)
    across = row_ids % side
    down = (row_ids // side) % side
    masks = jnp.stack([across > 0, across < side - 1, down > 0, down < side - 1])
    masks = jnp.broadcast_to(masks.astype(jnp.float32)[:, :, None], (4, row_count, 128))
    member = (seg_of_row[None, :] == jnp.arange(seg_count, dtype=jnp.int32)[:, None]).astype(
        jnp.bfloat16
    )
    member_rows = member.T
    crop_pixels = jnp.where(is_global, float(SIDE * SIDE), float(SMALL_SIDE * SMALL_SIDE))
    block_width = PACK * kernel.shape[2]
    block_count = kernel.shape[1] // PACK
    sides = (SIDE, SMALL_SIDE)

    def norm_rows(local_sums, work=(), inputs=()):
        sums, made = stream_sum(local_sums, work, inputs)
        average = sums[0] / stream_rows
        inv = lax.rsqrt(sums[1] / stream_rows - average * average + norm_epsilon)
        return average, inv, made

    def back_rows(local_sums, gain, inv, work=(), inputs=()):
        sums, made = stream_sum(local_sums, work, inputs)
        return sums, gain * inv, sums[0] / stream_rows, sums[1] / stream_rows, made

    hidden_one = jnp.dot(inputs, w_in, preferred_element_type=jnp.float32)
    sums = jnp.stack([jnp.sum(hidden_one, axis=0), jnp.sum(hidden_one * hidden_one, axis=0)])
    mean_one, inv_one, packed = norm_rows(
        sums,
        [functools.partial(pack_blocks, low, count) for low, count in quarters(block_count)],
        (kernel,),
    )
    packed = packed[-1]
    zero_row = jnp.zeros((width,), jnp.float32)
    scale_one = gain_one * inv_one
    par = jnp.stack(
        [scale_one, shift_one - mean_one * scale_one, inv_one, -mean_one * inv_one] + [zero_row] * 4
    )
    hidden_two, sums = conv_fwd(glob, hidden_one, par, masks, packed, block_width, sides)
    mean_two, inv_two, _ = norm_rows(sums[:2])
    centred_two = (hidden_two - mean_two) * inv_two
    pre_two = centred_two * gain_two + shift_two
    act_two = smooth_gate(pre_two)
    red_float = w_red.astype(jnp.float32)
    exp_float = w_exp.astype(jnp.float32)
    pooled = pool_dot(member, act_two) / crop_pixels
    reduce_pre = exact_dot(pooled, red_float) + b_red
    reduced = smooth_gate(reduce_pre)
    gate_values = jax.nn.sigmoid(exact_dot(reduced, exp_float) + b_exp)
    gate_rows = spread_dot(member_rows, gate_values)
    excited = (act_two * gate_rows).astype(jnp.bfloat16)
    hidden_three = jnp.dot(excited, w_out, preferred_element_type=jnp.float32)
    sums = jnp.stack([jnp.sum(hidden_three, axis=0), jnp.sum(hidden_three * hidden_three, axis=0)])
    mean_three, inv_three, _ = norm_rows(sums)
    centred_three = (hidden_three - mean_three) * inv_three
    summed_in = inputs.astype(jnp.float32) + centred_three * gain_three + shift_three
    output = smooth_gate(summed_in)
    pooled_out = (
        jnp.dot(
            member.astype(jnp.float32),
            output,
            precision=lax.Precision.HIGH,
            preferred_element_type=jnp.float32,
        )
        / crop_pixels
    )
    length_inv = lax.rsqrt(jnp.sum(pooled_out * pooled_out, axis=1, keepdims=True) + length_epsilon)
    unit_wide = pooled_out * length_inv
    unit_rows = unit_wide.astype(jnp.bfloat16)
    match_matrix = jnp.dot(unit_rows, protos, preferred_element_type=jnp.float32)

    every = match_matrix[:IMG_DEV]
    for mask in bits_of(devices):
        every = jnp.concatenate([every, swap(every, "img", mask)], axis=0)
    plan_rows = jnp.exp(every / sharpness)
    for sweep_index in range(3):
        plan_rows = plan_rows / jnp.sum(plan_rows, axis=0, keepdims=True)
        plan_rows = plan_rows / jnp.sum(plan_rows, axis=1, keepdims=True)
    codes = plan_rows[:IMG_DEV]
    partner = lax.ppermute(codes, "crop", [(0, 1), (1, 0)])
    both_codes = lax.ppermute(codes, "crop", [(0, 2), (1, 3)]) + lax.ppermute(
        codes, "crop", [(0, 3), (1, 2)]
    )
    wide_target = jnp.concatenate(
        [partner, jnp.zeros((seg_count - IMG_DEV, proto_count), jnp.float32)], axis=0
    )
    ends = [jnp.sum(counts[0, : i + 1]) for i in range(IMG_DEV)]
    first_slot = jnp.maximum(crop_index - 2, 0) * seg_count
    order_here = lax.dynamic_slice_in_dim(slot_order[0], first_slot, seg_count)
    owner = sum((order_here >= end).astype(jnp.int32) for end in ends)
    narrow_target = jnp.zeros((seg_count, proto_count), jnp.float32)
    for i in range(IMG_DEV):
        narrow_target = jnp.where(owner[:, None] == i, both_codes[i : i + 1], narrow_target)
    target = jnp.where(is_global, wide_target, narrow_target)
    sharpened = match_matrix / sharpening_divisor
    shifted = sharpened - jnp.max(sharpened, axis=1, keepdims=True)
    log_probs = shifted - jnp.log(jnp.sum(jnp.exp(shifted), axis=1, keepdims=True))
    loss_here = -jnp.sum(target * log_probs) / couple_number
    scores_wide = (jnp.exp(log_probs) * jnp.sum(target, axis=1, keepdims=True) - target) / (
        sharpening_divisor * couple_number
    )
    grad_scores = scores_wide.astype(jnp.bfloat16)

    grad_unit = jnp.einsum("sk,wk->sw", grad_scores, protos, preferred_element_type=jnp.float32)
    inner_term = jnp.sum(pooled_out * grad_unit, axis=1, keepdims=True)
    grad_pooled_out = (
        length_inv * grad_unit - pooled_out * length_inv * length_inv * length_inv * inner_term
    )
    grad_output = spread_dot(member_rows, grad_pooled_out / crop_pixels)
    grad_summed = grad_output * smooth_slope(summed_in)
    sums_three, scale_three, first, second, _ = back_rows(
        jnp.stack([jnp.sum(grad_summed, axis=0), jnp.sum(grad_summed * centred_three, axis=0)]),
        gain_three,
        inv_three,
    )
    grad_three_low = (scale_three * (grad_summed - first - centred_three * second)).astype(
        jnp.bfloat16
    )
    if fast:
        share = width // devices
        height = slab_rows(width, devices)
        chip = img_index // 2
        near = jnp.stack([core, chip, crop_index & 1, crop_index >> 1]).astype(jnp.int32)
        far = jnp.stack([1 - core, chip, crop_index & 1, crop_index >> 1]).astype(jnp.int32)

        def kept(value):
            skip = core * (value.shape[0] - share)
            return lax.dynamic_slice_in_dim(value, skip, share, axis=0)

        seen_scores = lax.all_gather(
            jnp.concatenate(
                [
                    unit_wide,
                    jnp.zeros((seg_count, WIDE - width), jnp.float32),
                    scores_wide,
                    jnp.zeros((seg_count, WIDE_PROTOS - proto_count), jnp.float32),
                ],
                axis=1,
            ),
            "img",
            tiled=True,
        )

    grad_excited = jnp.einsum(
        "rv,wv->rw", grad_three_low, w_out, preferred_element_type=jnp.float32
    )
    flow = Flow()
    if fast:
        grad_excited, seen_scores = tie(grad_excited, seen_scores)
        protos_sum = CropSum(
            share_product(
                lax.dynamic_slice_in_dim(seen_scores, img_index * share, height, axis=1),
                seen_scores[:, WIDE:],
            )
        )
        (protos_sum.keep, grad_excited) = tie(protos_sum.keep, grad_excited)
        flow.begin(protos_sum)
    grad_gate = pool_dot(member, grad_excited * act_two)
    grad_gate_pre = grad_gate * gate_values * (1.0 - gate_values)
    grad_reduce_pre = exact_dot(grad_gate_pre, exp_float.T) * smooth_slope(reduce_pre)
    grad_pooled = exact_dot(grad_reduce_pre, red_float.T)
    grad_act_two = grad_excited * gate_rows + spread_dot(member_rows, grad_pooled / crop_pixels)
    grad_pre_two = grad_act_two * smooth_slope(pre_two)
    bias_row = jnp.concatenate(
        [
            jnp.sum(grad_reduce_pre, axis=0),
            loss_here.reshape(1),
            jnp.zeros((width - squeeze - 1,), jnp.float32),
        ]
    )
    local_two = jnp.stack(
        [
            jnp.sum(grad_pre_two, axis=0),
            jnp.sum(grad_pre_two * centred_two, axis=0),
            jnp.sum(grad_gate_pre, axis=0),
            bias_row,
        ]
    )
    work = []
    if fast:
        seen_gates = lax.all_gather(
            jnp.concatenate([pooled, reduced, grad_reduce_pre, grad_gate_pre], axis=1),
            "img",
            tiled=True,
        )

        def out_far(left, right):
            return far_product(far, left, right, devices, 0)

        def proto_step(left, right, arrived):
            return flow.advance(protos_sum, arrived)

        work = [out_far, proto_step]
    sums_two, scale_two, first, second, made = back_rows(
        local_two, gain_two, inv_two, work, (excited, grad_three_low)
    )
    if fast:
        arrived = [swap(v, "img", 1) for v in made[-1]]
    grad_two_low = (scale_two * (grad_pre_two - first - centred_two * second)).astype(jnp.bfloat16)
    if fast:
        grad_two_low, arrived = tie(grad_two_low, arrived)
        arrived = flow.advance(protos_sum, arrived)
        outs = HighChain(*near_product(near, excited, grad_three_low, devices, 0, arrived))
        outs.keep, outs.away, grad_two_low = tie(outs.keep, outs.away, grad_two_low)
        flow.begin(outs)
    grad_pre_one, sums = conv_dgrad(
        glob, grad_two_low, hidden_one, par, masks, packed, block_width, sides
    )

    def some_wgrad(low, count, grad, done=None):
        return conv_wgrad(
            glob, grad, hidden_one, par, masks, low, count, block_count, block_width, sides, done
        )

    cut = block_count // 2
    steps = [
        functools.partial(some_wgrad, 0, cut),
        functools.partial(some_wgrad, cut, block_count - cut),
    ]
    early = []
    if fast:
        grad_two_low, grad_pre_one, sums = tie(grad_two_low, grad_pre_one, sums)
        units = steps[0](grad_two_low)
        units = flow.advance(outs, units)
        units, sums = tie(units, sums)

        def my_columns(value):
            count = value.shape[1] // devices
            return lax.dynamic_slice_in_dim(value, img_index * count, count, axis=1)

        def shares_of(seen):
            seen = flow.advance(protos_sum, seen)
            return (
                exact_dot(
                    my_columns(seen[:, :width]).T, seen[:, width + squeeze : width + 2 * squeeze]
                ),
                exact_dot(my_columns(seen[:, width : width + squeeze]).T, seen[:, width + 2 * squeeze :]),
            )

        early = [shares_of]
    sums_one, scale_one, first, second, made = back_rows(
        sums[:2], gain_one, inv_one, early, (seen_gates,) if fast else ()
    )
    centred_one = (hidden_one - mean_one) * inv_one
    grad_one_low = (scale_one * (grad_pre_one - first - centred_one * second)).astype(jnp.bfloat16)
    if fast:
        share_red, share_exp = made[-1]
        share_red, share_exp = lax.psum((share_red, share_exp), "crop")
        sent_far = far_product(far, inputs, grad_one_low, devices, LOW_COLUMNS)
        flow.sent[id(outs)], sent_far = tie(flow.sent[id(outs)], sent_far)
        outs.take(flow.sent[id(outs)])
        flow.begin(outs)
        arrived = [swap(v, "img", 1) for v in sent_far]
        parts = near_product(near, inputs, grad_one_low, devices, LOW_COLUMNS, arrived)
        ins = HighChain(*parts)
        units, grad_two_low, grad_one_low, ins.keep, ins.away = tie(
            units, grad_two_low, grad_one_low, ins.keep, ins.away
        )
        flow.begin(ins)
        units = steps[1](grad_two_low, units)
        units = flow.advance(outs, units)
        units = flow.advance(protos_sum, units)
        gw = kernel.shape[2]
        unit_size = gw * gw * PACK
        units = units.reshape(-1, 256)
        swapped = unit_call(far, units, devices, kernel.size, gw)
        swapped, units, grad_one_low = tie(swapped, units, grad_one_low)
        swapped, units, grad_one_low = flow.advance(ins, (swapped, units, grad_one_low))
        swapped = swap(swapped, "img", 1)
        grad_inputs = (
            jnp.einsum("rv,wv->rw", grad_one_low, w_in, preferred_element_type=jnp.float32)
            + grad_summed
        )
        swapped, grad_inputs = tie(swapped, grad_inputs)
        gks = HighChain(*unit_call(near, units, devices, kernel.size, gw, swapped))
        flow.begin(gks)
        chains = [ins, outs, gks]
        last = None
        for chain in (chains[index] for index in TAIL):
            arrived = flow.sent[id(chain)]
            if last is not None:
                arrived, _ = tie(arrived, (last.keep, last.away))
            chain.take(arrived)
            if chain.step < chain.steps:
                flow.begin(chain)
            last = chain
    else:
        made = None
        for step in steps:
            made = step(grad_two_low, made)
        small_kernel = made
        grad_inputs = (
            jnp.einsum("rv,wv->rw", grad_one_low, w_in, preferred_element_type=jnp.float32)
            + grad_summed
        )

    last = jnp.concatenate([sums_one, sums_two, sums_three], axis=0)
    last = last + swap(last, "crop", 2)
    tail = (
        last[5, :squeeze],
        last[4],
        last[1],
        last[0],
        last[3],
        last[2],
        last[7],
        last[6],
    )
    loss_total = last[5, squeeze]

    if fast:
        flat_in = kept(ins.result()[:, :width]).reshape(-1)
        flat_out = kept(outs.result()[:, :width]).reshape(-1)
        flat_protos = protos_sum.result()[:share, :proto_count].reshape(-1)
        flat_red = share_red.reshape(-1)
        flat_exp = share_exp.reshape(-1)
        total = kernel.size // devices
        first_unit = total * img_index // unit_size
        start = unit_start(img_index, total, unit_size, gw, units.size // 256)
        span = -(-total // unit_size) + 1
        mine = jnp.pad(gks.result(), ((0, gw), (0, 0)))
        mine = lax.dynamic_slice_in_dim(mine, first_unit * gw - start, span * gw, axis=0)
        mine = mine[:, : PACK * gw].reshape(span, gw, PACK, gw).transpose(0, 2, 1, 3).reshape(-1)
        flat_kernel = lax.dynamic_slice_in_dim(mine, total * img_index - unit_size * first_unit, total)
        shares = (flat_in, flat_kernel, flat_red, flat_exp, flat_out, flat_protos)
    else:
        gw = kernel.shape[2]
        grads = (
            jnp.einsum("rw,rv->wv", inputs, grad_one_low, preferred_element_type=jnp.float32),
            small_kernel[..., : PACK * gw]
            .reshape(9, block_count, gw, PACK, gw)
            .transpose(0, 1, 3, 2, 4),
            exact_dot(pooled.T, grad_reduce_pre),
            exact_dot(reduced.T, grad_gate_pre),
            jnp.einsum("rw,rv->wv", excited, grad_three_low, preferred_element_type=jnp.float32),
            jnp.einsum("sw,sk->wk", unit_rows, grad_scores, preferred_element_type=jnp.float32),
        )
        shares = tuple(
            lax.psum(
                lax.psum_scatter(grad.reshape(-1), "img", scatter_dimension=0, tiled=True), "crop"
            )
            for grad in grads
        )
    return (
        loss_total,
        output.astype(jnp.bfloat16).reshape(pixels.shape),
        grad_inputs.reshape(pixels.shape),
        *shares,
        *tail,
    )


def solution(mesh):
    return jax.shard_map(
        shards,
        mesh=mesh,
        in_specs=(P("crop", "img", None, None), P("img", None), P("img", None)) + (P(),) * 14,
        out_specs=(P(), P("crop", "img", None, None), P("crop", "img", None, None))
        + (P("img"),) * 6
        + (P(),) * 8,
        check_vma=False,
    )
```

```python
import functools
import jax
import jax.numpy as jnp
from jax import lax
from jax.experimental import pallas as pl
from jax.experimental.pallas import tpu as pltpu

VMEM_LIMIT = 56 * 1024 * 1024
PACK = 4
EDGE = 16
CHUNK = 112


def cost(micros):
    return pl.CostEstimate(flops=micros * 1000000, bytes_accessed=micros * 1000, transcendentals=0)


def params():
    return pltpu.CompilerParams(vmem_limit_bytes=VMEM_LIMIT)


def lane_of(rows):
    return lax.broadcasted_iota(jnp.int32, (rows, 128), 1)


def take(refs, start, rows, skip, width):
    a, b, c = [ref[start : start + rows, :].astype(jnp.float32) for ref in refs]
    back = lax.rem(128 - skip, 128)
    a, b, c = [pltpu.roll(v, back, 1) for v in (a, b, c)]
    lane = lane_of(rows)
    near = lane < 128 - skip
    return jnp.where(near, a, b), jnp.where(lane < width - 128, jnp.where(near, b, c), 0.0)


def put(ref, start, rows, base, skip, first, second):
    first, second = pltpu.roll(first, skip, 1), pltpu.roll(second, skip, 1)
    lane = lane_of(rows)
    inside = lane >= skip
    last = jnp.minimum(base + 2, ref.shape[1] // 128 - 1)

    def at(tile):
        return (slice(start, start + rows), pl.ds(pl.multiple_of(tile * 128, 128), 128))

    ref[at(last)] = second
    ref[at(base + 1)] = jnp.where(inside, second, first)
    ref[at(base)] = jnp.where(inside, first, ref[at(base)])


def place_of(block, width):
    start = block * width
    base = start // 128
    return base, start - base * 128


def clear_edges(ref):
    @pl.when(pl.program_id(0) == 0)
    def _():
        ref[0:EDGE, :] = jnp.zeros((EDGE, ref.shape[1]), ref.dtype)
        ref[ref.shape[0] - EDGE :, :] = jnp.zeros((EDGE, ref.shape[1]), ref.dtype)


def chunks(rows):
    return range(0, rows, CHUNK)


def fill_act(h_refs, p_refs, skip, width, starts, act):
    scale = take(p_refs, 0, 8, skip, width)
    for r in starts:
        for tile, h in enumerate(take(h_refs, r, CHUNK, skip, width)):
            pre = h * scale[tile][0:1] + scale[tile][1:2]
            value = pre * jax.nn.sigmoid(pre)
            act[EDGE + r : EDGE + r + CHUNK, 128 * tile : 128 * tile + 128] = value.astype(
                jnp.bfloat16
            ).astype(jnp.float32)


def fill_grad(g_refs, skip, width, starts, grad):
    for r in starts:
        for tile, g in enumerate(take(g_refs, r, CHUNK, skip, width)):
            grad[EDGE + r : EDGE + r + CHUNK, 128 * tile : 128 * tile + 128] = g


def stack(source, mask_ref, low, high, step, starts, dest):
    for r in starts:
        for tile in range(2):
            cols = slice(128 * tile, 128 * tile + 128)
            here = slice(r, r + CHUNK)
            before = source[EDGE + r - step : EDGE + r - step + CHUNK, cols] * mask_ref[low, here, :]
            after = source[EDGE + r + step : EDGE + r + step + CHUNK, cols] * mask_ref[high, here, :]
            middle = source[EDGE + r : EDGE + r + CHUNK, cols]
            dest[here, 128 * tile : 128 * tile + 128] = before.astype(jnp.bfloat16)
            dest[here, 256 + 128 * tile : 384 + 128 * tile] = middle.astype(jnp.bfloat16)
            dest[here, 512 + 128 * tile : 640 + 128 * tile] = after.astype(jnp.bfloat16)


def fwd_step(width, side, glob_ref, refs):
    h_refs, p_refs, (mask_ref, k_ref, out_ref, st_ref, act, cols, wide) = refs[:3], refs[3:6], refs[6:]
    rows = h_refs[0].shape[0]
    base, skip = place_of(pl.program_id(0), width)
    starts = list(chunks(rows))
    fill_act(h_refs, p_refs, skip, width, starts[:1], act)
    for i, r in enumerate(starts):
        fill_act(h_refs, p_refs, skip, width, starts[i + 1 : i + 2], act)
        stack(act, mask_ref, 0, 1, 1, [r], cols)
        wide[EDGE + r : EDGE + r + CHUNK, :] = jnp.dot(
            cols[r : r + CHUNK, :], k_ref[0], preferred_element_type=jnp.float32
        )
    sums = [jnp.zeros((8, 128), jnp.float32)] * 4
    for r in starts:
        here = slice(r, r + CHUNK)
        tiles = []
        for tile in range(2):
            lo = 128 * tile
            total = (
                wide[EDGE + r : EDGE + r + CHUNK, 256 + lo : 384 + lo]
                + wide[EDGE + r - side : EDGE + r - side + CHUNK, lo : 128 + lo] * mask_ref[2, here, :]
                + wide[EDGE + r + side : EDGE + r + side + CHUNK, 512 + lo : 640 + lo] * mask_ref[3, here, :]
            )
            tiles.append(total)
            sums[tile] += jnp.sum(total.reshape(-1, 8, 128), axis=0)
            sums[2 + tile] += jnp.sum((total * total).reshape(-1, 8, 128), axis=0)
        put(out_ref, r, CHUNK, base, skip, *tiles)
    put_sums(st_ref, base, skip, sums)


def put_sums(st_ref, base, skip, sums):
    line = lax.broadcasted_iota(jnp.int32, (8, 128), 0)
    tiles = [
        jnp.where(
            line == 0,
            jnp.sum(sums[tile], axis=0, keepdims=True),
            jnp.sum(sums[2 + tile], axis=0, keepdims=True),
        )
        for tile in range(2)
    ]
    put(st_ref, 0, 8, base, skip, *tiles)


def dgrad_step(width, side, glob_ref, refs):
    g_refs, h_refs, p_refs = refs[:3], refs[3:6], refs[6:9]
    mask_ref, k_ref, out_ref, st_ref, grad, lines, wide = refs[9:]
    rows = h_refs[0].shape[0]
    base, skip = place_of(pl.program_id(0), width)
    starts = list(chunks(rows))
    fill_grad(g_refs, skip, width, starts[:1], grad)
    for i, r in enumerate(starts):
        fill_grad(g_refs, skip, width, starts[i + 1 : i + 2], grad)
        stack_lines(grad, mask_ref, side, [r], lines)
    wide[EDGE : EDGE + rows, :] = lax.dot_general(
        lines[...], k_ref[0], (((1,), (1,)), ((), ())), preferred_element_type=jnp.float32
    )
    par = take(p_refs, 0, 8, skip, width)
    sums = [jnp.zeros((8, 128), jnp.float32)] * 4
    for r in starts:
        here = slice(r, r + CHUNK)
        h_tiles = take(h_refs, r, CHUNK, skip, width)
        tiles = []
        for tile in range(2):
            lo = 128 * tile
            total = (
                wide[EDGE + r : EDGE + r + CHUNK, 256 + lo : 384 + lo]
                + wide[EDGE + r + 1 : EDGE + r + 1 + CHUNK, lo : 128 + lo] * mask_ref[1, here, :]
                + wide[EDGE + r - 1 : EDGE + r - 1 + CHUNK, 512 + lo : 640 + lo] * mask_ref[0, here, :]
            )
            p = par[tile]
            pre = h_tiles[tile] * p[0:1] + p[1:2]
            sig = jax.nn.sigmoid(pre)
            ga = total * (sig * (1.0 + pre * (1.0 - sig)))
            xhat = h_tiles[tile] * p[2:3] + p[3:4]
            tiles.append(ga)
            sums[tile] += jnp.sum(ga.reshape(-1, 8, 128), axis=0)
            sums[2 + tile] += jnp.sum((ga * xhat).reshape(-1, 8, 128), axis=0)
        put(out_ref, r, CHUNK, base, skip, *tiles)
    put_sums(st_ref, base, skip, sums)


def stack_lines(grad, mask_ref, side, starts, dest):
    for r in starts:
        for tile in range(2):
            cols = slice(128 * tile, 128 * tile + 128)
            here = slice(r, r + CHUNK)
            below = grad[EDGE + r + side : EDGE + r + side + CHUNK, cols] * mask_ref[3, here, :]
            above = grad[EDGE + r - side : EDGE + r - side + CHUNK, cols] * mask_ref[2, here, :]
            middle = grad[EDGE + r : EDGE + r + CHUNK, cols]
            dest[here, 128 * tile : 128 * tile + 128] = below.astype(jnp.bfloat16)
            dest[here, 256 + 128 * tile : 384 + 128 * tile] = middle.astype(jnp.bfloat16)
            dest[here, 512 + 128 * tile : 640 + 128 * tile] = above.astype(jnp.bfloat16)


def wgrad_step(width, side, glob_ref, refs):
    g_refs, h_refs, p_refs = refs[:3], refs[3:6], refs[6:9]
    mask_ref, out_ref, source, grad, cols, lines = refs[9], *refs[-5:]
    rows = h_refs[0].shape[0]
    block = pl.program_id(0) + glob_ref[1]
    _, skip = place_of(block, width)
    starts = list(chunks(rows))
    fill_act(h_refs, p_refs, skip, width, starts, source)
    fill_grad(g_refs, skip, width, starts, grad)
    stack(source, mask_ref, 0, 1, 1, starts, cols)
    stack_lines(grad, mask_ref, side, starts, lines)
    gw = width // PACK
    lanes = lax.broadcasted_iota(jnp.int32, (gw, 256), 1)
    for dx in range(3):
        acc = lax.dot_general(
            cols[:, 256 * dx : 256 * dx + 256],
            lines[...],
            (((0,), (0,)), ((), ())),
            preferred_element_type=jnp.float32,
        )
        for dy in range(3):
            small = jnp.zeros((gw, 256), jnp.float32)
            for g in range(PACK):
                piece = acc[gw * g : gw * g + gw, 256 * dy : 256 * dy + 256]
                small = jnp.where((lanes >= gw * g) & (lanes < gw * g + gw), piece, small)
            out_ref[3 * dy + dx, 0] = small


def conv_kernel(step, tall, width, sides, glob_ref, *refs):
    for ref in refs:
        if ref.shape[0] == tall:
            clear_edges(ref)
    for flag, side in ((1, sides[0]), (0, sides[1])):

        @pl.when(glob_ref[0] == flag)
        def _(side=side):
            step(width, side, glob_ref, refs)


def pack_kernel(gw, k_ref, out_ref):
    width = PACK * gw
    lane = lax.broadcasted_iota(jnp.int32, (gw, 256), 1)
    row = lax.broadcasted_iota(jnp.int32, (gw, 256), 0)
    spread = jnp.zeros((gw, 256), jnp.float32)
    for g in range(PACK):
        spread = jnp.where(lane == row + gw * g, 1.0, spread)
    spread = spread.astype(jnp.bfloat16)
    lane = lax.broadcasted_iota(jnp.int32, (width, 256), 1)
    row = lax.broadcasted_iota(jnp.int32, (width, 256), 0)
    inside = lane < 0
    for g in range(PACK):
        low, high = gw * g, gw * g + gw
        inside = inside | ((lane >= low) & (lane < high) & (row >= low) & (row < high))
    rest = jnp.zeros((256 - width, 256), jnp.float32)
    for dy in range(3):
        for dx in range(3):
            tap = k_ref[3 * dy + dx].astype(jnp.float32).reshape(width, gw).astype(jnp.bfloat16)
            wide = jnp.dot(tap, spread, preferred_element_type=jnp.float32)
            out_ref[0, 256 * dx : 256 * dx + 256, 256 * dy : 256 * dy + 256] = jnp.concatenate(
                [jnp.where(inside, wide, 0.0), rest], axis=0
            ).astype(jnp.bfloat16)


def pack_blocks(first, count, kernel, done=None):
    taps, groups, gw, _ = kernel.shape
    given = () if done is None else (done,)

    def body(k_ref, *refs):
        pack_kernel(gw, k_ref, refs[-1])

    return pl.pallas_call(
        body,
        grid=(count,),
        in_specs=[pl.BlockSpec((taps, PACK, gw, gw), lambda b: (0, b + first, 0, 0))]
        + [pl.BlockSpec(memory_space=pl.ANY)] * len(given),
        out_specs=pl.BlockSpec((1, 768, 768), lambda b: (b + first, 0, 0)),
        out_shape=jax.ShapeDtypeStruct((groups // PACK, 768, 768), jnp.bfloat16),
        input_output_aliases={1: 0} if given else {},
        compiler_params=params(),
        cost_estimate=cost(3),
        name="pack",
    )(kernel, *given)


def tile_specs(rows, width, chans, first=0):
    def spec(j):
        last = -(-chans // 128) - 1
        return pl.BlockSpec(
            (rows, 128), lambda b, s: (0, jnp.minimum((b + first) * width // 128 + j, last))
        )

    return [spec(j) for j in range(3)]


def conv_specs(rows):
    whole = lambda r: pl.BlockSpec((r, 2048), lambda b, s: (0, 0))
    mask = pl.BlockSpec((4, rows, 128), lambda b, s: (0, 0, 0))
    kern = pl.BlockSpec((1, 768, 768), lambda b, s: (b, 0, 0))
    return whole, mask, kern


def conv_scratch(rows, count):
    tall = rows + 2 * EDGE
    return [pltpu.VMEM((tall, 256), jnp.float32)] + [pltpu.VMEM((rows, 768), jnp.bfloat16)] * count


def conv_fwd(glob, h, par, masks, packed, width, sides):
    rows, chans = h.shape
    whole, mask, kern = conv_specs(rows)
    tiles = functools.partial(tile_specs, width=width, chans=chans)
    return pl.pallas_call(
        functools.partial(conv_kernel, fwd_step, rows + 2 * EDGE, width, sides),
        grid_spec=pltpu.PrefetchScalarGridSpec(
            num_scalar_prefetch=1,
            grid=(packed.shape[0],),
            in_specs=tiles(rows) + tiles(8) + [mask, kern],
            out_specs=[whole(rows), whole(8)],
            scratch_shapes=conv_scratch(rows, 1) + [pltpu.VMEM((rows + 2 * EDGE, 768), jnp.float32)],
        ),
        out_shape=[
            jax.ShapeDtypeStruct((rows, chans), jnp.float32),
            jax.ShapeDtypeStruct((8, chans), jnp.float32),
        ],
        compiler_params=params(),
        cost_estimate=cost(20),
        name="conv_fwd",
    )(glob, h, h, h, par, par, par, masks, packed)


def conv_dgrad(glob, grad, h, par, masks, packed, width, sides):
    rows, chans = h.shape
    whole, mask, kern = conv_specs(rows)
    tiles = functools.partial(tile_specs, width=width, chans=chans)
    return pl.pallas_call(
        functools.partial(conv_kernel, dgrad_step, rows + 2 * EDGE, width, sides),
        grid_spec=pltpu.PrefetchScalarGridSpec(
            num_scalar_prefetch=1,
            grid=(packed.shape[0],),
            in_specs=tiles(rows) + tiles(rows) + tiles(8) + [mask, kern],
            out_specs=[whole(rows), whole(8)],
            scratch_shapes=conv_scratch(rows, 1) + [pltpu.VMEM((rows + 2 * EDGE, 768), jnp.float32)],
        ),
        out_shape=[
            jax.ShapeDtypeStruct((rows, chans), jnp.float32),
            jax.ShapeDtypeStruct((8, chans), jnp.float32),
        ],
        compiler_params=params(),
        cost_estimate=cost(20),
        name="conv_dgrad",
    )(glob, grad, grad, grad, h, h, h, par, par, par, masks, packed)


def conv_wgrad(glob, grad, h, par, masks, first, count, blocks, width, sides, done=None):
    rows, chans = h.shape
    whole, mask, kern = conv_specs(rows)
    tiles = functools.partial(tile_specs, width=width, chans=chans, first=first)
    gw = width // PACK
    given = () if done is None else (done,)
    return pl.pallas_call(
        functools.partial(conv_kernel, wgrad_step, rows + 2 * EDGE, width, sides),
        grid_spec=pltpu.PrefetchScalarGridSpec(
            num_scalar_prefetch=1,
            grid=(count,),
            in_specs=tiles(rows) + tiles(rows) + tiles(8) + [mask]
            + [pl.BlockSpec(memory_space=pl.ANY)] * len(given),
            out_specs=pl.BlockSpec((9, 1, gw, 256), lambda b, s: (0, b + first, 0, 0)),
            scratch_shapes=conv_scratch(rows, 0) + conv_scratch(rows, 2),
        ),
        out_shape=jax.ShapeDtypeStruct((9, blocks, gw, 256), jnp.float32),
        input_output_aliases={11: 0} if given else {},
        compiler_params=params(),
        cost_estimate=cost(2 * count),
        name="conv_wgrad",
    )(
        jnp.concatenate([glob, jnp.full((1,), first, jnp.int32)]),
        grad,
        grad,
        grad,
        h,
        h,
        h,
        par,
        par,
        par,
        masks,
        *given,
    )


from jax.experimental.layout import Layout, with_layout_constraint
from jax.sharding import PartitionSpec as P

IMG_DEV = 4
SIDE = 14
SMALL_SIDE = 7
LOW_COLUMNS = 0
TAIL = (0, 1, 2, 0, 2, 1, 0, 2, 0, 2, 1, 2, 0, 2)
WIDE = 2048
WIDE_PROTOS = 3072

norm_epsilon = 1e-05
length_epsilon = 1e-06
sharpening_divisor = 0.1
sharpness = 0.05
exact_mode = lax.Precision.HIGHEST


def plain(value):
    return with_layout_constraint(value, Layout(major_to_minor=tuple(range(value.ndim))))


def swap(value, axis, mask):
    pairs = [(source, source ^ mask) for source in range(lax.axis_size(axis))]
    if value.ndim < 3:
        return lax.ppermute(value, axis, pairs)
    return plain(lax.ppermute(plain(value), axis, pairs))


def tie(*values):
    return lax.optimization_barrier(values)


def smooth_gate(values):
    return values * jax.nn.sigmoid(values)


def smooth_slope(values):
    sigma_values = jax.nn.sigmoid(values)
    return sigma_values * (1.0 + values * (1.0 - sigma_values))


def exact_dot(left, right):
    return jnp.dot(left, right, precision=exact_mode, preferred_element_type=jnp.float32)


def spread_dot(member_rows, values):
    terms, rest = [], values
    for _ in range(3):
        term = lax.reduce_precision(rest, 8, 7)
        terms.append(term.astype(jnp.bfloat16))
        rest = rest - term
    return jnp.dot(
        jnp.concatenate([member_rows] * 3, axis=1),
        jnp.concatenate(terms, axis=0),
        preferred_element_type=jnp.float32,
    )


def pool_dot(member, values):
    return jnp.dot(member, values.astype(jnp.bfloat16), preferred_element_type=jnp.float32)


def bits_of(size):
    return [1 << bit for bit in range(size.bit_length() - 1)]


def stream_sum(value, work=(), inputs=()):
    made = []
    if work:
        value, inputs = tie(value, inputs)
    for k, mask in enumerate([0] + bits_of(lax.axis_size("img"))):
        other = swap(value, "img", mask) if mask else swap(value, "crop", 1)
        if k < len(work):
            made.append(work[k](*inputs, *made[-1:]))
            value, other, inputs, made[-1] = tie(value, other, inputs, made[-1])
        value = value + other
    return value, made


def quarters(blocks):
    cuts = [blocks * i // 4 for i in range(5)]
    return [(low, high - low) for low, high in zip(cuts, cuts[1:])]


def pick(value, index, axis):
    return lax.dynamic_index_in_dim(value, index, axis, keepdims=False)


def slab_rows(width, devices):
    return -(-(width // devices) // 8) * 8


def slab_offset(index, width, devices):
    share = width // devices
    return 2 * share * (index // 2) + (index % 2) * (2 * share - slab_rows(width, devices))


def slab_part(devices, width, height, place_ref, left_ref, right_ref):
    step = pl.program_id(0)
    half = devices // 4
    apart = jnp.where(step < half, 2 * step, 2 * (step - half) + 1)
    index = 2 * (apart ^ place_ref[1]) + place_ref[0]
    offset = slab_offset(index, width, devices)
    base = jnp.minimum(offset // 128, left_ref.shape[1] // 128 - 3) * 128
    wide = left_ref[:, pl.ds(pl.multiple_of(base, 128), 384)].astype(jnp.float32)
    shift = offset - base
    moved = pltpu.roll(wide, jnp.where(shift == 0, 0, 384 - shift), 1)[:, :height]
    return lax.dot_general(
        moved.astype(jnp.bfloat16),
        right_ref[...],
        (((0,), (0,)), ((), ())),
        preferred_element_type=jnp.float32,
    )


def far_kernel(devices, width, height, low, place_ref, left_ref, right_ref, *refs):
    acc = slab_part(devices, width, height, place_ref, left_ref, right_ref)
    if low:
        refs[0][0] = acc[:, :low]
    refs[-1][0] = acc[:, low:]


def near_kernel(devices, width, height, low, place_ref, left_ref, right_ref, *refs):
    held = refs[-1]
    keep_x, send_x, keep_y, send_y = refs[-5:-1]
    acc = slab_part(devices, width, height, place_ref, left_ref, right_ref)
    step = pl.program_id(0)
    if low:
        low_in, high_in, keep_low, send_low = refs[:4]
        total = acc[:, :low] + low_in[0]

        @pl.when(step < devices // 4)
        def _():
            keep_low[0] = total

        @pl.when(step >= devices // 4)
        def _():
            send_low[0] = total

    else:
        high_in = refs[0]
    held[...] = acc[:, low:] + high_in[0]
    rows = height // 8
    bits = (place_ref[2], place_ref[3])
    for half, keep, send in ((0, keep_x, send_x), (1, keep_y, send_y)):
        first, second = bits[half], bits[1 - half]
        for other, ref in ((0, keep), (1, send)):
            for last in range(2):
                block = 4 * half + 2 * (first ^ other) + (second ^ last)
                ref[last, 0] = held[pl.ds(pl.multiple_of(block * rows, rows), rows), :]


def slab_specs(devices, rows, height, low):
    sides = [pl.BlockSpec((rows, WIDE), lambda t, c: (0, 0))] * 2
    widths = [low, WIDE - low] if low else [WIDE]
    parts = [pl.BlockSpec((1, height, n), lambda t, c: (t, 0, 0)) for n in widths]
    shapes = [jax.ShapeDtypeStruct((devices // 2, height, n), jnp.float32) for n in widths]
    return sides, parts, shapes


def far_product(place, left, right, devices, low):
    rows, width = left.shape
    height = slab_rows(width, devices)
    sides, parts, shapes = slab_specs(devices, rows, height, low)
    return pl.pallas_call(
        functools.partial(far_kernel, devices, width, height, low),
        grid_spec=pltpu.PrefetchScalarGridSpec(
            num_scalar_prefetch=1, grid=(devices // 2,), in_specs=sides, out_specs=parts
        ),
        out_shape=shapes,
        compiler_params=pltpu.CompilerParams(vmem_limit_bytes=40 * 1024 * 1024),
        cost_estimate=cost(9),
        name="far_product",
    )(place, left, right)


def near_product(place, left, right, devices, low, arrived):
    rows, width = left.shape
    height = slab_rows(width, devices)
    sides, parts, _ = slab_specs(devices, rows, height, low)
    chips, half = devices // 2, devices // 4
    high = WIDE - low
    piece = pl.BlockSpec((2, 1, height // 8, high), lambda t, c: (0, t, 0, 0))
    out_specs = [piece] * 4
    out_shape = [jax.ShapeDtypeStruct((2, chips, height // 8, high), jnp.float32)] * 4
    if low:
        out_specs = [
            pl.BlockSpec((1, height, low), lambda t, c: (jnp.minimum(t, half - 1), 0, 0)),
            pl.BlockSpec((1, height, low), lambda t, c: (jnp.maximum(t - half, 0), 0, 0)),
        ] + out_specs
        out_shape = [jax.ShapeDtypeStruct((half, height, low), jnp.float32)] * 2 + out_shape
    return pl.pallas_call(
        functools.partial(near_kernel, devices, width, height, low),
        grid_spec=pltpu.PrefetchScalarGridSpec(
            num_scalar_prefetch=1,
            grid=(chips,),
            in_specs=sides + parts,
            out_specs=out_specs,
            scratch_shapes=[pltpu.VMEM((height, high), jnp.float32)],
        ),
        out_shape=out_shape,
        compiler_params=pltpu.CompilerParams(vmem_limit_bytes=48 * 1024 * 1024),
        cost_estimate=cost(13),
        name="near_product",
    )(place, left, right, *arrived)


UNIT_ROWS = 704


def unit_start(index, share, unit, gw, rows):
    return jnp.minimum((share * index // unit) * gw, rows - UNIT_ROWS)


def unit_part(devices, size, gw, place_ref, units_ref):
    step = pl.program_id(0)
    half = devices // 4
    apart = jnp.where(step < half, 2 * step, 2 * (step - half) + 1)
    index = 2 * (apart ^ place_ref[1]) + place_ref[0]
    start = unit_start(index, size // devices, gw * gw * PACK, gw, units_ref.shape[0])
    return pl.multiple_of(start, 8)


def far_units_kernel(devices, size, gw, place_ref, units_ref, out_ref):
    start = unit_part(devices, size, gw, place_ref, units_ref)
    out_ref[0] = units_ref[pl.ds(start, UNIT_ROWS), :]


def near_units_kernel(devices, size, gw, place_ref, units_ref, in_ref, *refs):
    keep_x, send_x, keep_y, send_y = refs
    start = unit_part(devices, size, gw, place_ref, units_ref)
    rows = UNIT_ROWS // 8
    bits = (place_ref[2], place_ref[3])
    for half, keep, send in ((0, keep_x, send_x), (1, keep_y, send_y)):
        first, second = bits[half], bits[1 - half]
        for other, ref in ((0, keep), (1, send)):
            for last in range(2):
                block = 4 * half + 2 * (first ^ other) + (second ^ last)
                skip = pl.multiple_of(block * rows, 8)
                ref[last, 0] = (
                    units_ref[pl.ds(pl.multiple_of(start + skip, 8), rows), :]
                    + in_ref[0, pl.ds(skip, rows), :]
                )


def unit_call(place, units, devices, size, gw, arrived=None):
    rows = units.shape[0]
    chips = devices // 2
    part = pl.BlockSpec((1, UNIT_ROWS, 256), lambda t, c: (t, 0, 0))
    if arrived is None:
        body, extra = far_units_kernel, ()
        out_specs, out_shape = part, jax.ShapeDtypeStruct((chips, UNIT_ROWS, 256), jnp.float32)
    else:
        body, extra = near_units_kernel, (arrived,)
        piece = (2, chips, UNIT_ROWS // 8, 256)
        out_specs = [pl.BlockSpec((2, 1) + piece[2:], lambda t, c: (0, t, 0, 0))] * 4
        out_shape = [jax.ShapeDtypeStruct(piece, jnp.float32)] * 4
    return pl.pallas_call(
        functools.partial(body, devices, size, gw),
        grid_spec=pltpu.PrefetchScalarGridSpec(
            num_scalar_prefetch=1,
            grid=(chips,),
            in_specs=[pl.BlockSpec((rows, 256), lambda t, c: (0, 0))] + [part] * len(extra),
            out_specs=out_specs,
        ),
        out_shape=out_shape,
        compiler_params=pltpu.CompilerParams(vmem_limit_bytes=32 * 1024 * 1024),
        cost_estimate=cost(3),
        name="units",
    )(place, units, *extra)


def share_kernel(left_ref, right_ref, out_ref):
    out_ref[...] = lax.dot_general(
        left_ref[...].astype(jnp.bfloat16),
        right_ref[...].astype(jnp.bfloat16),
        (((0,), (0,)), ((), ())),
        preferred_element_type=jnp.float32,
    )


def share_product(left, right):
    return pl.pallas_call(
        share_kernel,
        out_shape=jax.ShapeDtypeStruct((left.shape[1], right.shape[1]), jnp.float32),
        compiler_params=pltpu.CompilerParams(vmem_limit_bytes=32 * 1024 * 1024),
        cost_estimate=cost(3),
        name="share_product",
    )(left, right)


def crop_bits():
    crop = lax.axis_index("crop")
    return (crop & 1, crop >> 1)


def crop_halves(value):
    lead, rows, cols = value.shape
    whole = value.reshape(lead, 2, 2, 2, rows // 8, cols)
    return [whole[:, 0], whole[:, 1]]


CROP_ORDER = ((0, 1), (1, 0))


def crop_send(parts, step):
    bits = crop_bits()
    return [
        swap(pick(part, 1 - bits[order[step]], 1), "crop", 1 << order[step])
        for part, order in zip(parts, CROP_ORDER)
    ]


def crop_add(parts, arrived, step):
    bits = crop_bits()
    return [
        pick(part, bits[order[step]], 1) + other
        for part, other, order in zip(parts, arrived, CROP_ORDER)
    ]


def crop_fetch(parts, step):
    return [swap(part, "crop", 1 << order[1 - step]) for part, order in zip(parts, CROP_ORDER)]


def crop_join(parts, arrived, step):
    bits = crop_bits()
    joined = []
    for part, other, order in zip(parts, arrived, CROP_ORDER):
        upper = bits[order[1 - step]] == 1
        joined.append(
            jnp.stack([jnp.where(upper, other, part), jnp.where(upper, part, other)], axis=1)
        )
    return joined


def crop_whole(parts):
    both = jnp.stack(parts, axis=1)
    return both.reshape(both.shape[0], -1, both.shape[-1])


def chip_swap(value, step):
    return swap(value, "img", 2 << step)


class LowChain:
    def __init__(self, keep, send):
        self.keep, self.away = keep, [send]
        self.chips = keep.shape[0].bit_length()
        self.steps, self.step = self.chips + 4, 0

    def send(self):
        if self.step < self.chips:
            return [chip_swap(v, self.step) for v in self.away]
        if self.step < self.chips + 2:
            return crop_send(self.keep, self.step - self.chips)
        return crop_fetch(self.keep, self.step - self.chips - 2)

    def take(self, arrived):
        step, chips = self.step, self.chips
        if step < chips:
            total = self.keep + arrived[0]
            half = total.shape[0] // 2
            self.keep, self.away = total[:half], [total[half:]]
            if step == chips - 1:
                self.keep, self.away = crop_halves(total), []
        elif step < chips + 2:
            self.keep = crop_add(self.keep, arrived, step - chips)
        else:
            self.keep = crop_join(self.keep, arrived, step - chips - 2)
        self.step += 1

    def result(self):
        return crop_whole(self.keep)[0]


class HighChain:
    def __init__(self, keep_x, send_x, keep_y, send_y):
        self.keep, self.away = [keep_x, keep_y], [send_x, send_y]
        self.chips = keep_x.shape[1].bit_length() - 1
        self.steps, self.step = self.chips + 4, 0

    def send(self):
        step = self.step
        if step < 2:
            return [swap(v, "crop", 1 << order[step]) for v, order in zip(self.away, CROP_ORDER)]
        if step < self.chips + 2:
            return [chip_swap(v, step - 2) for v in self.away]
        return crop_fetch(self.keep, step - self.chips - 2)

    def take(self, arrived):
        step, chips = self.step, self.chips
        if step < chips + 2:
            total = [keep + other for keep, other in zip(self.keep, arrived)]
            if step == 0:
                self.keep, self.away = [v[0] for v in total], [v[1] for v in total]
            else:
                if step == 1:
                    total = [jnp.concatenate(total, axis=1)]
                half = total[0].shape[0] // 2
                self.keep, self.away = [total[0][:half]], [total[0][half:]]
            if step == chips + 1:
                rows = total[0].shape[1] // 2
                self.keep, self.away = [total[0][:, :rows], total[0][:, rows:]], []
        else:
            self.keep = crop_join(self.keep, arrived, step - chips - 2)
        self.step += 1

    def result(self):
        return crop_whole(self.keep)[0]


class CropSum:
    steps = 4

    def __init__(self, value):
        self.away = []
        self.keep = crop_halves(value[None])
        self.step = 0

    def send(self):
        if self.step < 2:
            return crop_send(self.keep, self.step)
        return crop_fetch(self.keep, self.step - 2)

    def take(self, arrived):
        if self.step < 2:
            self.keep = crop_add(self.keep, arrived, self.step)
        else:
            self.keep = crop_join(self.keep, arrived, self.step - 2)
        self.step += 1

    def result(self):
        return crop_whole(self.keep)[0]


class Flow:
    def __init__(self):
        self.sent = {}

    def begin(self, chain):
        self.sent[id(chain)] = chain.send()

    def advance(self, chain, beside):
        arrived, beside = tie(self.sent[id(chain)], beside)
        chain.take(arrived)
        (chain.keep, chain.away), beside = tie((chain.keep, chain.away), beside)
        if chain.step < chain.steps:
            self.begin(chain)
        return beside


def shards(
    pixels,
    counts,
    slot_order,
    w_in,
    kernel,
    w_red,
    b_red,
    w_exp,
    b_exp,
    w_out,
    gain_one,
    shift_one,
    gain_two,
    shift_two,
    gain_three,
    shift_three,
    protos,
):
    row_count = pixels.shape[2]
    width = pixels.shape[3]
    proto_count = protos.shape[1]
    squeeze = w_red.shape[1]
    seg_count = row_count // (SMALL_SIDE * SMALL_SIDE)
    slot_total = slot_order.shape[1]
    devices = lax.axis_size("img")
    img_index = lax.axis_index("img")
    crop_index = lax.axis_index("crop")
    core = img_index % 2
    fast = width % devices == 0 and (2 * width // devices) % 8 == 0
    is_global = crop_index < 2
    glob = is_global.astype(jnp.int32).reshape(1)
    stream_rows = 2.0 * devices * row_count
    couple_number = 2.0 * devices * (IMG_DEV + slot_total)
    inputs = pixels.reshape(row_count, width)
    row_ids = jnp.arange(row_count, dtype=jnp.int32)
    side = jnp.where(is_global, SIDE, SMALL_SIDE)
    seg_of_row = row_ids // (side * side)
    across = row_ids % side
    down = (row_ids // side) % side
    masks = jnp.stack([across > 0, across < side - 1, down > 0, down < side - 1])
    masks = jnp.broadcast_to(masks.astype(jnp.float32)[:, :, None], (4, row_count, 128))
    member = (seg_of_row[None, :] == jnp.arange(seg_count, dtype=jnp.int32)[:, None]).astype(
        jnp.bfloat16
    )
    member_rows = member.T
    crop_pixels = jnp.where(is_global, float(SIDE * SIDE), float(SMALL_SIDE * SMALL_SIDE))
    block_width = PACK * kernel.shape[2]
    block_count = kernel.shape[1] // PACK
    sides = (SIDE, SMALL_SIDE)

    def norm_rows(local_sums, work=(), inputs=()):
        sums, made = stream_sum(local_sums, work, inputs)
        average = sums[0] / stream_rows
        inv = lax.rsqrt(sums[1] / stream_rows - average * average + norm_epsilon)
        return average, inv, made

    def back_rows(local_sums, gain, inv, work=(), inputs=()):
        sums, made = stream_sum(local_sums, work, inputs)
        return sums, gain * inv, sums[0] / stream_rows, sums[1] / stream_rows, made

    hidden_one = jnp.dot(inputs, w_in, preferred_element_type=jnp.float32)
    sums = jnp.stack([jnp.sum(hidden_one, axis=0), jnp.sum(hidden_one * hidden_one, axis=0)])
    mean_one, inv_one, packed = norm_rows(
        sums,
        [functools.partial(pack_blocks, low, count) for low, count in quarters(block_count)],
        (kernel,),
    )
    packed = packed[-1]
    zero_row = jnp.zeros((width,), jnp.float32)
    scale_one = gain_one * inv_one
    par = jnp.stack(
        [scale_one, shift_one - mean_one * scale_one, inv_one, -mean_one * inv_one] + [zero_row] * 4
    )
    hidden_two, sums = conv_fwd(glob, hidden_one, par, masks, packed, block_width, sides)
    mean_two, inv_two, _ = norm_rows(sums[:2])
    centred_two = (hidden_two - mean_two) * inv_two
    pre_two = centred_two * gain_two + shift_two
    act_two = smooth_gate(pre_two)
    red_float = w_red.astype(jnp.float32)
    exp_float = w_exp.astype(jnp.float32)
    pooled = pool_dot(member, act_two) / crop_pixels
    reduce_pre = exact_dot(pooled, red_float) + b_red
    reduced = smooth_gate(reduce_pre)
    gate_values = jax.nn.sigmoid(exact_dot(reduced, exp_float) + b_exp)
    gate_rows = spread_dot(member_rows, gate_values)
    excited = (act_two * gate_rows).astype(jnp.bfloat16)
    hidden_three = jnp.dot(excited, w_out, preferred_element_type=jnp.float32)
    sums = jnp.stack([jnp.sum(hidden_three, axis=0), jnp.sum(hidden_three * hidden_three, axis=0)])
    mean_three, inv_three, _ = norm_rows(sums)
    centred_three = (hidden_three - mean_three) * inv_three
    summed_in = inputs.astype(jnp.float32) + centred_three * gain_three + shift_three
    output = smooth_gate(summed_in)
    pooled_out = (
        jnp.dot(
            member.astype(jnp.float32),
            output,
            precision=lax.Precision.HIGH,
            preferred_element_type=jnp.float32,
        )
        / crop_pixels
    )
    length_inv = lax.rsqrt(jnp.sum(pooled_out * pooled_out, axis=1, keepdims=True) + length_epsilon)
    unit_wide = pooled_out * length_inv
    unit_rows = unit_wide.astype(jnp.bfloat16)
    match_matrix = jnp.dot(unit_rows, protos, preferred_element_type=jnp.float32)

    every = match_matrix[:IMG_DEV]
    for mask in bits_of(devices):
        every = jnp.concatenate([every, swap(every, "img", mask)], axis=0)
    plan_rows = jnp.exp(every / sharpness)
    for sweep_index in range(3):
        plan_rows = plan_rows / jnp.sum(plan_rows, axis=0, keepdims=True)
        plan_rows = plan_rows / jnp.sum(plan_rows, axis=1, keepdims=True)
    codes = plan_rows[:IMG_DEV]
    partner = lax.ppermute(codes, "crop", [(0, 1), (1, 0)])
    both_codes = lax.ppermute(codes, "crop", [(0, 2), (1, 3)]) + lax.ppermute(
        codes, "crop", [(0, 3), (1, 2)]
    )
    wide_target = jnp.concatenate(
        [partner, jnp.zeros((seg_count - IMG_DEV, proto_count), jnp.float32)], axis=0
    )
    ends = [jnp.sum(counts[0, : i + 1]) for i in range(IMG_DEV)]
    first_slot = jnp.maximum(crop_index - 2, 0) * seg_count
    order_here = lax.dynamic_slice_in_dim(slot_order[0], first_slot, seg_count)
    owner = sum((order_here >= end).astype(jnp.int32) for end in ends)
    narrow_target = jnp.zeros((seg_count, proto_count), jnp.float32)
    for i in range(IMG_DEV):
        narrow_target = jnp.where(owner[:, None] == i, both_codes[i : i + 1], narrow_target)
    target = jnp.where(is_global, wide_target, narrow_target)
    sharpened = match_matrix / sharpening_divisor
    shifted = sharpened - jnp.max(sharpened, axis=1, keepdims=True)
    log_probs = shifted - jnp.log(jnp.sum(jnp.exp(shifted), axis=1, keepdims=True))
    loss_here = -jnp.sum(target * log_probs) / couple_number
    scores_wide = (jnp.exp(log_probs) * jnp.sum(target, axis=1, keepdims=True) - target) / (
        sharpening_divisor * couple_number
    )
    grad_scores = scores_wide.astype(jnp.bfloat16)

    grad_unit = jnp.einsum("sk,wk->sw", grad_scores, protos, preferred_element_type=jnp.float32)
    inner_term = jnp.sum(pooled_out * grad_unit, axis=1, keepdims=True)
    grad_pooled_out = (
        length_inv * grad_unit - pooled_out * length_inv * length_inv * length_inv * inner_term
    )
    grad_output = spread_dot(member_rows, grad_pooled_out / crop_pixels)
    grad_summed = grad_output * smooth_slope(summed_in)
    sums_three, scale_three, first, second, _ = back_rows(
        jnp.stack([jnp.sum(grad_summed, axis=0), jnp.sum(grad_summed * centred_three, axis=0)]),
        gain_three,
        inv_three,
    )
    grad_three_low = (scale_three * (grad_summed - first - centred_three * second)).astype(
        jnp.bfloat16
    )
    if fast:
        share = width // devices
        height = slab_rows(width, devices)
        chip = img_index // 2
        near = jnp.stack([core, chip, crop_index & 1, crop_index >> 1]).astype(jnp.int32)
        far = jnp.stack([1 - core, chip, crop_index & 1, crop_index >> 1]).astype(jnp.int32)

        def kept(value):
            skip = core * (value.shape[0] - share)
            return lax.dynamic_slice_in_dim(value, skip, share, axis=0)

        seen_scores = lax.all_gather(
            jnp.concatenate(
                [
                    unit_wide,
                    jnp.zeros((seg_count, WIDE - width), jnp.float32),
                    scores_wide,
                    jnp.zeros((seg_count, WIDE_PROTOS - proto_count), jnp.float32),
                ],
                axis=1,
            ),
            "img",
            tiled=True,
        )

    grad_excited = jnp.einsum(
        "rv,wv->rw", grad_three_low, w_out, preferred_element_type=jnp.float32
    )
    flow = Flow()
    if fast:
        grad_excited, seen_scores = tie(grad_excited, seen_scores)
        protos_sum = CropSum(
            share_product(
                lax.dynamic_slice_in_dim(seen_scores, img_index * share, height, axis=1),
                seen_scores[:, WIDE:],
            )
        )
        (protos_sum.keep, grad_excited) = tie(protos_sum.keep, grad_excited)
        flow.begin(protos_sum)
    grad_gate = pool_dot(member, grad_excited * act_two)
    grad_gate_pre = grad_gate * gate_values * (1.0 - gate_values)
    grad_reduce_pre = exact_dot(grad_gate_pre, exp_float.T) * smooth_slope(reduce_pre)
    grad_pooled = exact_dot(grad_reduce_pre, red_float.T)
    grad_act_two = grad_excited * gate_rows + spread_dot(member_rows, grad_pooled / crop_pixels)
    grad_pre_two = grad_act_two * smooth_slope(pre_two)
    bias_row = jnp.concatenate(
        [
            jnp.sum(grad_reduce_pre, axis=0),
            loss_here.reshape(1),
            jnp.zeros((width - squeeze - 1,), jnp.float32),
        ]
    )
    local_two = jnp.stack(
        [
            jnp.sum(grad_pre_two, axis=0),
            jnp.sum(grad_pre_two * centred_two, axis=0),
            jnp.sum(grad_gate_pre, axis=0),
            bias_row,
        ]
    )
    work = []
    if fast:
        seen_gates = lax.all_gather(
            jnp.concatenate([pooled, reduced, grad_reduce_pre, grad_gate_pre], axis=1),
            "img",
            tiled=True,
        )

        def out_far(left, right):
            return far_product(far, left, right, devices, 0)

        def proto_step(left, right, arrived):
            return flow.advance(protos_sum, arrived)

        work = [out_far, proto_step]
    sums_two, scale_two, first, second, made = back_rows(
        local_two, gain_two, inv_two, work, (excited, grad_three_low)
    )
    if fast:
        arrived = [swap(v, "img", 1) for v in made[-1]]
    grad_two_low = (scale_two * (grad_pre_two - first - centred_two * second)).astype(jnp.bfloat16)
    if fast:
        grad_two_low, arrived = tie(grad_two_low, arrived)
        arrived = flow.advance(protos_sum, arrived)
        outs = HighChain(*near_product(near, excited, grad_three_low, devices, 0, arrived))
        outs.keep, outs.away, grad_two_low = tie(outs.keep, outs.away, grad_two_low)
        flow.begin(outs)
    grad_pre_one, sums = conv_dgrad(
        glob, grad_two_low, hidden_one, par, masks, packed, block_width, sides
    )

    def some_wgrad(low, count, grad, done=None):
        return conv_wgrad(
            glob, grad, hidden_one, par, masks, low, count, block_count, block_width, sides, done
        )

    cut = block_count // 2
    steps = [
        functools.partial(some_wgrad, 0, cut),
        functools.partial(some_wgrad, cut, block_count - cut),
    ]
    early = []
    if fast:
        grad_two_low, grad_pre_one, sums = tie(grad_two_low, grad_pre_one, sums)
        units = steps[0](grad_two_low)
        units = flow.advance(outs, units)
        units, sums = tie(units, sums)

        def my_columns(value):
            count = value.shape[1] // devices
            return lax.dynamic_slice_in_dim(value, img_index * count, count, axis=1)

        def shares_of(seen):
            seen = flow.advance(protos_sum, seen)
            return (
                exact_dot(
                    my_columns(seen[:, :width]).T, seen[:, width + squeeze : width + 2 * squeeze]
                ),
                exact_dot(my_columns(seen[:, width : width + squeeze]).T, seen[:, width + 2 * squeeze :]),
            )

        early = [shares_of]
    sums_one, scale_one, first, second, made = back_rows(
        sums[:2], gain_one, inv_one, early, (seen_gates,) if fast else ()
    )
    last = jnp.concatenate([sums_one, sums_two, sums_three], axis=0)
    last = last + swap(last, "crop", 2)
    centred_one = (hidden_one - mean_one) * inv_one
    grad_one_low = (scale_one * (grad_pre_one - first - centred_one * second)).astype(jnp.bfloat16)
    if fast:
        share_red, share_exp = made[-1]
        share_red, share_exp = lax.optimization_barrier(
            lax.psum((share_red, share_exp), "crop")
        )
        sent_far = far_product(far, inputs, grad_one_low, devices, LOW_COLUMNS)
        flow.sent[id(outs)], sent_far = tie(flow.sent[id(outs)], sent_far)
        outs.take(flow.sent[id(outs)])
        flow.begin(outs)
        arrived = [swap(v, "img", 1) for v in sent_far]
        last, arrived = tie(last, arrived)
        parts = near_product(near, inputs, grad_one_low, devices, LOW_COLUMNS, arrived)
        ins = HighChain(*parts)
        units, grad_two_low, grad_one_low, ins.keep, ins.away = tie(
            units, grad_two_low, grad_one_low, ins.keep, ins.away
        )
        flow.begin(ins)
        units = steps[1](grad_two_low, units)
        units = flow.advance(outs, units)
        units = flow.advance(protos_sum, units)
        gw = kernel.shape[2]
        unit_size = gw * gw * PACK
        units = units.reshape(-1, 256)
        swapped = unit_call(far, units, devices, kernel.size, gw)
        flat_protos = protos_sum.result()[:share, :proto_count].reshape(-1)
        swapped, units, grad_one_low, flat_protos = flow.advance(
            ins, (swapped, units, grad_one_low, flat_protos)
        )
        swapped = swap(swapped, "img", 1)
        grad_inputs = (
            jnp.einsum("rv,wv->rw", grad_one_low, w_in, preferred_element_type=jnp.float32)
            + grad_summed
        )
        swapped, grad_inputs = tie(swapped, grad_inputs)
        gks = HighChain(*unit_call(near, units, devices, kernel.size, gw, swapped))
        flow.begin(gks)
        chains = [ins, outs, gks]
        last_chain = None
        flat_out = None
        for chain in (chains[index] for index in TAIL):
            landed = flow.sent[id(chain)]
            if last_chain is not None:
                landed, _ = tie(landed, (last_chain.keep, last_chain.away))
            if chain is ins and chain.step == 5:
                flat_red = share_red.reshape(-1)
                flat_exp = share_exp.reshape(-1)
                landed, flat_out, flat_red, flat_exp = tie(landed, flat_out, flat_red, flat_exp)
            chain.take(landed)
            if chain.step < chain.steps:
                flow.begin(chain)
            if chain is ins and chain.step == 3:
                share_red, share_exp, _ = tie(share_red, share_exp, (ins.keep, ins.away))
            if chain is outs and chain.step == chain.steps:
                flat_out = kept(outs.result()[:, :width]).reshape(-1)
            last_chain = chain
    else:
        made = None
        for step in steps:
            made = step(grad_two_low, made)
        small_kernel = made
        grad_inputs = (
            jnp.einsum("rv,wv->rw", grad_one_low, w_in, preferred_element_type=jnp.float32)
            + grad_summed
        )

    if fast:
        flat_in = kept(ins.result()[:, :width]).reshape(-1)
        total = kernel.size // devices
        first_unit = total * img_index // unit_size
        start = unit_start(img_index, total, unit_size, gw, units.size // 256)
        span = -(-total // unit_size) + 1
        mine = jnp.pad(gks.result(), ((0, gw), (0, 0)))
        mine = lax.dynamic_slice_in_dim(mine, first_unit * gw - start, span * gw, axis=0)
        mine = mine[:, : PACK * gw].reshape(span, gw, PACK, gw).transpose(0, 2, 1, 3).reshape(-1)
        flat_kernel = lax.dynamic_slice_in_dim(mine, total * img_index - unit_size * first_unit, total)
        shares = (flat_in, flat_kernel, flat_red, flat_exp, flat_out, flat_protos)
    else:
        gw = kernel.shape[2]
        grads = (
            jnp.einsum("rw,rv->wv", inputs, grad_one_low, preferred_element_type=jnp.float32),
            small_kernel[..., : PACK * gw]
            .reshape(9, block_count, gw, PACK, gw)
            .transpose(0, 1, 3, 2, 4),
            exact_dot(pooled.T, grad_reduce_pre),
            exact_dot(reduced.T, grad_gate_pre),
            jnp.einsum("rw,rv->wv", excited, grad_three_low, preferred_element_type=jnp.float32),
            jnp.einsum("sw,sk->wk", unit_rows, grad_scores, preferred_element_type=jnp.float32),
        )
        shares = tuple(
            lax.psum(
                lax.psum_scatter(grad.reshape(-1), "img", scatter_dimension=0, tiled=True), "crop"
            )
            for grad in grads
        )
    tail = (
        last[5, :squeeze],
        last[4],
        last[1],
        last[0],
        last[3],
        last[2],
        last[7],
        last[6],
    )
    loss_total = last[5, squeeze]

    return (
        loss_total,
        output.astype(jnp.bfloat16).reshape(pixels.shape),
        grad_inputs.reshape(pixels.shape),
        *shares,
        *tail,
    )


def solution(mesh):
    return jax.shard_map(
        shards,
        mesh=mesh,
        in_specs=(P("crop", "img", None, None), P("img", None), P("img", None)) + (P(),) * 14,
        out_specs=(P(), P("crop", "img", None, None), P("crop", "img", None, None))
        + (P("img"),) * 6
        + (P(),) * 8,
        check_vma=False,
    )
```

```python
import functools
import jax
import jax.numpy as jnp
from jax import lax
from jax.experimental import pallas as pl
from jax.experimental.pallas import tpu as pltpu

VMEM_LIMIT = 56 * 1024 * 1024
PACK = 4
EDGE = 16
CHUNK = 112


def cost(micros):
    return pl.CostEstimate(flops=micros * 1000000, bytes_accessed=micros * 1000, transcendentals=0)


def params():
    return pltpu.CompilerParams(vmem_limit_bytes=VMEM_LIMIT)


def lane_of(rows):
    return lax.broadcasted_iota(jnp.int32, (rows, 128), 1)


def take(refs, start, rows, skip, width):
    a, b, c = [ref[start : start + rows, :].astype(jnp.float32) for ref in refs]
    back = lax.rem(128 - skip, 128)
    a, b, c = [pltpu.roll(v, back, 1) for v in (a, b, c)]
    lane = lane_of(rows)
    near = lane < 128 - skip
    return jnp.where(near, a, b), jnp.where(lane < width - 128, jnp.where(near, b, c), 0.0)


def put(ref, start, rows, base, skip, first, second):
    first, second = pltpu.roll(first, skip, 1), pltpu.roll(second, skip, 1)
    lane = lane_of(rows)
    inside = lane >= skip
    last = jnp.minimum(base + 2, ref.shape[1] // 128 - 1)

    def at(tile):
        return (slice(start, start + rows), pl.ds(pl.multiple_of(tile * 128, 128), 128))

    ref[at(last)] = second
    ref[at(base + 1)] = jnp.where(inside, second, first)
    ref[at(base)] = jnp.where(inside, first, ref[at(base)])


def place_of(block, width):
    start = block * width
    base = start // 128
    return base, start - base * 128


def clear_edges(ref):
    @pl.when(pl.program_id(0) == 0)
    def _():
        ref[0:EDGE, :] = jnp.zeros((EDGE, ref.shape[1]), ref.dtype)
        ref[ref.shape[0] - EDGE :, :] = jnp.zeros((EDGE, ref.shape[1]), ref.dtype)


def chunks(rows):
    return range(0, rows, CHUNK)


def fill_act(h_refs, p_refs, skip, width, starts, act):
    scale = take(p_refs, 0, 8, skip, width)
    for r in starts:
        for tile, h in enumerate(take(h_refs, r, CHUNK, skip, width)):
            pre = h * scale[tile][0:1] + scale[tile][1:2]
            value = pre * jax.nn.sigmoid(pre)
            act[EDGE + r : EDGE + r + CHUNK, 128 * tile : 128 * tile + 128] = value.astype(
                jnp.bfloat16
            ).astype(jnp.float32)


def fill_grad(g_refs, skip, width, starts, grad):
    for r in starts:
        for tile, g in enumerate(take(g_refs, r, CHUNK, skip, width)):
            grad[EDGE + r : EDGE + r + CHUNK, 128 * tile : 128 * tile + 128] = g


def stack(source, mask_ref, low, high, step, starts, dest):
    for r in starts:
        for tile in range(2):
            cols = slice(128 * tile, 128 * tile + 128)
            here = slice(r, r + CHUNK)
            before = source[EDGE + r - step : EDGE + r - step + CHUNK, cols] * mask_ref[low, here, :]
            after = source[EDGE + r + step : EDGE + r + step + CHUNK, cols] * mask_ref[high, here, :]
            middle = source[EDGE + r : EDGE + r + CHUNK, cols]
            dest[here, 128 * tile : 128 * tile + 128] = before.astype(jnp.bfloat16)
            dest[here, 256 + 128 * tile : 384 + 128 * tile] = middle.astype(jnp.bfloat16)
            dest[here, 512 + 128 * tile : 640 + 128 * tile] = after.astype(jnp.bfloat16)


def fwd_step(width, side, glob_ref, refs):
    h_refs, p_refs, (mask_ref, k_ref, out_ref, st_ref, act, cols, wide) = refs[:3], refs[3:6], refs[6:]
    rows = h_refs[0].shape[0]
    base, skip = place_of(pl.program_id(0), width)
    starts = list(chunks(rows))
    fill_act(h_refs, p_refs, skip, width, starts[:1], act)
    for i, r in enumerate(starts):
        fill_act(h_refs, p_refs, skip, width, starts[i + 1 : i + 2], act)
        stack(act, mask_ref, 0, 1, 1, [r], cols)
        wide[EDGE + r : EDGE + r + CHUNK, :] = jnp.dot(
            cols[r : r + CHUNK, :], k_ref[0], preferred_element_type=jnp.float32
        )
    sums = [jnp.zeros((8, 128), jnp.float32)] * 4
    for r in starts:
        here = slice(r, r + CHUNK)
        tiles = []
        for tile in range(2):
            lo = 128 * tile
            total = (
                wide[EDGE + r : EDGE + r + CHUNK, 256 + lo : 384 + lo]
                + wide[EDGE + r - side : EDGE + r - side + CHUNK, lo : 128 + lo] * mask_ref[2, here, :]
                + wide[EDGE + r + side : EDGE + r + side + CHUNK, 512 + lo : 640 + lo] * mask_ref[3, here, :]
            )
            tiles.append(total)
            sums[tile] += jnp.sum(total.reshape(-1, 8, 128), axis=0)
            sums[2 + tile] += jnp.sum((total * total).reshape(-1, 8, 128), axis=0)
        put(out_ref, r, CHUNK, base, skip, *tiles)
    put_sums(st_ref, base, skip, sums)


def put_sums(st_ref, base, skip, sums):
    line = lax.broadcasted_iota(jnp.int32, (8, 128), 0)
    tiles = [
        jnp.where(
            line == 0,
            jnp.sum(sums[tile], axis=0, keepdims=True),
            jnp.sum(sums[2 + tile], axis=0, keepdims=True),
        )
        for tile in range(2)
    ]
    put(st_ref, 0, 8, base, skip, *tiles)


def dgrad_step(width, side, glob_ref, refs):
    g_refs, h_refs, p_refs = refs[:3], refs[3:6], refs[6:9]
    mask_ref, k_ref, out_ref, st_ref, grad, lines, wide = refs[9:]
    rows = h_refs[0].shape[0]
    base, skip = place_of(pl.program_id(0), width)
    starts = list(chunks(rows))
    fill_grad(g_refs, skip, width, starts[:1], grad)
    for i, r in enumerate(starts):
        fill_grad(g_refs, skip, width, starts[i + 1 : i + 2], grad)
        stack_lines(grad, mask_ref, side, [r], lines)
    wide[EDGE : EDGE + rows, :] = lax.dot_general(
        lines[...], k_ref[0], (((1,), (1,)), ((), ())), preferred_element_type=jnp.float32
    )
    par = take(p_refs, 0, 8, skip, width)
    sums = [jnp.zeros((8, 128), jnp.float32)] * 4
    for r in starts:
        here = slice(r, r + CHUNK)
        h_tiles = take(h_refs, r, CHUNK, skip, width)
        tiles = []
        for tile in range(2):
            lo = 128 * tile
            total = (
                wide[EDGE + r : EDGE + r + CHUNK, 256 + lo : 384 + lo]
                + wide[EDGE + r + 1 : EDGE + r + 1 + CHUNK, lo : 128 + lo] * mask_ref[1, here, :]
                + wide[EDGE + r - 1 : EDGE + r - 1 + CHUNK, 512 + lo : 640 + lo] * mask_ref[0, here, :]
            )
            p = par[tile]
            pre = h_tiles[tile] * p[0:1] + p[1:2]
            sig = jax.nn.sigmoid(pre)
            ga = total * (sig * (1.0 + pre * (1.0 - sig)))
            xhat = h_tiles[tile] * p[2:3] + p[3:4]
            tiles.append(ga)
            sums[tile] += jnp.sum(ga.reshape(-1, 8, 128), axis=0)
            sums[2 + tile] += jnp.sum((ga * xhat).reshape(-1, 8, 128), axis=0)
        put(out_ref, r, CHUNK, base, skip, *tiles)
    put_sums(st_ref, base, skip, sums)


def stack_lines(grad, mask_ref, side, starts, dest):
    for r in starts:
        for tile in range(2):
            cols = slice(128 * tile, 128 * tile + 128)
            here = slice(r, r + CHUNK)
            below = grad[EDGE + r + side : EDGE + r + side + CHUNK, cols] * mask_ref[3, here, :]
            above = grad[EDGE + r - side : EDGE + r - side + CHUNK, cols] * mask_ref[2, here, :]
            middle = grad[EDGE + r : EDGE + r + CHUNK, cols]
            dest[here, 128 * tile : 128 * tile + 128] = below.astype(jnp.bfloat16)
            dest[here, 256 + 128 * tile : 384 + 128 * tile] = middle.astype(jnp.bfloat16)
            dest[here, 512 + 128 * tile : 640 + 128 * tile] = above.astype(jnp.bfloat16)


def wgrad_step(width, side, glob_ref, refs):
    g_refs, h_refs, p_refs = refs[:3], refs[3:6], refs[6:9]
    mask_ref, out_ref, source, grad, cols, lines = refs[9], *refs[-5:]
    rows = h_refs[0].shape[0]
    block = pl.program_id(0) + glob_ref[1]
    _, skip = place_of(block, width)
    starts = list(chunks(rows))
    fill_act(h_refs, p_refs, skip, width, starts, source)
    fill_grad(g_refs, skip, width, starts, grad)
    stack(source, mask_ref, 0, 1, 1, starts, cols)
    stack_lines(grad, mask_ref, side, starts, lines)
    gw = width // PACK
    lanes = lax.broadcasted_iota(jnp.int32, (gw, 256), 1)
    for dx in range(3):
        acc = lax.dot_general(
            cols[:, 256 * dx : 256 * dx + 256],
            lines[...],
            (((0,), (0,)), ((), ())),
            preferred_element_type=jnp.float32,
        )
        for dy in range(3):
            small = jnp.zeros((gw, 256), jnp.float32)
            for g in range(PACK):
                piece = acc[gw * g : gw * g + gw, 256 * dy : 256 * dy + 256]
                small = jnp.where((lanes >= gw * g) & (lanes < gw * g + gw), piece, small)
            out_ref[3 * dy + dx, 0] = small


def conv_kernel(step, tall, width, sides, glob_ref, *refs):
    for ref in refs:
        if ref.shape[0] == tall:
            clear_edges(ref)
    for flag, side in ((1, sides[0]), (0, sides[1])):

        @pl.when(glob_ref[0] == flag)
        def _(side=side):
            step(width, side, glob_ref, refs)


def pack_kernel(gw, k_ref, out_ref):
    width = PACK * gw
    lane = lax.broadcasted_iota(jnp.int32, (gw, 256), 1)
    row = lax.broadcasted_iota(jnp.int32, (gw, 256), 0)
    spread = jnp.zeros((gw, 256), jnp.float32)
    for g in range(PACK):
        spread = jnp.where(lane == row + gw * g, 1.0, spread)
    spread = spread.astype(jnp.bfloat16)
    lane = lax.broadcasted_iota(jnp.int32, (width, 256), 1)
    row = lax.broadcasted_iota(jnp.int32, (width, 256), 0)
    inside = lane < 0
    for g in range(PACK):
        low, high = gw * g, gw * g + gw
        inside = inside | ((lane >= low) & (lane < high) & (row >= low) & (row < high))
    rest = jnp.zeros((256 - width, 256), jnp.float32)
    for dy in range(3):
        for dx in range(3):
            tap = k_ref[3 * dy + dx].astype(jnp.float32).reshape(width, gw).astype(jnp.bfloat16)
            wide = jnp.dot(tap, spread, preferred_element_type=jnp.float32)
            out_ref[0, 256 * dx : 256 * dx + 256, 256 * dy : 256 * dy + 256] = jnp.concatenate(
                [jnp.where(inside, wide, 0.0), rest], axis=0
            ).astype(jnp.bfloat16)


def pack_blocks(first, count, kernel, done=None):
    taps, groups, gw, _ = kernel.shape
    given = () if done is None else (done,)

    def body(k_ref, *refs):
        pack_kernel(gw, k_ref, refs[-1])

    return pl.pallas_call(
        body,
        grid=(count,),
        in_specs=[pl.BlockSpec((taps, PACK, gw, gw), lambda b: (0, b + first, 0, 0))]
        + [pl.BlockSpec(memory_space=pl.ANY)] * len(given),
        out_specs=pl.BlockSpec((1, 768, 768), lambda b: (b + first, 0, 0)),
        out_shape=jax.ShapeDtypeStruct((groups // PACK, 768, 768), jnp.bfloat16),
        input_output_aliases={1: 0} if given else {},
        compiler_params=params(),
        cost_estimate=cost(3),
        name="pack",
    )(kernel, *given)


def tile_specs(rows, width, chans, first=0):
    def spec(j):
        last = -(-chans // 128) - 1
        return pl.BlockSpec(
            (rows, 128), lambda b, s: (0, jnp.minimum((b + first) * width // 128 + j, last))
        )

    return [spec(j) for j in range(3)]


def conv_specs(rows):
    whole = lambda r: pl.BlockSpec((r, 2048), lambda b, s: (0, 0))
    mask = pl.BlockSpec((4, rows, 128), lambda b, s: (0, 0, 0))
    kern = pl.BlockSpec((1, 768, 768), lambda b, s: (b, 0, 0))
    return whole, mask, kern


def conv_scratch(rows, count):
    tall = rows + 2 * EDGE
    return [pltpu.VMEM((tall, 256), jnp.float32)] + [pltpu.VMEM((rows, 768), jnp.bfloat16)] * count


def conv_fwd(glob, h, par, masks, packed, width, sides):
    rows, chans = h.shape
    whole, mask, kern = conv_specs(rows)
    tiles = functools.partial(tile_specs, width=width, chans=chans)
    return pl.pallas_call(
        functools.partial(conv_kernel, fwd_step, rows + 2 * EDGE, width, sides),
        grid_spec=pltpu.PrefetchScalarGridSpec(
            num_scalar_prefetch=1,
            grid=(packed.shape[0],),
            in_specs=tiles(rows) + tiles(8) + [mask, kern],
            out_specs=[whole(rows), whole(8)],
            scratch_shapes=conv_scratch(rows, 1) + [pltpu.VMEM((rows + 2 * EDGE, 768), jnp.float32)],
        ),
        out_shape=[
            jax.ShapeDtypeStruct((rows, chans), jnp.float32),
            jax.ShapeDtypeStruct((8, chans), jnp.float32),
        ],
        compiler_params=params(),
        cost_estimate=cost(20),
        name="conv_fwd",
    )(glob, h, h, h, par, par, par, masks, packed)


def conv_dgrad(glob, grad, h, par, masks, packed, width, sides):
    rows, chans = h.shape
    whole, mask, kern = conv_specs(rows)
    tiles = functools.partial(tile_specs, width=width, chans=chans)
    return pl.pallas_call(
        functools.partial(conv_kernel, dgrad_step, rows + 2 * EDGE, width, sides),
        grid_spec=pltpu.PrefetchScalarGridSpec(
            num_scalar_prefetch=1,
            grid=(packed.shape[0],),
            in_specs=tiles(rows) + tiles(rows) + tiles(8) + [mask, kern],
            out_specs=[whole(rows), whole(8)],
            scratch_shapes=conv_scratch(rows, 1) + [pltpu.VMEM((rows + 2 * EDGE, 768), jnp.float32)],
        ),
        out_shape=[
            jax.ShapeDtypeStruct((rows, chans), jnp.float32),
            jax.ShapeDtypeStruct((8, chans), jnp.float32),
        ],
        compiler_params=params(),
        cost_estimate=cost(20),
        name="conv_dgrad",
    )(glob, grad, grad, grad, h, h, h, par, par, par, masks, packed)


def conv_wgrad(glob, grad, h, par, masks, first, count, blocks, width, sides, done=None):
    rows, chans = h.shape
    whole, mask, kern = conv_specs(rows)
    tiles = functools.partial(tile_specs, width=width, chans=chans, first=first)
    gw = width // PACK
    given = () if done is None else (done,)
    return pl.pallas_call(
        functools.partial(conv_kernel, wgrad_step, rows + 2 * EDGE, width, sides),
        grid_spec=pltpu.PrefetchScalarGridSpec(
            num_scalar_prefetch=1,
            grid=(count,),
            in_specs=tiles(rows) + tiles(rows) + tiles(8) + [mask]
            + [pl.BlockSpec(memory_space=pl.ANY)] * len(given),
            out_specs=pl.BlockSpec((9, 1, gw, 256), lambda b, s: (0, b + first, 0, 0)),
            scratch_shapes=conv_scratch(rows, 0) + conv_scratch(rows, 2),
        ),
        out_shape=jax.ShapeDtypeStruct((9, blocks, gw, 256), jnp.float32),
        input_output_aliases={11: 0} if given else {},
        compiler_params=params(),
        cost_estimate=cost(2 * count),
        name="conv_wgrad",
    )(
        jnp.concatenate([glob, jnp.full((1,), first, jnp.int32)]),
        grad,
        grad,
        grad,
        h,
        h,
        h,
        par,
        par,
        par,
        masks,
        *given,
    )


from jax.experimental.layout import Layout, with_layout_constraint
from jax.sharding import PartitionSpec as P

IMG_DEV = 4
SIDE = 14
SMALL_SIDE = 7
LOW_COLUMNS = 0
TAIL = (0, 1, 2, 0, 2, 1, 0, 2, 0, 2, 1, 2, 0, 2)
WIDE = 2048
WIDE_PROTOS = 3072

norm_epsilon = 1e-05
length_epsilon = 1e-06
sharpening_divisor = 0.1
sharpness = 0.05
exact_mode = lax.Precision.HIGHEST


def plain(value):
    return with_layout_constraint(value, Layout(major_to_minor=tuple(range(value.ndim))))


def swap(value, axis, mask):
    pairs = [(source, source ^ mask) for source in range(lax.axis_size(axis))]
    if value.ndim < 3:
        return lax.ppermute(value, axis, pairs)
    return plain(lax.ppermute(plain(value), axis, pairs))


def tie(*values):
    return lax.optimization_barrier(values)


def smooth_gate(values):
    return values * jax.nn.sigmoid(values)


def smooth_slope(values):
    sigma_values = jax.nn.sigmoid(values)
    return sigma_values * (1.0 + values * (1.0 - sigma_values))


def exact_dot(left, right):
    return jnp.dot(left, right, precision=exact_mode, preferred_element_type=jnp.float32)


def spread_dot(member_rows, values):
    terms, rest = [], values
    for _ in range(3):
        term = lax.reduce_precision(rest, 8, 7)
        terms.append(term.astype(jnp.bfloat16))
        rest = rest - term
    return jnp.dot(
        jnp.concatenate([member_rows] * 3, axis=1),
        jnp.concatenate(terms, axis=0),
        preferred_element_type=jnp.float32,
    )


def pool_dot(member, values):
    return jnp.dot(member, values.astype(jnp.bfloat16), preferred_element_type=jnp.float32)


def bits_of(size):
    return [1 << bit for bit in range(size.bit_length() - 1)]


def stream_sum(value, work=(), inputs=()):
    made = []
    if work:
        value, inputs = tie(value, inputs)
    for k, mask in enumerate([0] + bits_of(lax.axis_size("img"))):
        other = swap(value, "img", mask) if mask else swap(value, "crop", 1)
        if k < len(work):
            made.append(work[k](*inputs, *made[-1:]))
            value, other, inputs, made[-1] = tie(value, other, inputs, made[-1])
        value = value + other
    return value, made


def quarters(blocks):
    cuts = [blocks * i // 4 for i in range(5)]
    return [(low, high - low) for low, high in zip(cuts, cuts[1:])]


def pick(value, index, axis):
    return lax.dynamic_index_in_dim(value, index, axis, keepdims=False)


def slab_rows(width, devices):
    return -(-(width // devices) // 8) * 8


def slab_offset(index, width, devices):
    share = width // devices
    return 2 * share * (index // 2) + (index % 2) * (2 * share - slab_rows(width, devices))


def slab_part(devices, width, height, place_ref, left_ref, right_ref):
    step = pl.program_id(0)
    half = devices // 4
    apart = jnp.where(step < half, 2 * step, 2 * (step - half) + 1)
    index = 2 * (apart ^ place_ref[1]) + place_ref[0]
    offset = slab_offset(index, width, devices)
    base = jnp.minimum(offset // 128, left_ref.shape[1] // 128 - 3) * 128
    wide = left_ref[:, pl.ds(pl.multiple_of(base, 128), 384)].astype(jnp.float32)
    shift = offset - base
    moved = pltpu.roll(wide, jnp.where(shift == 0, 0, 384 - shift), 1)[:, :height]
    return lax.dot_general(
        moved.astype(jnp.bfloat16),
        right_ref[...],
        (((0,), (0,)), ((), ())),
        preferred_element_type=jnp.float32,
    )


def far_kernel(devices, width, height, low, place_ref, left_ref, right_ref, *refs):
    acc = slab_part(devices, width, height, place_ref, left_ref, right_ref)
    if low:
        refs[0][0] = acc[:, :low]
    refs[-1][0] = acc[:, low:]


def near_kernel(devices, width, height, low, place_ref, left_ref, right_ref, *refs):
    held = refs[-1]
    keep_x, send_x, keep_y, send_y = refs[-5:-1]
    acc = slab_part(devices, width, height, place_ref, left_ref, right_ref)
    step = pl.program_id(0)
    if low:
        low_in, high_in, keep_low, send_low = refs[:4]
        total = acc[:, :low] + low_in[0]

        @pl.when(step < devices // 4)
        def _():
            keep_low[0] = total

        @pl.when(step >= devices // 4)
        def _():
            send_low[0] = total

    else:
        high_in = refs[0]
    held[...] = acc[:, low:] + high_in[0]
    rows = height // 8
    bits = (place_ref[2], place_ref[3])
    for half, keep, send in ((0, keep_x, send_x), (1, keep_y, send_y)):
        first, second = bits[half], bits[1 - half]
        for other, ref in ((0, keep), (1, send)):
            for last in range(2):
                block = 4 * half + 2 * (first ^ other) + (second ^ last)
                ref[last, 0] = held[pl.ds(pl.multiple_of(block * rows, rows), rows), :]


def slab_specs(devices, rows, height, low):
    sides = [pl.BlockSpec((rows, WIDE), lambda t, c: (0, 0))] * 2
    widths = [low, WIDE - low] if low else [WIDE]
    parts = [pl.BlockSpec((1, height, n), lambda t, c: (t, 0, 0)) for n in widths]
    shapes = [jax.ShapeDtypeStruct((devices // 2, height, n), jnp.float32) for n in widths]
    return sides, parts, shapes


def far_product(place, left, right, devices, low):
    rows, width = left.shape
    height = slab_rows(width, devices)
    sides, parts, shapes = slab_specs(devices, rows, height, low)
    return pl.pallas_call(
        functools.partial(far_kernel, devices, width, height, low),
        grid_spec=pltpu.PrefetchScalarGridSpec(
            num_scalar_prefetch=1, grid=(devices // 2,), in_specs=sides, out_specs=parts
        ),
        out_shape=shapes,
        compiler_params=pltpu.CompilerParams(vmem_limit_bytes=40 * 1024 * 1024),
        cost_estimate=cost(9),
        name="far_product",
    )(place, left, right)


def near_product(place, left, right, devices, low, arrived):
    rows, width = left.shape
    height = slab_rows(width, devices)
    sides, parts, _ = slab_specs(devices, rows, height, low)
    chips, half = devices // 2, devices // 4
    high = WIDE - low
    piece = pl.BlockSpec((2, 1, height // 8, high), lambda t, c: (0, t, 0, 0))
    out_specs = [piece] * 4
    out_shape = [jax.ShapeDtypeStruct((2, chips, height // 8, high), jnp.float32)] * 4
    if low:
        out_specs = [
            pl.BlockSpec((1, height, low), lambda t, c: (jnp.minimum(t, half - 1), 0, 0)),
            pl.BlockSpec((1, height, low), lambda t, c: (jnp.maximum(t - half, 0), 0, 0)),
        ] + out_specs
        out_shape = [jax.ShapeDtypeStruct((half, height, low), jnp.float32)] * 2 + out_shape
    return pl.pallas_call(
        functools.partial(near_kernel, devices, width, height, low),
        grid_spec=pltpu.PrefetchScalarGridSpec(
            num_scalar_prefetch=1,
            grid=(chips,),
            in_specs=sides + parts,
            out_specs=out_specs,
            scratch_shapes=[pltpu.VMEM((height, high), jnp.float32)],
        ),
        out_shape=out_shape,
        compiler_params=pltpu.CompilerParams(vmem_limit_bytes=48 * 1024 * 1024),
        cost_estimate=cost(13),
        name="near_product",
    )(place, left, right, *arrived)


UNIT_ROWS = 704


def unit_start(index, share, unit, gw, rows):
    return jnp.minimum((share * index // unit) * gw, rows - UNIT_ROWS)


def unit_part(devices, size, gw, place_ref, units_ref):
    step = pl.program_id(0)
    half = devices // 4
    apart = jnp.where(step < half, 2 * step, 2 * (step - half) + 1)
    index = 2 * (apart ^ place_ref[1]) + place_ref[0]
    start = unit_start(index, size // devices, gw * gw * PACK, gw, units_ref.shape[0])
    return pl.multiple_of(start, 8)


def far_units_kernel(devices, size, gw, place_ref, units_ref, out_ref):
    start = unit_part(devices, size, gw, place_ref, units_ref)
    out_ref[0] = units_ref[pl.ds(start, UNIT_ROWS), :]


def near_units_kernel(devices, size, gw, place_ref, units_ref, in_ref, *refs):
    keep_x, send_x, keep_y, send_y = refs
    start = unit_part(devices, size, gw, place_ref, units_ref)
    rows = UNIT_ROWS // 8
    bits = (place_ref[2], place_ref[3])
    for half, keep, send in ((0, keep_x, send_x), (1, keep_y, send_y)):
        first, second = bits[half], bits[1 - half]
        for other, ref in ((0, keep), (1, send)):
            for last in range(2):
                block = 4 * half + 2 * (first ^ other) + (second ^ last)
                skip = pl.multiple_of(block * rows, 8)
                ref[last, 0] = (
                    units_ref[pl.ds(pl.multiple_of(start + skip, 8), rows), :]
                    + in_ref[0, pl.ds(skip, rows), :]
                )


def unit_call(place, units, devices, size, gw, arrived=None):
    rows = units.shape[0]
    chips = devices // 2
    part = pl.BlockSpec((1, UNIT_ROWS, 256), lambda t, c: (t, 0, 0))
    if arrived is None:
        body, extra = far_units_kernel, ()
        out_specs, out_shape = part, jax.ShapeDtypeStruct((chips, UNIT_ROWS, 256), jnp.float32)
    else:
        body, extra = near_units_kernel, (arrived,)
        piece = (2, chips, UNIT_ROWS // 8, 256)
        out_specs = [pl.BlockSpec((2, 1) + piece[2:], lambda t, c: (0, t, 0, 0))] * 4
        out_shape = [jax.ShapeDtypeStruct(piece, jnp.float32)] * 4
    return pl.pallas_call(
        functools.partial(body, devices, size, gw),
        grid_spec=pltpu.PrefetchScalarGridSpec(
            num_scalar_prefetch=1,
            grid=(chips,),
            in_specs=[pl.BlockSpec((rows, 256), lambda t, c: (0, 0))] + [part] * len(extra),
            out_specs=out_specs,
        ),
        out_shape=out_shape,
        compiler_params=pltpu.CompilerParams(vmem_limit_bytes=32 * 1024 * 1024),
        cost_estimate=cost(3),
        name="units",
    )(place, units, *extra)


def share_kernel(left_ref, right_ref, out_ref):
    out_ref[...] = lax.dot_general(
        left_ref[...].astype(jnp.bfloat16),
        right_ref[...].astype(jnp.bfloat16),
        (((0,), (0,)), ((), ())),
        preferred_element_type=jnp.float32,
    )


def share_product(left, right):
    return pl.pallas_call(
        share_kernel,
        out_shape=jax.ShapeDtypeStruct((left.shape[1], right.shape[1]), jnp.float32),
        compiler_params=pltpu.CompilerParams(vmem_limit_bytes=32 * 1024 * 1024),
        cost_estimate=cost(3),
        name="share_product",
    )(left, right)


def crop_bits():
    crop = lax.axis_index("crop")
    return (crop & 1, crop >> 1)


def crop_halves(value):
    lead, rows, cols = value.shape
    whole = value.reshape(lead, 2, 2, 2, rows // 8, cols)
    return [whole[:, 0], whole[:, 1]]


CROP_ORDER = ((0, 1), (1, 0))


def crop_send(parts, step):
    bits = crop_bits()
    return [
        swap(pick(part, 1 - bits[order[step]], 1), "crop", 1 << order[step])
        for part, order in zip(parts, CROP_ORDER)
    ]


def crop_add(parts, arrived, step):
    bits = crop_bits()
    return [
        pick(part, bits[order[step]], 1) + other
        for part, other, order in zip(parts, arrived, CROP_ORDER)
    ]


def crop_fetch(parts, step):
    return [swap(part, "crop", 1 << order[1 - step]) for part, order in zip(parts, CROP_ORDER)]


def crop_join(parts, arrived, step):
    bits = crop_bits()
    joined = []
    for part, other, order in zip(parts, arrived, CROP_ORDER):
        upper = bits[order[1 - step]] == 1
        joined.append(
            jnp.stack([jnp.where(upper, other, part), jnp.where(upper, part, other)], axis=1)
        )
    return joined


def crop_whole(parts):
    both = jnp.stack(parts, axis=1)
    return both.reshape(both.shape[0], -1, both.shape[-1])


def chip_swap(value, step):
    return swap(value, "img", 2 << step)


class LowChain:
    def __init__(self, keep, send):
        self.keep, self.away = keep, [send]
        self.chips = keep.shape[0].bit_length()
        self.steps, self.step = self.chips + 4, 0

    def send(self):
        if self.step < self.chips:
            return [chip_swap(v, self.step) for v in self.away]
        if self.step < self.chips + 2:
            return crop_send(self.keep, self.step - self.chips)
        return crop_fetch(self.keep, self.step - self.chips - 2)

    def take(self, arrived):
        step, chips = self.step, self.chips
        if step < chips:
            total = self.keep + arrived[0]
            half = total.shape[0] // 2
            self.keep, self.away = total[:half], [total[half:]]
            if step == chips - 1:
                self.keep, self.away = crop_halves(total), []
        elif step < chips + 2:
            self.keep = crop_add(self.keep, arrived, step - chips)
        else:
            self.keep = crop_join(self.keep, arrived, step - chips - 2)
        self.step += 1

    def result(self):
        return crop_whole(self.keep)[0]


class HighChain:
    def __init__(self, keep_x, send_x, keep_y, send_y):
        self.keep, self.away = [keep_x, keep_y], [send_x, send_y]
        self.chips = keep_x.shape[1].bit_length() - 1
        self.steps, self.step = self.chips + 4, 0

    def send(self):
        step = self.step
        if step < 2:
            return [swap(v, "crop", 1 << order[step]) for v, order in zip(self.away, CROP_ORDER)]
        if step < self.chips + 2:
            return [chip_swap(v, step - 2) for v in self.away]
        return crop_fetch(self.keep, step - self.chips - 2)

    def take(self, arrived):
        step, chips = self.step, self.chips
        if step < chips + 2:
            total = [keep + other for keep, other in zip(self.keep, arrived)]
            if step == 0:
                self.keep, self.away = [v[0] for v in total], [v[1] for v in total]
            else:
                if step == 1:
                    total = [jnp.concatenate(total, axis=1)]
                half = total[0].shape[0] // 2
                self.keep, self.away = [total[0][:half]], [total[0][half:]]
            if step == chips + 1:
                rows = total[0].shape[1] // 2
                self.keep, self.away = [total[0][:, :rows], total[0][:, rows:]], []
        else:
            self.keep = crop_join(self.keep, arrived, step - chips - 2)
        self.step += 1

    def result(self):
        return crop_whole(self.keep)[0]


class CropSum:
    steps = 4

    def __init__(self, value):
        self.away = []
        self.keep = crop_halves(value[None])
        self.step = 0

    def send(self):
        if self.step < 2:
            return crop_send(self.keep, self.step)
        return crop_fetch(self.keep, self.step - 2)

    def take(self, arrived):
        if self.step < 2:
            self.keep = crop_add(self.keep, arrived, self.step)
        else:
            self.keep = crop_join(self.keep, arrived, self.step - 2)
        self.step += 1

    def result(self):
        return crop_whole(self.keep)[0]


class Flow:
    def __init__(self):
        self.sent = {}

    def begin(self, chain):
        self.sent[id(chain)] = chain.send()

    def advance(self, chain, beside):
        arrived, beside = tie(self.sent[id(chain)], beside)
        chain.take(arrived)
        (chain.keep, chain.away), beside = tie((chain.keep, chain.away), beside)
        if chain.step < chain.steps:
            self.begin(chain)
        return beside


def shards(
    pixels,
    counts,
    slot_order,
    w_in,
    kernel,
    w_red,
    b_red,
    w_exp,
    b_exp,
    w_out,
    gain_one,
    shift_one,
    gain_two,
    shift_two,
    gain_three,
    shift_three,
    protos,
):
    row_count = pixels.shape[2]
    width = pixels.shape[3]
    proto_count = protos.shape[1]
    squeeze = w_red.shape[1]
    seg_count = row_count // (SMALL_SIDE * SMALL_SIDE)
    slot_total = slot_order.shape[1]
    devices = lax.axis_size("img")
    img_index = lax.axis_index("img")
    crop_index = lax.axis_index("crop")
    core = img_index % 2
    fast = width % devices == 0 and (2 * width // devices) % 8 == 0
    is_global = crop_index < 2
    glob = is_global.astype(jnp.int32).reshape(1)
    stream_rows = 2.0 * devices * row_count
    couple_number = 2.0 * devices * (IMG_DEV + slot_total)
    inputs = pixels.reshape(row_count, width)
    row_ids = jnp.arange(row_count, dtype=jnp.int32)
    side = jnp.where(is_global, SIDE, SMALL_SIDE)
    seg_of_row = row_ids // (side * side)
    across = row_ids % side
    down = (row_ids // side) % side
    masks = jnp.stack([across > 0, across < side - 1, down > 0, down < side - 1])
    masks = jnp.broadcast_to(masks.astype(jnp.float32)[:, :, None], (4, row_count, 128))
    member = (seg_of_row[None, :] == jnp.arange(seg_count, dtype=jnp.int32)[:, None]).astype(
        jnp.bfloat16
    )
    member_rows = member.T
    crop_pixels = jnp.where(is_global, float(SIDE * SIDE), float(SMALL_SIDE * SMALL_SIDE))
    block_width = PACK * kernel.shape[2]
    block_count = kernel.shape[1] // PACK
    sides = (SIDE, SMALL_SIDE)

    def norm_rows(local_sums, work=(), inputs=()):
        sums, made = stream_sum(local_sums, work, inputs)
        average = sums[0] / stream_rows
        inv = lax.rsqrt(sums[1] / stream_rows - average * average + norm_epsilon)
        return average, inv, made

    def back_rows(local_sums, gain, inv, work=(), inputs=()):
        sums, made = stream_sum(local_sums, work, inputs)
        return sums, gain * inv, sums[0] / stream_rows, sums[1] / stream_rows, made

    hidden_one = jnp.dot(inputs, w_in, preferred_element_type=jnp.float32)
    sums = jnp.stack([jnp.sum(hidden_one, axis=0), jnp.sum(hidden_one * hidden_one, axis=0)])
    mean_one, inv_one, packed = norm_rows(
        sums,
        [functools.partial(pack_blocks, low, count) for low, count in quarters(block_count)],
        (kernel,),
    )
    packed = packed[-1]
    zero_row = jnp.zeros((width,), jnp.float32)
    scale_one = gain_one * inv_one
    par = jnp.stack(
        [scale_one, shift_one - mean_one * scale_one, inv_one, -mean_one * inv_one] + [zero_row] * 4
    )
    hidden_two, sums = conv_fwd(glob, hidden_one, par, masks, packed, block_width, sides)
    mean_two, inv_two, _ = norm_rows(sums[:2])
    centred_two = (hidden_two - mean_two) * inv_two
    pre_two = centred_two * gain_two + shift_two
    act_two = smooth_gate(pre_two)
    red_float = w_red.astype(jnp.float32)
    exp_float = w_exp.astype(jnp.float32)
    pooled = pool_dot(member, act_two) / crop_pixels
    reduce_pre = exact_dot(pooled, red_float) + b_red
    reduced = smooth_gate(reduce_pre)
    gate_values = jax.nn.sigmoid(exact_dot(reduced, exp_float) + b_exp)
    gate_rows = spread_dot(member_rows, gate_values)
    excited = (act_two * gate_rows).astype(jnp.bfloat16)
    hidden_three = jnp.dot(excited, w_out, preferred_element_type=jnp.float32)
    sums = jnp.stack([jnp.sum(hidden_three, axis=0), jnp.sum(hidden_three * hidden_three, axis=0)])
    mean_three, inv_three, _ = norm_rows(sums)
    centred_three = (hidden_three - mean_three) * inv_three
    summed_in = inputs.astype(jnp.float32) + centred_three * gain_three + shift_three
    output = smooth_gate(summed_in)
    pooled_out = (
        jnp.dot(
            member.astype(jnp.float32),
            output,
            precision=lax.Precision.HIGH,
            preferred_element_type=jnp.float32,
        )
        / crop_pixels
    )
    length_inv = lax.rsqrt(jnp.sum(pooled_out * pooled_out, axis=1, keepdims=True) + length_epsilon)
    unit_wide = pooled_out * length_inv
    unit_rows = unit_wide.astype(jnp.bfloat16)
    match_matrix = jnp.dot(unit_rows, protos, preferred_element_type=jnp.float32)

    every = match_matrix[:IMG_DEV]
    if devices <= 8:
        every = jnp.concatenate([every, swap(every, "img", 1)], axis=0)
        every = jnp.concatenate(
            [every] + [swap(every, "img", mask) for mask in range(2, devices, 2)], axis=0
        )
    else:
        for mask in bits_of(devices):
            every = jnp.concatenate([every, swap(every, "img", mask)], axis=0)
    plan_rows = jnp.exp(every / sharpness)
    for sweep_index in range(3):
        plan_rows = plan_rows / jnp.sum(plan_rows, axis=0, keepdims=True)
        plan_rows = plan_rows / jnp.sum(plan_rows, axis=1, keepdims=True)
    codes = plan_rows[:IMG_DEV]
    partner = lax.ppermute(codes, "crop", [(0, 1), (1, 0)])
    both_codes = lax.ppermute(codes, "crop", [(0, 2), (1, 3)]) + lax.ppermute(
        codes, "crop", [(0, 3), (1, 2)]
    )
    wide_target = jnp.concatenate(
        [partner, jnp.zeros((seg_count - IMG_DEV, proto_count), jnp.float32)], axis=0
    )
    ends = [jnp.sum(counts[0, : i + 1]) for i in range(IMG_DEV)]
    first_slot = jnp.maximum(crop_index - 2, 0) * seg_count
    order_here = lax.dynamic_slice_in_dim(slot_order[0], first_slot, seg_count)
    owner = sum((order_here >= end).astype(jnp.int32) for end in ends)
    narrow_target = jnp.zeros((seg_count, proto_count), jnp.float32)
    for i in range(IMG_DEV):
        narrow_target = jnp.where(owner[:, None] == i, both_codes[i : i + 1], narrow_target)
    target = jnp.where(is_global, wide_target, narrow_target)
    sharpened = match_matrix / sharpening_divisor
    shifted = sharpened - jnp.max(sharpened, axis=1, keepdims=True)
    log_probs = shifted - jnp.log(jnp.sum(jnp.exp(shifted), axis=1, keepdims=True))
    loss_here = -jnp.sum(target * log_probs) / couple_number
    scores_wide = (jnp.exp(log_probs) * jnp.sum(target, axis=1, keepdims=True) - target) / (
        sharpening_divisor * couple_number
    )
    grad_scores = scores_wide.astype(jnp.bfloat16)

    grad_unit = jnp.einsum("sk,wk->sw", grad_scores, protos, preferred_element_type=jnp.float32)
    inner_term = jnp.sum(pooled_out * grad_unit, axis=1, keepdims=True)
    grad_pooled_out = (
        length_inv * grad_unit - pooled_out * length_inv * length_inv * length_inv * inner_term
    )
    grad_output = spread_dot(member_rows, grad_pooled_out / crop_pixels)
    grad_summed = grad_output * smooth_slope(summed_in)
    sums_three, scale_three, first, second, _ = back_rows(
        jnp.stack([jnp.sum(grad_summed, axis=0), jnp.sum(grad_summed * centred_three, axis=0)]),
        gain_three,
        inv_three,
    )
    grad_three_low = (scale_three * (grad_summed - first - centred_three * second)).astype(
        jnp.bfloat16
    )
    if fast:
        share = width // devices
        height = slab_rows(width, devices)
        chip = img_index // 2
        near = jnp.stack([core, chip, crop_index & 1, crop_index >> 1]).astype(jnp.int32)
        far = jnp.stack([1 - core, chip, crop_index & 1, crop_index >> 1]).astype(jnp.int32)

        def kept(value):
            skip = core * (value.shape[0] - share)
            return lax.dynamic_slice_in_dim(value, skip, share, axis=0)

        seen_scores = lax.all_gather(
            jnp.concatenate(
                [
                    unit_wide,
                    jnp.zeros((seg_count, WIDE - width), jnp.float32),
                    scores_wide,
                    jnp.zeros((seg_count, WIDE_PROTOS - proto_count), jnp.float32),
                ],
                axis=1,
            ),
            "img",
            tiled=True,
        )

    grad_excited = jnp.einsum(
        "rv,wv->rw", grad_three_low, w_out, preferred_element_type=jnp.float32
    )
    flow = Flow()
    if fast:
        grad_excited, seen_scores = tie(grad_excited, seen_scores)
        protos_sum = CropSum(
            share_product(
                lax.dynamic_slice_in_dim(seen_scores, img_index * share, height, axis=1),
                seen_scores[:, WIDE:],
            )
        )
        (protos_sum.keep, grad_excited) = tie(protos_sum.keep, grad_excited)
        flow.begin(protos_sum)
    grad_gate = pool_dot(member, grad_excited * act_two)
    grad_gate_pre = grad_gate * gate_values * (1.0 - gate_values)
    grad_reduce_pre = exact_dot(grad_gate_pre, exp_float.T) * smooth_slope(reduce_pre)
    grad_pooled = exact_dot(grad_reduce_pre, red_float.T)
    grad_act_two = grad_excited * gate_rows + spread_dot(member_rows, grad_pooled / crop_pixels)
    grad_pre_two = grad_act_two * smooth_slope(pre_two)
    bias_row = jnp.concatenate(
        [
            jnp.sum(grad_reduce_pre, axis=0),
            loss_here.reshape(1),
            jnp.zeros((width - squeeze - 1,), jnp.float32),
        ]
    )
    local_two = jnp.stack(
        [
            jnp.sum(grad_pre_two, axis=0),
            jnp.sum(grad_pre_two * centred_two, axis=0),
            jnp.sum(grad_gate_pre, axis=0),
            bias_row,
        ]
    )
    work = []
    if fast:
        seen_gates = lax.all_gather(
            jnp.concatenate([pooled, reduced, grad_reduce_pre, grad_gate_pre], axis=1),
            "img",
            tiled=True,
        )

        def out_far(left, right):
            return far_product(far, left, right, devices, 0)

        def proto_step(left, right, arrived):
            return flow.advance(protos_sum, arrived)

        work = [out_far, proto_step]
    sums_two, scale_two, first, second, made = back_rows(
        local_two, gain_two, inv_two, work, (excited, grad_three_low)
    )
    if fast:
        arrived = [swap(v, "img", 1) for v in made[-1]]
    grad_two_low = (scale_two * (grad_pre_two - first - centred_two * second)).astype(jnp.bfloat16)
    if fast:
        grad_two_low, arrived = tie(grad_two_low, arrived)
        arrived = flow.advance(protos_sum, arrived)
        outs = HighChain(*near_product(near, excited, grad_three_low, devices, 0, arrived))
        outs.keep, outs.away, grad_two_low = tie(outs.keep, outs.away, grad_two_low)
        flow.begin(outs)
    grad_pre_one, sums = conv_dgrad(
        glob, grad_two_low, hidden_one, par, masks, packed, block_width, sides
    )

    def some_wgrad(low, count, grad, done=None):
        return conv_wgrad(
            glob, grad, hidden_one, par, masks, low, count, block_count, block_width, sides, done
        )

    cut = block_count // 2
    steps = [
        functools.partial(some_wgrad, 0, cut),
        functools.partial(some_wgrad, cut, block_count - cut),
    ]
    early = []
    if fast:
        grad_two_low, grad_pre_one, sums = tie(grad_two_low, grad_pre_one, sums)
        units = steps[0](grad_two_low)
        units = flow.advance(outs, units)
        units, sums = tie(units, sums)

        def my_columns(value):
            count = value.shape[1] // devices
            return lax.dynamic_slice_in_dim(value, img_index * count, count, axis=1)

        def shares_of(seen):
            seen = flow.advance(protos_sum, seen)
            return (
                exact_dot(
                    my_columns(seen[:, :width]).T, seen[:, width + squeeze : width + 2 * squeeze]
                ),
                exact_dot(my_columns(seen[:, width : width + squeeze]).T, seen[:, width + 2 * squeeze :]),
            )

        early = [shares_of]
    sums_one, scale_one, first, second, made = back_rows(
        sums[:2], gain_one, inv_one, early, (seen_gates,) if fast else ()
    )
    last = jnp.concatenate([sums_one, sums_two, sums_three], axis=0)
    last = last + swap(last, "crop", 2)
    centred_one = (hidden_one - mean_one) * inv_one
    grad_one_low = (scale_one * (grad_pre_one - first - centred_one * second)).astype(jnp.bfloat16)
    if fast:
        share_red, share_exp = made[-1]
        share_red, share_exp = lax.optimization_barrier(
            lax.psum((share_red, share_exp), "crop")
        )
        sent_far = far_product(far, inputs, grad_one_low, devices, LOW_COLUMNS)
        flow.sent[id(outs)], sent_far = tie(flow.sent[id(outs)], sent_far)
        outs.take(flow.sent[id(outs)])
        flow.begin(outs)
        arrived = [swap(v, "img", 1) for v in sent_far]
        last, arrived = tie(last, arrived)
        parts = near_product(near, inputs, grad_one_low, devices, LOW_COLUMNS, arrived)
        ins = HighChain(*parts)
        units, grad_two_low, grad_one_low, ins.keep, ins.away = tie(
            units, grad_two_low, grad_one_low, ins.keep, ins.away
        )
        flow.begin(ins)
        units = steps[1](grad_two_low, units)
        units = flow.advance(outs, units)
        units = flow.advance(protos_sum, units)
        gw = kernel.shape[2]
        unit_size = gw * gw * PACK
        units = units.reshape(-1, 256)
        swapped = unit_call(far, units, devices, kernel.size, gw)
        flat_protos = protos_sum.result()[:share, :proto_count].reshape(-1)
        swapped, units, grad_one_low, flat_protos = flow.advance(
            ins, (swapped, units, grad_one_low, flat_protos)
        )
        swapped = swap(swapped, "img", 1)
        grad_inputs = (
            jnp.einsum("rv,wv->rw", grad_one_low, w_in, preferred_element_type=jnp.float32)
            + grad_summed
        )
        swapped, grad_inputs = tie(swapped, grad_inputs)
        gks = HighChain(*unit_call(near, units, devices, kernel.size, gw, swapped))
        flow.begin(gks)
        chains = [ins, outs, gks]
        last_chain = None
        flat_out = None
        for chain in (chains[index] for index in TAIL):
            landed = flow.sent[id(chain)]
            if last_chain is not None:
                landed, _ = tie(landed, (last_chain.keep, last_chain.away))
            if chain is ins and chain.step == 5:
                flat_red = share_red.reshape(-1)
                flat_exp = share_exp.reshape(-1)
                landed, flat_out, flat_red, flat_exp = tie(landed, flat_out, flat_red, flat_exp)
            chain.take(landed)
            if chain.step < chain.steps:
                flow.begin(chain)
            if chain is ins and chain.step == 3:
                share_red, share_exp, _ = tie(share_red, share_exp, (ins.keep, ins.away))
            if chain is outs and chain.step == chain.steps:
                flat_out = kept(outs.result()[:, :width]).reshape(-1)
            last_chain = chain
    else:
        made = None
        for step in steps:
            made = step(grad_two_low, made)
        small_kernel = made
        grad_inputs = (
            jnp.einsum("rv,wv->rw", grad_one_low, w_in, preferred_element_type=jnp.float32)
            + grad_summed
        )

    if fast:
        flat_in = kept(ins.result()[:, :width]).reshape(-1)
        total = kernel.size // devices
        first_unit = total * img_index // unit_size
        start = unit_start(img_index, total, unit_size, gw, units.size // 256)
        span = -(-total // unit_size) + 1
        mine = jnp.pad(gks.result(), ((0, gw), (0, 0)))
        mine = lax.dynamic_slice_in_dim(mine, first_unit * gw - start, span * gw, axis=0)
        mine = mine[:, : PACK * gw].reshape(span, gw, PACK, gw).transpose(0, 2, 1, 3).reshape(-1)
        flat_kernel = lax.dynamic_slice_in_dim(mine, total * img_index - unit_size * first_unit, total)
        shares = (flat_in, flat_kernel, flat_red, flat_exp, flat_out, flat_protos)
    else:
        gw = kernel.shape[2]
        grads = (
            jnp.einsum("rw,rv->wv", inputs, grad_one_low, preferred_element_type=jnp.float32),
            small_kernel[..., : PACK * gw]
            .reshape(9, block_count, gw, PACK, gw)
            .transpose(0, 1, 3, 2, 4),
            exact_dot(pooled.T, grad_reduce_pre),
            exact_dot(reduced.T, grad_gate_pre),
            jnp.einsum("rw,rv->wv", excited, grad_three_low, preferred_element_type=jnp.float32),
            jnp.einsum("sw,sk->wk", unit_rows, grad_scores, preferred_element_type=jnp.float32),
        )
        shares = tuple(
            lax.psum(
                lax.psum_scatter(grad.reshape(-1), "img", scatter_dimension=0, tiled=True), "crop"
            )
            for grad in grads
        )
    tail = (
        last[5, :squeeze],
        last[4],
        last[1],
        last[0],
        last[3],
        last[2],
        last[7],
        last[6],
    )
    loss_total = last[5, squeeze]

    return (
        loss_total,
        output.astype(jnp.bfloat16).reshape(pixels.shape),
        grad_inputs.reshape(pixels.shape),
        *shares,
        *tail,
    )


def solution(mesh):
    return jax.shard_map(
        shards,
        mesh=mesh,
        in_specs=(P("crop", "img", None, None), P("img", None), P("img", None)) + (P(),) * 14,
        out_specs=(P(), P("crop", "img", None, None), P("crop", "img", None, None))
        + (P("img"),) * 6
        + (P(),) * 8,
        check_vma=False,
    )
```
